256 devices in a mesh: row: 16 (over z, core), col: 16 (over x, y).
Axes of the slice: x: 4, y: 4, z: 8, core: 2. Of those that a mesh axis runs over, the one named last changes fastest.
Arguments:
- hidden: bfloat16 [16, 2048, 2560], P('row', 'col'), may hold values from -6 to 6
- grad_out: bfloat16 [16, 2048, 2560], P('row', 'col'), may hold values from -6 to 6
- w_key: bfloat16 [1280, 2560], P('row'), may hold values from -0.15625 to 0.15625
- w_value: bfloat16 [1280, 2560], P('row'), may hold values from -0.15625 to 0.15625
- depthwise_weight: float32 [4, 2560], replicated, may hold values from -3 to 3
- table: float32 [10240, 1280], P(('row', 'col')), may hold values from -6 to 6
- adam_m: float32 [10240, 1280], P(('row', 'col')), may hold values from -4 to 4
- adam_v: float32 [10240, 1280], P(('row', 'col')), may hold values from 0.25 to 4
- row_owner: int32 [16, 2304, 1], P('row', 'col'), may hold values from 0 to 255; in each aligned block of 144 rows (0 to 143, 144 to 287, ..., all dimensions but the last counted through in order) at most 2 rows name the same one
- row_local: int32 [16, 2304], P('row', 'col'), may hold values from 0 to 39
- expand_index: int32 [16, 2048, 2], P('row', 'col'), may hold values from 0 to 143
- doc_lengths: int32 [16, 8], P('row'), may hold values from 1 to 1024, 2048 in all within a row
Outputs:
- memory_out: bfloat16 [16, 2048, 2560], P('row', 'col')
- new_table: float32 [10240, 1280], P(('row', 'col'))
- new_moment: float32 [10240, 1280], P(('row', 'col'))
- new_second: float32 [10240, 1280], P(('row', 'col'))
The draws below stay inside these ranges and needn't reach their ends.
Inputs may be any that keep to these rules, and one draw needn't show every extreme that they name: `row_owner`: among the 144 slots of one device's row list no owner is named more than 2 times, a bound that some block reaches. `doc_lengths`: the 8 lengths of a sequence sum to 2048; the largest is exactly 1024.
All inputs are finite; a program needn't handle non-finite values.
Results may differ from the reference program's by a relative error of at most 0.009.
Values may be sent and summed in bfloat16 or wider, within the bound.
A program may use at most 64 MiB of HBM per device.

```python
import math
import jax
import jax.numpy as jnp
import numpy as np
from jax import lax

D = 2560
E = 1280
LOOKUPS = 2
KW = 4
DILATION_STEP = 3
DOCS = 8
TOK_DEV = 128
R_DEV = 40
U = 144
CAP = 2
SEQ = 2048
BATCH = 16
TABLE = 10240
N_COL = 16
DEVICES = 256


def touch_ends(values, own_key, low, largest):
    extent = values.shape
    index_at = [jax.random.randint(jax.random.fold_in(own_key, axis), (), 0, extent[axis]) for axis in range(len(extent))]
    values = values.at[tuple(index_at)].set(low)
    longest = extent.index(max(extent))
    index_at[longest] = (index_at[longest] + 1) % extent[longest]
    return values.at[tuple(index_at)].set(largest)


def block_levels(own_key, shape, split, low, high):
    def one(dim, blocks):
        draws = jax.random.uniform(jax.random.fold_in(jax.random.fold_in(own_key, 6), dim), (blocks,), jnp.float32, low / len(split), high / len(split))
        return jnp.repeat(jnp.exp(draws), shape[dim] // blocks).reshape((-1,) + (1,) * (len(shape) - dim - 1))

    gain = one(*split[0])
    for cut in split[1:]:
        gain = gain * one(*cut)
    return gain


def profile(count, total, reach, lean):
    weights = [(1 << 20) // math.isqrt(grade ** lean) + 1 for grade in range(2, count + 1)]
    spare, given = total - reach - (count - 1), [1] * (count - 1)
    while spare > 0:
        movable = [i for i in range(count - 1) if given[i] < reach]
        pool, left = sum([weights[i] for i in movable]), spare
        for i in movable:
            addition = min(reach - given[i], max(1, left * weights[i] // pool), spare)
            given[i] = given[i] + addition
            spare = spare - addition
    return np.array([reach] + given)


def ragged_sizes(stream_key, count, total, reach, skew):
    if count == 2:
        one = jax.random.randint(stream_key, (), max(1, total - reach), min(reach, total - 1) + 1)
        return jnp.stack([one, total - one])
    sizes = jnp.asarray(profile(count, total, reach, skew), jnp.int32)
    twos = (count - 1) // 2
    giver, sink = sizes[1:1 + 2 * twos:2], sizes[2:2 + 2 * twos:2]
    slack = jnp.minimum(giver - 1, reach - sink)
    moved = jax.random.randint(jax.random.fold_in(stream_key, 1), (twos,), 0, 1 << 20) % (slack + 1)
    sizes = sizes.at[1:1 + 2 * twos:2].set(giver - moved).at[2:2 + 2 * twos:2].set(sink + moved)
    return sizes[jax.random.permutation(jax.random.fold_in(stream_key, 2), count)]


def shared_out(own_key, own, number, rows, amount, top, bound, skew):
    sequence = jax.random.permutation(own_key, amount)
    packed, ordinary = shares(amount, rows * top, bound, skew, True), shares(amount, rows * top, bound, skew, False)
    places = jnp.arange(amount)

    def named(tallies, turn):
        used = int((tallies > 0).sum())
        fixed = max(1, used // 4)
        passed = fixed + (places - fixed + turn * (used - fixed)) % max(1, amount - fixed)
        return jnp.zeros((amount,), jnp.int32).at[sequence[jnp.where(places < fixed, places, passed)]].set(jnp.asarray(tallies, jnp.int32))

    tallies = jnp.where(number % 4 == 0, named(packed, number // 4), named(ordinary, number - number // 4 - 1))
    mixed = jax.random.permutation(jax.random.fold_in(own, 3), amount)
    donor, sink = mixed[0:amount // 2 * 2:2], mixed[1:amount // 2 * 2:2]
    slack = jnp.minimum(tallies[donor] - 1, bound - tallies[sink]) // 2
    slack = jnp.where((donor == sequence[0]) | (sink == sequence[0]) | (tallies[sink] == 0), 0, jnp.maximum(slack, 0))
    passed = jax.random.randint(jax.random.fold_in(own, 4), (amount // 2,), 0, 1 << 20) % (slack + 1)
    tallies = tallies.at[donor].add(-passed).at[sink].add(passed)
    members = jnp.searchsorted(jnp.cumsum(tallies), jnp.arange(rows * top), side="right").astype(jnp.int32)
    table = members.reshape(top, rows).T
    table = table[jax.random.permutation(jax.random.fold_in(own, 1), rows)]
    turn = jax.random.randint(jax.random.fold_in(own, 2), (rows, 1), 0, top)
    return jnp.take_along_axis(table, (jnp.arange(top)[None, :] + turn) % top, axis=1)


def shares(number_of, total, reach, lean, full):
    weights = [(1 << 20) // math.isqrt(rank ** lean) + 1 for rank in range(1, number_of + 1)]
    largest = reach if full else min(reach, max(-(-total // number_of), total * weights[0] // sum(weights)))
    least = 1 if total - largest >= number_of - 1 else 0
    holding, surplus = [largest] + [least] * (number_of - 1), total - largest - least * (number_of - 1)
    while surplus > 0:
        free = [i for i in range(1, number_of) if holding[i] < largest] or [i for i in range(1, number_of) if holding[i] < reach]
        whole, budget = sum([weights[i] for i in free]), surplus
        for i in free:
            more = min(reach - holding[i], max(1, budget * weights[i] // whole), surplus)
            holding[i] = holding[i] + more
            surplus = surplus - more
    return np.array(holding)


def normal_values(own_key, shape, spread, most, split=(), kind=jnp.bfloat16):
    array = jax.random.normal(own_key, shape, jnp.float32) * spread
    if len(split) > 0:
        array = block_levels(own_key, shape, split, -0.22, 0.18) * array
    return jnp.clip(array, min=-most, max=most).astype(kind)


def setup_inputs(seed: int = 0) -> dict:
    key_of = jax.random.split(jax.random.key(seed), 13)
    hidden = normal_values(key_of[0], (BATCH, SEQ, D), 1.0, 6.0, ((0, 16), (1, 16)))
    grad_out = normal_values(key_of[1], (BATCH, SEQ, D), 1.0, 6.0, ((0, 16), (1, 16)))
    w_key = normal_values(key_of[2], (E, D), E ** -0.5, 0.15625, ((0, 16),))
    w_value = normal_values(key_of[3], (E, D), E ** -0.5, 0.15625, ((0, 16),))
    depthwise_weight = normal_values(key_of[4], (KW, D), 0.5, 3.0, (), jnp.float32)
    table = normal_values(key_of[5], (TABLE, E), 1.0, 6.0, ((0, 256),), jnp.float32)
    adam_m = normal_values(key_of[6], (TABLE, E), 0.5, 4.0, ((0, 256),), jnp.float32)
    adam_v = jnp.clip(jnp.exp(math.log(4.0) - 2.7725887 * jax.random.uniform(key_of[7], (TABLE, E), jnp.float32) ** block_levels(key_of[7], (TABLE, E), ((0, 256),), -0.2, 0.2)), 0.25, 4.0)
    row_owner_keys = jax.random.split(jax.random.fold_in(key_of[8], 1), BATCH * (N_COL * U) // U)
    row_owner_turns = jax.random.permutation(jax.random.fold_in(key_of[8], 3), BATCH * (N_COL * U) // U)
    row_owner = jax.vmap(lambda own, number: shared_out(jax.random.fold_in(key_of[8], 2), own, number, U, DEVICES, 1, CAP, 2))(row_owner_keys, row_owner_turns).reshape((BATCH, N_COL * U, 1))
    row_local = touch_ends(jax.random.randint(key_of[9], (BATCH, N_COL * U), 0, R_DEV), jax.random.fold_in(key_of[9], 1), 0, R_DEV - 1).astype(jnp.int32)
    expand_index = touch_ends(jax.random.randint(key_of[10], (BATCH, SEQ, LOOKUPS), 0, U), jax.random.fold_in(key_of[10], 1), 0, U - 1).astype(jnp.int32)
    doc_lengths = jax.vmap(lambda own: ragged_sizes(own, DOCS, SEQ, SEQ // 2, 0))(jax.random.split(key_of[11], BATCH)).reshape((BATCH, DOCS)).astype(jnp.int32)
    return dict(hidden=hidden, grad_out=grad_out, w_key=w_key, w_value=w_value, depthwise_weight=depthwise_weight, table=table, adam_m=adam_m, adam_v=adam_v, row_owner=row_owner, row_local=row_local, expand_index=expand_index, doc_lengths=doc_lengths)


NORM_EPS = 1e-06
BETA_ONE = 0.9
BETA_TWO = 0.95
ADAM_EPS = 1e-08
LEARN_RATE = 0.01
DECAY_RATE = 0.1
STEP_COUNT = 10.0

def rms_scale(values):
    return lax.rsqrt(lax.optimization_barrier(jnp.mean(values * values, axis=-1, keepdims=True)) + NORM_EPS)

def doc_index(positions, lengths):
    doc_ends = jnp.cumsum(lengths, dtype=jnp.int32)
    return lax.optimization_barrier(jnp.sum((positions[:, None] >= doc_ends[None, :-1]).astype(jnp.int32), axis=1))

def adamw_update(current, moment, second, gradient):
    moment_new = BETA_ONE * moment + (1.0 - BETA_ONE) * gradient
    second_new = BETA_TWO * second + (1.0 - BETA_TWO) * gradient * gradient
    first_hat = moment_new / (1.0 - BETA_ONE ** STEP_COUNT)
    second_hat = second_new / (1.0 - BETA_TWO ** STEP_COUNT)
    updated = current - LEARN_RATE * (first_hat / (jnp.sqrt(second_hat) + ADAM_EPS) + DECAY_RATE * current)
    return (updated, moment_new, second_new)

def lowered_rows(values, shift_amount):
    if shift_amount == 0:
        return values
    return jnp.pad(values[:values.shape[0] - shift_amount], ((shift_amount, 0), (0, 0)))

def raised_rows(values, shift_amount):
    if shift_amount == 0:
        return values
    return jnp.pad(values[shift_amount:], ((0, shift_amount), (0, 0)))

def reference(hidden, grad_out, w_key, w_value, depthwise_weight, table, adam_m, adam_v, row_owner, row_local, expand_index, doc_lengths):
    table16 = table.astype(jnp.bfloat16)
    slot_ids = (row_owner[:, :, 0] * R_DEV + row_local).astype(jnp.int32)
    positions = jnp.arange(SEQ, dtype=jnp.int32)
    shard_base = positions // TOK_DEV * U
    root_width = jnp.sqrt(jnp.float32(D))

    def one_sequence(row_grad, inputs):
        hidden_seq, grad_seq, slot_seq, expand_seq, lengths = inputs
        token_row = jnp.take(slot_seq, shard_base[:, None] + expand_seq).astype(jnp.int32)
        fetched = jnp.take(table16, token_row, axis=0).astype(jnp.float32)
        memory = lax.optimization_barrier(jnp.sum(fetched, axis=1)).astype(jnp.bfloat16)
        key = jnp.dot(memory, w_key, preferred_element_type=jnp.float32)
        value = jnp.dot(memory, w_value, preferred_element_type=jnp.float32)
        key_scale = rms_scale(key)
        key_norm = key * key_scale
        hidden_f = hidden_seq.astype(jnp.float32)
        hidden_norm = hidden_f * rms_scale(hidden_f)
        gate = jax.nn.sigmoid(lax.optimization_barrier(jnp.sum(hidden_norm * key_norm, axis=-1, keepdims=True)) / root_width)
        gated = (gate * value).astype(jnp.bfloat16)
        gated_f = gated.astype(jnp.float32)
        gated_scale = rms_scale(gated_f)
        gated_normalized = gated_f * gated_scale
        doc_ids = doc_index(positions, lengths)
        document_masks = []
        for kernel_tap_index in range(KW):
            shift_amount = kernel_tap_index * DILATION_STEP
            source = positions - shift_amount
            same_doc = (source >= 0) & (doc_ids[jnp.maximum(source, 0)] == doc_ids)
            document_masks.append(same_doc.astype(jnp.float32)[:, None])
        convolved_rows = jnp.zeros((SEQ, D), jnp.float32)
        for kernel_tap_index in range(KW):
            convolved_rows = convolved_rows + depthwise_weight[kernel_tap_index] * lowered_rows(gated_normalized, kernel_tap_index * DILATION_STEP) * document_masks[kernel_tap_index]
        out_seq = (jax.nn.silu(convolved_rows) + gated_f).astype(jnp.bfloat16)
        grad_f = grad_seq.astype(jnp.float32)
        sig = jax.nn.sigmoid(convolved_rows)
        convolution_gradient = grad_f * sig * (1.0 + convolved_rows * (1.0 - sig))
        normalized_gradient = jnp.zeros((SEQ, D), jnp.float32)
        for kernel_tap_index in range(KW):
            normalized_gradient = normalized_gradient + depthwise_weight[kernel_tap_index] * raised_rows(convolution_gradient * document_masks[kernel_tap_index], kernel_tap_index * DILATION_STEP)
        gated_grad = grad_f + gated_scale * (normalized_gradient - gated_normalized * lax.optimization_barrier(jnp.mean(gated_normalized * normalized_gradient, axis=-1, keepdims=True)))
        value_grad = gated_grad * gate
        score_grad = gate * (1.0 - gate) * lax.optimization_barrier(jnp.sum(gated_grad * value, axis=-1, keepdims=True))
        target = score_grad * hidden_norm / root_width
        key_grad = key_scale * (target - key_norm * lax.optimization_barrier(jnp.mean(key_norm * target, axis=-1, keepdims=True)))
        key_grad16 = key_grad.astype(jnp.bfloat16)
        value_grad16 = value_grad.astype(jnp.bfloat16)
        memory_grad = (jnp.dot(key_grad16, w_key.T, preferred_element_type=jnp.float32) + jnp.dot(value_grad16, w_value.T, preferred_element_type=jnp.float32)).astype(jnp.bfloat16)
        memory_grad_f = memory_grad.astype(jnp.float32)
        for lookup in range(LOOKUPS):
            row_grad = row_grad + jax.ops.segment_sum(memory_grad_f, token_row[:, lookup], num_segments=TABLE)
        return (row_grad, out_seq)
    start_grad = jnp.zeros((TABLE, E), jnp.float32)
    row_grad, memory_out = lax.scan(one_sequence, start_grad, (hidden, grad_out, slot_ids, expand_index, doc_lengths))
    new_table, new_moment, new_second = adamw_update(table, adam_m, adam_v, row_grad)
    return (memory_out, new_table, new_moment, new_second)
```

```python
import jax
import jax.numpy as jnp
from jax import lax
from jax.experimental import pallas as pl
from jax.experimental.pallas import tpu as pltpu
from jax.sharding import PartitionSpec as P

DILATION_STEP = 3
NORM_EPS = 1e-06
BETA_ONE = 0.9
BETA_TWO = 0.95
ADAM_EPS = 1e-08
LEARN_RATE = 0.01
DECAY_RATE = 0.1
STEP_COUNT = 10.0

Z, X, Y = 8, 4, 4
PLANE = 2 * X * Y
D, E = 2560, 1280
TOK, U, R_DEV = 128, 144, 40
HALF = E // 2
TROWS = 48
MSG = 2 * Z
PLACES = PLANE * MSG
CB = 512
NB = 2 * D // CB
WROWS = 80

MESH = pl.DeviceIdType.MESH
F32, BF16, I32 = jnp.float32, jnp.bfloat16, jnp.int32


class Here:
    def __init__(self):
        self.row = lax.axis_index("row")
        self.col = lax.axis_index("col")
        self.z = self.row // 2
        self.core = self.row % 2
        self.x = self.col // Y
        self.y = self.col % Y
        self.plane = self.core * (X * Y) + self.col

    def mate(self, i):
        q = lax.rem(self.plane + i, PLANE)
        return q, (self.z * 2 + q // (X * Y), q % (X * Y))

    def zed(self, step):
        return lax.rem(self.z + step + Z, Z)

    def at_z(self, step):
        return (self.zed(step) * 2 + self.core, self.col)

    def exx(self, step):
        return lax.rem(self.x + step + X, X)

    def wye(self, step):
        return lax.rem(self.y + step + Y, Y)

    def at_x(self, step):
        return (self.row, self.exx(step) * Y + self.y)

    def at_y(self, step):
        return (self.row, self.x * Y + self.wye(step))

    def partner(self):
        return (self.z * 2 + 1 - self.core, self.col)


def remote(src, dst, send, recv, device):
    return pltpu.make_async_remote_copy(
        src_ref=src, dst_ref=dst, send_sem=send, recv_sem=recv, device_id=device, device_id_type=MESH
    )


def greet(here):
    barrier = pltpu.get_barrier_semaphore()

    def one(i, carry):
        _, device = here.mate(i)
        pl.semaphore_signal(barrier, inc=1, device_id=device, device_id_type=MESH)
        return carry

    lax.fori_loop(1, PLANE, one, 0)
    for step in (1, -1):
        pl.semaphore_signal(barrier, inc=1, device_id=here.at_z(step), device_id_type=MESH)
    return lambda: pl.semaphore_wait(barrier, PLANE + 1)


def iota(shape, dim):
    return lax.broadcasted_iota(I32, shape, dim)


def one_hot(mask):
    return jnp.where(mask, 1.0, 0.0).astype(BF16)


def plan_slots(owner_ref, local_ref, expand_ref, spread, req_out):
    owner_c = owner_ref[...]
    eye = iota((U, U), 0) == iota((U, U), 1)
    owner_r = jnp.sum(jnp.where(eye, owner_c, 0), axis=0, keepdims=True)
    local_c = jnp.sum(jnp.where(eye, local_ref[...], 0), axis=1, keepdims=True)
    before = (owner_c == owner_r) & (iota((U, U), 1) < iota((U, U), 0))
    rank_c = jnp.sum(jnp.where(before, 1, 0), axis=1, keepdims=True)
    k_c = (owner_c >> 5) * 2 + rank_c
    place_c = (owner_c & 31) * MSG + k_c
    mates = one_hot((owner_r & 31) == iota((PLANE, U), 0))
    wanted = jnp.where(k_c == iota((U, 128), 1), local_c + 1, 0).astype(F32).astype(BF16)
    request = jnp.dot(mates, wanted, preferred_element_type=F32)
    for q in range(PLANE):
        req_out[q] = request[q : q + 1, :]
    expand = expand_ref[...]
    reads = jnp.zeros((TOK, U), F32)
    for lookup in range(2):
        reads = reads + jnp.where(expand[:, lookup : lookup + 1] == iota((TOK, U), 1), 1.0, 0.0)
    places = one_hot(place_c == iota((U, PLACES), 1))
    spread[...] = jnp.dot(reads.astype(BF16), places, preferred_element_type=F32).astype(BF16)


def plan_serve(req_in, serve):
    asked = req_in[:, 0, :].astype(BF16)
    owner_rows = one_hot(iota((PLACES, PLANE), 0) // MSG == iota((PLACES, PLANE), 1))
    wide = jnp.dot(owner_rows, asked, preferred_element_type=F32)
    k = iota((PLACES, 128), 0) % MSG
    value = jnp.sum(jnp.where(k == iota((PLACES, 128), 1), wide, 0.0), axis=1, keepdims=True)
    zed = (iota((PLACES, 1), 0) % MSG) // 2
    target = jnp.where(value > 0.5, zed * TROWS + value.astype(I32) - 1, -1)
    serve[...] = one_hot(target == iota((PLACES, Z * TROWS), 1))


def send_mates(here, src, dst, send, recv):
    def one(i, carry):
        q, device = here.mate(i)
        remote(src.at[q], dst.at[here.plane], send, recv, device).start()
        return carry

    lax.fori_loop(1, PLANE, one, 0)


def mates_arrived(here, dst, recv):
    ref = dst.at[pl.ds(0, PLANE - 1)]
    pltpu.make_async_copy(ref, ref, recv).wait()


def mates_sent(here, src, send):
    ref = src.at[pl.ds(0, PLANE - 1)]
    pltpu.make_async_copy(ref, ref, send).wait()


class Ring:
    def __init__(self, here, block, send, recv, far):
        self.here, self.block, self.send, self.recv, self.far = here, block, send, recv, far

    def copy(self, way, step):
        sign = 1 if way == 0 else -1
        ref = self.block(self.here.zed(-sign * (step - 1)))
        return remote(ref, ref, self.send.at[way, step - 1], self.recv.at[way, step - 1], self.here.at_z(sign))

    def steps(self, way):
        return Z // 2 if way == self.far else Z // 2 - 1

    def start(self, step):
        for way in range(2):
            if step <= self.steps(way):
                self.copy(way, step).start()

    def arrived(self, step):
        got = []
        for way in range(2):
            if step <= self.steps(way):
                sign = 1 if way == 0 else -1
                ref = self.block(self.here.zed(-sign * step))
                remote(ref, ref, self.send.at[way, step - 1], self.recv.at[way, step - 1], self.here.at_z(-sign)).wait_recv()
                got.append(-sign * step)
        return got

    def drain(self):
        for way in range(2):
            for step in range(1, self.steps(way) + 1):
                self.copy(way, step).wait_send()


class Cross:
    def __init__(self, here, axis, weights, base, send, recv):
        self.here, self.weights, self.base, self.send, self.recv = here, weights, base, send, recv
        self.at = here.at_x if axis == "x" else here.at_y
        self.place = here.exx if axis == "x" else here.wye

    def copy(self, way, zz, i):
        sign = 1 if way % 2 == 0 else -1
        if way < 2:
            ref = self.weights.at[self.base + self.place(0), zz, self.here.core]
        else:
            ref = self.weights.at[self.base + self.place(-sign), zz, self.here.core, :, pl.ds((way - 2) * (CB // 2), CB // 2)]
        return remote(ref, ref, self.send.at[way, i], self.recv.at[way, i], self.at(sign))

    def got(self, way, zz, i):
        sign = 1 if way % 2 == 0 else -1
        if way < 2:
            ref = self.weights.at[self.base + self.place(-sign), zz, self.here.core]
        else:
            ref = self.weights.at[
                self.base + self.place(-2 * sign), zz, self.here.core, :, pl.ds((way - 2) * (CB // 2), CB // 2)
            ]
        return remote(ref, ref, self.send.at[way, i], self.recv.at[way, i], self.at(-sign))

    def start(self, zz, i):
        for way in (0, 1):
            self.copy(way, zz, i).start()

    def relay(self, zz, i):
        for way in (0, 1):
            self.got(way, zz, i).wait_recv()
            self.copy(way + 2, zz, i).start()

    def finish(self, zz, i):
        for way in (2, 3):
            self.got(way, zz, i).wait_recv()

    def drain(self, zz, i):
        for way in range(4):
            self.copy(way, zz, i).wait_send()


def gather_kernel(
    owner_ref, local_ref, expand_ref, table_ref, wk_ref, wv_ref,
    memory_ref, spread_ref, serve_ref, key_ref, value_ref,
    weights, tab, req_out, req_in, reply, fetched,
    load_sem, store_sem, req_send, req_recv, rep_send, rep_recv, tz_send, tz_recv, wz_send, wz_recv,
    xy_send, xy_recv, core_send, core_recv,
):
    here = Here()
    greeted = greet(here)
    loads = []
    for b in range(NB):
        src = wk_ref if b < NB // 2 else wv_ref
        loads.append(
            pltpu.make_async_copy(
                src.at[:, pl.ds((b % (NB // 2)) * CB, CB)], weights.at[b, here.z, here.core], load_sem.at[b]
            )
        )
        loads[-1].start()
    for h in range(2):
        tab[h, here.z, 0:R_DEV, :] = table_ref[:, h * HALF : (h + 1) * HALF].astype(BF16)
        tab[h, here.z, R_DEV:TROWS, :] = jnp.zeros((TROWS - R_DEV, HALF), BF16)
    plan_slots(owner_ref, local_ref, expand_ref, spread_ref, req_out)
    greeted()

    tables = [Ring(here, lambda zz, h=h: tab.at[h, zz], tz_send.at[h], tz_recv.at[h], h) for h in range(2)]
    for ring in tables:
        ring.start(1)
    send_mates(here, req_out, req_in, req_send, req_recv)
    req_in[here.plane] = req_out[here.plane]
    for load in loads:
        load.wait()
    crosses = [
        Cross(here, "x", weights, 0, xy_send.at[0], xy_recv.at[0]),
        Cross(here, "y", weights, NB // 2, xy_send.at[1], xy_recv.at[1]),
    ]
    order = [0, -1, 1, -2, 2, -3, 3, 4]
    zeds = [here.zed(step) for step in order]
    for step in (2, 3, 4):
        for ring in tables:
            ring.arrived(step - 1)
            ring.start(step)
    blocks = [here.x, NB // 2 + here.y, NB // 2 - 1, NB - 1]
    pieces = [
        Ring(here, lambda zz, b=b: weights.at[b, zz, here.core], wz_send.at[i], wz_recv.at[i], i % 2)
        for i, b in enumerate(blocks)
    ]
    for ring in pieces[:2]:
        ring.start(1)
    mates_arrived(here, req_in, req_recv)
    plan_serve(req_in, serve_ref)
    for h in range(2):
        tables[h].arrived(4)
        rows = jnp.dot(serve_ref[...], tab[h].reshape(Z * TROWS, HALF), preferred_element_type=F32)
        reply[h] = rows.astype(BF16).reshape(PLANE, MSG, HALF)
        fetched[h, here.plane] = reply[h, here.plane]
        send_mates(here, reply.at[h], fetched.at[h], rep_send.at[h], rep_recv.at[h])
    seen = 1
    relayed = 1
    for step in (1, 2, 3, 4):
        for ring in pieces[:2]:
            ring.arrived(step)
            if step < 4:
                ring.start(step + 1)
        if step == 3:
            for ring in pieces[2:]:
                ring.start(1)
        upto = min(Z, seen + 2)
        for i in range(seen, upto):
            for cross in crosses:
                cross.start(zeds[i], i)
        for i in range(relayed, seen):
            for cross in crosses:
                cross.relay(zeds[i], i)
        relayed, seen = seen, upto
    for i in range(relayed, Z):
        for cross in crosses:
            cross.relay(zeds[i], i)

    def to_partner(b):
        ref = weights.at[b, :, here.core]
        return remote(ref, ref, core_send.at[b], core_recv.at[b], here.partner())

    for b in (here.x, NB // 2 + here.y):
        to_partner(b).start()
    for step in (-1, 1):
        to_partner(here.exx(step)).start()
        to_partner(NB // 2 + here.wye(step)).start()
    for step in (1, 2, 3, 4):
        for ring in pieces[2:]:
            ring.arrived(step)
            if step < 4:
                ring.start(step + 1)
    for b in (NB // 2 - 1, NB - 1):
        to_partner(b).start()
    for i in range(1, Z):
        for cross in crosses:
            cross.finish(zeds[i], i)
    to_partner(here.exx(2)).start()
    to_partner(NB // 2 + here.wye(2)).start()
    for h in range(2):
        mates_arrived(here, fetched.at[h], rep_recv.at[h])
        memory_ref[:, h * HALF : (h + 1) * HALF] = jnp.dot(
            spread_ref[...], fetched[h].reshape(PLACES, HALF), preferred_element_type=F32
        ).astype(BF16)

    stores = []
    for b in range(NB):
        ref = weights.at[b, :, 1 - here.core]
        remote(ref, ref, core_send.at[b], core_recv.at[b], here.partner()).wait_recv()
        dst = key_ref if b < NB // 2 else value_ref
        stores.append(
            pltpu.make_async_copy(
                weights.at[b], dst.at[:, :, :, pl.ds((b % (NB // 2)) * CB, CB)], store_sem.at[b]
            )
        )
        stores[-1].start()
    for b in range(NB):
        to_partner(b).wait_send()
    for ring in tables + pieces:
        ring.drain()
    for i in range(1, Z):
        for cross in crosses:
            cross.drain(zeds[i], i)
    mates_sent(here, req_out, req_send)
    for h in range(2):
        mates_sent(here, reply.at[h], rep_send.at[h])
    for store in stores:
        store.wait()


def gather_call(owner, local, expand, table, w_key, w_value):
    vmem = pl.BlockSpec(memory_space=pltpu.VMEM)
    any_ = pl.BlockSpec(memory_space=pl.ANY)
    dma = pltpu.SemaphoreType.DMA
    return pl.pallas_call(
        gather_kernel,
        out_shape=(
            jax.ShapeDtypeStruct((TOK, E), BF16),
            jax.ShapeDtypeStruct((TOK, PLACES), BF16),
            jax.ShapeDtypeStruct((PLACES, Z * TROWS), BF16),
            jax.ShapeDtypeStruct((Z, 2, WROWS, D), BF16),
            jax.ShapeDtypeStruct((Z, 2, WROWS, D), BF16),
        ),
        in_specs=[vmem, vmem, vmem, vmem, any_, any_],
        out_specs=(vmem, vmem, vmem, any_, any_),
        scratch_shapes=[
            pltpu.VMEM((NB, Z, 2, WROWS, CB), BF16),
            pltpu.VMEM((2, Z, TROWS, HALF), BF16),
            pltpu.VMEM((PLANE, 1, 128), F32),
            pltpu.VMEM((PLANE, 1, 128), F32),
            pltpu.VMEM((2, PLANE, MSG, HALF), BF16),
            pltpu.VMEM((2, PLANE, MSG, HALF), BF16),
            dma((NB,)), dma((NB,)), dma, dma, dma((2,)), dma((2,)),
            dma((2, 2, 4)), dma((2, 2, 4)), dma((4, 2, 4)), dma((4, 2, 4)),
            dma((2, 4, Z)), dma((2, 4, Z)), dma((NB,)), dma((NB,)),
        ],
        compiler_params=pltpu.CompilerParams(
            collective_id=0, has_side_effects=True, vmem_limit_bytes=48 * 1024 * 1024
        ),
        name="gather_rows_and_weights",
    )(owner, local, expand, table, w_key, w_value)


def adamw(current, moment, second, gradient):
    moment_new = BETA_ONE * moment + (1.0 - BETA_ONE) * gradient
    second_new = BETA_TWO * second + (1.0 - BETA_TWO) * gradient * gradient
    first_hat = moment_new / (1.0 - BETA_ONE**STEP_COUNT)
    second_hat = second_new / (1.0 - BETA_TWO**STEP_COUNT)
    updated = current - LEARN_RATE * (first_hat / (jnp.sqrt(second_hat) + ADAM_EPS) + DECAY_RATE * current)
    return updated, moment_new, second_new


def transposed_dot(left, right):
    return lax.dot_general(left, right, (((0,), (0,)), ((), ())), preferred_element_type=F32)


def return_kernel(
    grad_ref, spread_ref, serve_ref, table_ref, m_ref, v_ref,
    out_table, out_m, out_v,
    slots, arrived, partial, give, take,
    slot_send, slot_recv, ring_send, ring_recv,
):
    here = Here()
    greeted = greet(here)
    for h in range(2):
        lanes = slice(h * HALF, (h + 1) * HALF)
        rows = transposed_dot(spread_ref[...], grad_ref[:, lanes])
        slots[h] = rows.astype(BF16).reshape(PLANE, MSG, HALF)
        arrived[h, here.plane] = slots[h, here.plane]
    greeted()
    for h in range(2):
        send_mates(here, slots.at[h], arrived.at[h], slot_send.at[h], slot_recv.at[h])

    def hop(h, way, step):
        sign = 1 if way == 0 else -1
        return remote(
            give.at[h, way, step - 1], take.at[h, way, step - 1],
            ring_send.at[h, way, step - 1], ring_recv.at[h, way, step - 1], here.at_z(sign),
        )

    def length(h, way):
        return Z // 2 if way == h else Z // 2 - 1

    def advance(h, step):
        for way in range(2):
            last = length(h, way)
            if step > last:
                continue
            sign = 1 if way == 0 else -1
            mine = partial[h, here.zed(sign * (last - step + 1))]
            if step > 1:
                hop(h, way, step - 1).wait_recv()
                mine = mine + take[h, way, step - 2].astype(F32)
            give[h, way, step - 1] = mine.astype(BF16)
            hop(h, way, step).start()

    for h in range(2):
        mates_arrived(here, arrived.at[h], slot_recv.at[h])
        rows = transposed_dot(serve_ref[...], arrived[h].reshape(PLACES, HALF))
        partial[h] = rows.reshape(Z, TROWS, HALF)
        advance(h, 1)
    for step in (2, 3, 4):
        for h in range(2):
            advance(h, step)
    for h in range(2):
        lanes = slice(h * HALF, (h + 1) * HALF)
        total = partial[h, here.z]
        for way in range(2):
            last = length(h, way)
            hop(h, way, last).wait_recv()
            total = total + take[h, way, last - 1].astype(F32)
        new_t, new_m, new_v = adamw(table_ref[:, lanes], m_ref[:, lanes], v_ref[:, lanes], total[:R_DEV])
        out_table[:, lanes] = new_t
        out_m[:, lanes] = new_m
        out_v[:, lanes] = new_v
    for h in range(2):
        mates_sent(here, slots.at[h], slot_send.at[h])
        for way in range(2):
            for step in range(1, length(h, way) + 1):
                hop(h, way, step).wait_send()


def return_call(memory_grad, spread, serve, table, adam_m, adam_v):
    vmem = pl.BlockSpec(memory_space=pltpu.VMEM)
    dma = pltpu.SemaphoreType.DMA
    return pl.pallas_call(
        return_kernel,
        out_shape=tuple(jax.ShapeDtypeStruct((R_DEV, E), F32) for _ in range(3)),
        in_specs=[vmem] * 6,
        out_specs=(vmem,) * 3,
        scratch_shapes=[
            pltpu.VMEM((2, PLANE, MSG, HALF), BF16),
            pltpu.VMEM((2, PLANE, MSG, HALF), BF16),
            pltpu.VMEM((2, Z, TROWS, HALF), F32),
            pltpu.VMEM((2, 2, 4, TROWS, HALF), BF16),
            pltpu.VMEM((2, 2, 4, TROWS, HALF), BF16),
            dma((2,)), dma((2,)), dma((2, 2, 4)), dma((2, 2, 4)),
        ],
        compiler_params=pltpu.CompilerParams(
            collective_id=1, has_side_effects=True, vmem_limit_bytes=32 * 1024 * 1024
        ),
        name="return_row_gradients",
    )(memory_grad, spread, serve, table, adam_m, adam_v)


def from_behind(value, axis, steps):
    count = lax.axis_size(axis)
    first, last = (max(0, -steps), min(count, count - steps))
    return lax.ppermute(value, axis, [(source, source + steps) for source in range(first, last)])


def rms_scale(values):
    return lax.rsqrt(jnp.mean(values * values, axis=-1, keepdims=True) + NORM_EPS)


def doc_index(positions, lengths):
    k = jnp.arange(lengths.shape[0], dtype=jnp.int32)
    doc_ends = jnp.sum(jnp.where(k[None, :] <= k[:, None], lengths[None, :], 0), axis=1)
    return jnp.sum((positions[:, None] >= doc_ends[None, :-1]).astype(jnp.int32), axis=1)


def contract_last(left, right):
    return lax.dot_general(
        left, right, (((1,), (1,)), ((), ())), preferred_element_type=jnp.float32
    )


def on_device(
    hidden, grad_out, w_key, w_value, depthwise_weight, table, adam_m, adam_v,
    row_owner, row_local, expand_index, doc_lengths,
):
    tok_count = hidden.shape[1]
    model_width = hidden.shape[2]
    kernel_taps = depthwise_weight.shape[0]
    border_rows = DILATION_STEP * (kernel_taps - 1)
    root_width = jnp.sqrt(jnp.float32(model_width))
    memory, spread, serve, key_full, value_full = gather_call(
        row_owner[0], row_local, expand_index[0], table, w_key, w_value
    )
    key_full = key_full.reshape(E, D)
    value_full = value_full.reshape(E, D)
    key = jnp.dot(memory, key_full, preferred_element_type=jnp.float32)
    value = jnp.dot(memory, value_full, preferred_element_type=jnp.float32)
    key_scale = rms_scale(key)
    key_norm = key * key_scale
    hidden_f = hidden[0].astype(jnp.float32)
    hidden_norm = hidden_f * rms_scale(hidden_f)
    gate = jax.nn.sigmoid(jnp.sum(hidden_norm * key_norm, axis=-1, keepdims=True) / root_width)
    gated = (gate * value).astype(jnp.bfloat16)
    gated_f = gated.astype(jnp.float32)
    gated_scale = rms_scale(gated_f)
    gated_normalized = gated_f * gated_scale
    lengths = doc_lengths[0]
    first_pos = lax.axis_index("col") * tok_count
    earlier = from_behind(gated[tok_count - border_rows :], "col", 1)
    extended = jnp.concatenate([earlier, gated], axis=0).astype(jnp.float32)
    extended_norm = extended * rms_scale(extended)
    pos_before = first_pos - border_rows + jnp.arange(tok_count + border_rows, dtype=jnp.int32)
    doc_before = doc_index(pos_before, lengths)
    doc_here = doc_before[border_rows:]
    convolved_rows = jnp.zeros((tok_count, model_width), jnp.float32)
    for kernel_tap_index in range(kernel_taps):
        shift_amount = kernel_tap_index * DILATION_STEP
        source_pos = pos_before[border_rows - shift_amount : border_rows - shift_amount + tok_count]
        source_doc = doc_before[border_rows - shift_amount : border_rows - shift_amount + tok_count]
        same_doc = ((source_pos >= 0) & (source_doc == doc_here)).astype(jnp.float32)[:, None]
        convolved_rows = (
            convolved_rows
            + depthwise_weight[kernel_tap_index]
            * extended_norm[border_rows - shift_amount : border_rows - shift_amount + tok_count]
            * same_doc
        )
    memory_out = (jax.nn.silu(convolved_rows) + gated_f).astype(jnp.bfloat16)
    grad_f = grad_out[0].astype(jnp.float32)
    sig = jax.nn.sigmoid(convolved_rows)
    convolution_gradient = grad_f * sig * (1.0 + convolved_rows * (1.0 - sig))
    next_rows = from_behind(
        convolution_gradient[:border_rows].astype(jnp.bfloat16), "col", -1
    ).astype(jnp.float32)
    grad_ext = jnp.concatenate([convolution_gradient, next_rows], axis=0)
    pos_after = first_pos + jnp.arange(tok_count + border_rows, dtype=jnp.int32)
    doc_after = doc_index(pos_after, lengths)
    normalized_gradient = jnp.zeros((tok_count, model_width), jnp.float32)
    for kernel_tap_index in range(kernel_taps):
        shift_amount = kernel_tap_index * DILATION_STEP
        same_doc = (
            doc_after[shift_amount : shift_amount + tok_count] == doc_after[:tok_count]
        ).astype(jnp.float32)[:, None]
        normalized_gradient = normalized_gradient + depthwise_weight[kernel_tap_index] * (
            grad_ext[shift_amount : shift_amount + tok_count] * same_doc
        )
    gated_grad = grad_f + gated_scale * (
        normalized_gradient
        - gated_normalized
        * jnp.mean(gated_normalized * normalized_gradient, axis=-1, keepdims=True)
    )
    value_grad = gated_grad * gate
    score_grad = gate * (1.0 - gate) * jnp.sum(gated_grad * value, axis=-1, keepdims=True)
    target = score_grad * hidden_norm / root_width
    key_grad = key_scale * (target - key_norm * jnp.mean(key_norm * target, axis=-1, keepdims=True))
    key_grad16 = key_grad.astype(jnp.bfloat16)
    value_grad16 = value_grad.astype(jnp.bfloat16)
    memory_grad = (
        contract_last(key_grad16, key_full) + contract_last(value_grad16, value_full)
    ).astype(jnp.bfloat16)
    new_table, new_moment, new_second = return_call(memory_grad, spread, serve, table, adam_m, adam_v)
    return (memory_out[None], new_table, new_moment, new_second)


def solution(mesh):
    placed = (
        P("row", "col", None),
        P("row", "col", None),
        P("row", None),
        P("row", None),
        P(),
        P(("row", "col"), None),
        P(("row", "col"), None),
        P(("row", "col"), None),
        P("row", "col", None),
        P("row", "col"),
        P("row", "col", None),
        P("row", None),
    )
    return jax.shard_map(
        on_device,
        mesh=mesh,
        in_specs=placed,
        out_specs=(
            P("row", "col", None),
            P(("row", "col"), None),
            P(("row", "col"), None),
            P(("row", "col"), None),
        ),
        check_vma=False,
    )
```

```python
import jax
import jax.numpy as jnp
from jax import lax
from jax.experimental import pallas as pl
from jax.experimental.pallas import tpu as pltpu
from jax.sharding import PartitionSpec as P

DILATION_STEP = 3
NORM_EPS = 1e-06
BETA_ONE = 0.9
BETA_TWO = 0.95
ADAM_EPS = 1e-08
LEARN_RATE = 0.01
DECAY_RATE = 0.1
STEP_COUNT = 10.0

Z, X, Y = 8, 4, 4
PLANE = 2 * X * Y
D, E = 2560, 1280
TOK, U, R_DEV = 128, 144, 40
CW = 256
NC = E // CW
TROWS = 48
MSG = 2 * Z
PLACES = PLANE * MSG
CB = 512
NB = 2 * D // CB
WROWS = 80
TILE = 16
PAD = 16
TAPS = 4

MESH = pl.DeviceIdType.MESH
F32, BF16, I32 = jnp.float32, jnp.bfloat16, jnp.int32


class Here:
    def __init__(self):
        self.row = lax.axis_index("row")
        self.col = lax.axis_index("col")
        self.z = self.row // 2
        self.core = self.row % 2
        self.x = self.col // Y
        self.y = self.col % Y
        self.plane = self.core * (X * Y) + self.col

    def mate(self, i):
        q = lax.rem(self.plane + i, PLANE)
        return q, (self.z * 2 + q // (X * Y), q % (X * Y))

    def zed(self, step):
        return lax.rem(self.z + step + Z, Z)

    def at_z(self, step):
        return (self.zed(step) * 2 + self.core, self.col)

    def exx(self, step):
        return lax.rem(self.x + step + X, X)

    def wye(self, step):
        return lax.rem(self.y + step + Y, Y)

    def at_x(self, step):
        return (self.row, self.exx(step) * Y + self.y)

    def at_y(self, step):
        return (self.row, self.x * Y + self.wye(step))

    def partner(self):
        return (self.z * 2 + 1 - self.core, self.col)


def remote(src, dst, send, recv, device):
    return pltpu.make_async_remote_copy(
        src_ref=src, dst_ref=dst, send_sem=send, recv_sem=recv, device_id=device, device_id_type=MESH
    )


def greet(here):
    barrier = pltpu.get_barrier_semaphore()

    def one(i, carry):
        _, device = here.mate(i)
        pl.semaphore_signal(barrier, inc=1, device_id=device, device_id_type=MESH)
        return carry

    lax.fori_loop(1, PLANE, one, 0)
    for step in (1, -1):
        pl.semaphore_signal(barrier, inc=1, device_id=here.at_z(step), device_id_type=MESH)
    return lambda: pl.semaphore_wait(barrier, PLANE + 1)


def iota(shape, dim):
    return lax.broadcasted_iota(I32, shape, dim)


def one_hot(mask):
    return jnp.where(mask, 1.0, 0.0).astype(BF16)


def nn(left, right):
    return jnp.dot(left, right, preferred_element_type=F32)


def tn(left, right):
    return lax.dot_general(left, right, (((0,), (0,)), ((), ())), preferred_element_type=F32)


def nt(left, right):
    return lax.dot_general(left, right, (((1,), (1,)), ((), ())), preferred_element_type=F32)


def column_of(row, size):
    eye = iota((size, size), 0) == iota((size, size), 1)
    return jnp.sum(jnp.where(eye, row, 0), axis=1, keepdims=True)


def plan_slots(owner_ref, local_ref, expand_ref, spread, spread_t, req_out):
    owner_r = owner_ref[...]
    owner_c = column_of(owner_r, U)
    local_c = column_of(local_ref[...], U)
    same = owner_c == owner_r
    earlier_c = same & (iota((U, U), 1) < iota((U, U), 0))
    earlier_r = same & (iota((U, U), 0) < iota((U, U), 1))
    k_c = (owner_c >> 5) * 2 + jnp.sum(jnp.where(earlier_c, 1, 0), axis=1, keepdims=True)
    k_r = (owner_r >> 5) * 2 + jnp.sum(jnp.where(earlier_r, 1, 0), axis=0, keepdims=True)
    mates = one_hot((owner_r & 31) == iota((PLANE, U), 0))
    wanted = jnp.where(k_c == iota((U, 128), 1), local_c + 1, 0).astype(F32).astype(BF16)
    request = nn(mates, wanted)
    for q in range(PLANE):
        req_out[q] = request[q : q + 1, :]
    expand = expand_ref[...]
    reads = jnp.zeros((U, TOK), F32)
    for lookup in range(2):
        reads = reads + jnp.where(expand[lookup : lookup + 1, :] == iota((U, TOK), 0), 1.0, 0.0)
    reads = reads.astype(BF16)
    places = one_hot((owner_c & 31) * MSG + k_c == iota((U, PLACES), 1))
    places_t = one_hot((owner_r & 31) * MSG + k_r == iota((PLACES, U), 0))
    spread[...] = tn(reads, places).astype(BF16)
    spread_t[...] = nn(places_t, reads).astype(BF16)


def plan_serve(req_in, serve, serve_t):
    asked = req_in[:, 0, :].astype(BF16)
    wide = nn(one_hot(iota((PLACES, PLANE), 0) // MSG == iota((PLACES, PLANE), 1)), asked)
    k = iota((PLACES, 128), 0) % MSG
    value = jnp.sum(jnp.where(k == iota((PLACES, 128), 1), wide, 0.0), axis=1, keepdims=True)
    zed = (iota((PLACES, 1), 0) % MSG) // 2
    target = jnp.where(value > 0.5, zed * TROWS + value.astype(I32) - 1, -1)
    serve[...] = one_hot(target == iota((PLACES, Z * TROWS), 1))
    tall = tn(asked, one_hot(iota((PLANE, PLACES), 1) // MSG == iota((PLANE, PLACES), 0)))
    k = iota((128, PLACES), 1) % MSG
    value = jnp.sum(jnp.where(k == iota((128, PLACES), 0), tall, 0.0), axis=0, keepdims=True)
    zed = (iota((1, PLACES), 1) % MSG) // 2
    target = jnp.where(value > 0.5, zed * TROWS + value.astype(I32) - 1, -1)
    serve_t[...] = one_hot(target == iota((Z * TROWS, PLACES), 0))


def plan_docs(here, lengths_ref, docs):
    n = lengths_ref.shape[1]
    length_c = column_of(lengths_ref[...], n)
    ends = jnp.sum(jnp.where(iota((n, n), 0) <= iota((n, n), 1), length_c, 0), axis=0, keepdims=True)
    rows = docs.shape[0]
    position = here.col * TOK - PAD + iota((rows, 1), 0)
    passed = (position >= ends) & (iota((rows, n), 1) < n - 1)
    doc = jnp.sum(jnp.where(passed, 1.0, 0.0), axis=1, keepdims=True)
    doc = jnp.where(position < 0, -1.0, jnp.where(position >= 16 * TOK, -2.0, doc))
    docs[...] = jnp.broadcast_to(doc, (rows, 128))


def send_mates(here, src, dst, send, recv):
    def one(i, carry):
        q, device = here.mate(i)
        remote(src.at[q], dst.at[here.plane], send, recv, device).start()
        return carry

    lax.fori_loop(1, PLANE, one, 0)


def mates_arrived(here, dst, recv):
    ref = dst.at[pl.ds(0, PLANE - 1)]
    pltpu.make_async_copy(ref, ref, recv).wait()


def mates_sent(here, src, send):
    ref = src.at[pl.ds(0, PLANE - 1)]
    pltpu.make_async_copy(ref, ref, send).wait()


class Ring:
    def __init__(self, here, block, send, recv, far):
        self.here, self.block, self.send, self.recv, self.far = here, block, send, recv, far

    def copy(self, way, step):
        sign = 1 if way == 0 else -1
        ref = self.block(self.here.zed(-sign * (step - 1)))
        return remote(ref, ref, self.send.at[way, step - 1], self.recv.at[way, step - 1], self.here.at_z(sign))

    def steps(self, way):
        return Z // 2 if way == self.far else Z // 2 - 1

    def start(self, step):
        for way in range(2):
            if step <= self.steps(way):
                self.copy(way, step).start()

    def arrived(self, step):
        got = []
        for way in range(2):
            if step <= self.steps(way):
                sign = 1 if way == 0 else -1
                ref = self.block(self.here.zed(-sign * step))
                remote(ref, ref, self.send.at[way, step - 1], self.recv.at[way, step - 1], self.here.at_z(-sign)).wait_recv()
                got.append(-sign * step)
        return got

    def drain(self):
        for way in range(2):
            for step in range(1, self.steps(way) + 1):
                self.copy(way, step).wait_send()


class Cross:
    def __init__(self, here, axis, weights, base, send, recv):
        self.here, self.weights, self.base, self.send, self.recv = here, weights, base, send, recv
        self.at = here.at_x if axis == "x" else here.at_y
        self.place = here.exx if axis == "x" else here.wye

    def copy(self, way, zz, i):
        sign = 1 if way % 2 == 0 else -1
        if way < 2:
            ref = self.weights.at[self.base + self.place(0), zz, self.here.core]
        else:
            ref = self.weights.at[self.base + self.place(-sign), zz, self.here.core, :, pl.ds((way - 2) * (CB // 2), CB // 2)]
        return remote(ref, ref, self.send.at[way, i], self.recv.at[way, i], self.at(sign))

    def got(self, way, zz, i):
        sign = 1 if way % 2 == 0 else -1
        if way < 2:
            ref = self.weights.at[self.base + self.place(-sign), zz, self.here.core]
        else:
            ref = self.weights.at[
                self.base + self.place(-2 * sign), zz, self.here.core, :, pl.ds((way - 2) * (CB // 2), CB // 2)
            ]
        return remote(ref, ref, self.send.at[way, i], self.recv.at[way, i], self.at(-sign))

    def start(self, zz, i):
        for way in (0, 1):
            self.copy(way, zz, i).start()

    def relay(self, zz, i):
        for way in (0, 1):
            self.got(way, zz, i).wait_recv()
            self.copy(way + 2, zz, i).start()

    def finish(self, zz, i):
        for way in (2, 3):
            self.got(way, zz, i).wait_recv()

    def drain(self, zz, i):
        for way in range(4):
            self.copy(way, zz, i).wait_send()


def lanes(b):
    return slice((b % (NB // 2)) * CB, (b % (NB // 2) + 1) * CB)


def row_tile(t):
    return pl.ds(pl.multiple_of(t * TILE, TILE), TILE)


def mean_scale(total):
    return lax.rsqrt(total / D + NORM_EPS)


BLOCKS = range(NB // 2)
STATS = ("key_scale", "hidden_scale", "score", "gate", "gated_scale")


def keep(stats, name, rows, value):
    stats[STATS.index(name), rows, :] = jnp.broadcast_to(value, (TILE, 128))


def kept(stats, name, rows):
    return stats[STATS.index(name), rows, :][:, 0:1]


def gate_tile(t, keys, values, hidden, gated, gnorm, stats):
    rows = row_tile(t)
    kk = jnp.zeros((TILE, CB), F32)
    hh, hk = kk, kk
    for b in BLOCKS:
        key = keys[b, rows, :]
        hid = hidden[rows, lanes(b)].astype(F32)
        kk, hh, hk = kk + key * key, hh + hid * hid, hk + hid * key
    key_scale = mean_scale(jnp.sum(kk, axis=1, keepdims=True))
    hidden_scale = mean_scale(jnp.sum(hh, axis=1, keepdims=True))
    score = jnp.sum(hk, axis=1, keepdims=True) * key_scale * hidden_scale
    gate = jax.nn.sigmoid(score / D**0.5)
    gg = jnp.zeros((TILE, CB), F32)
    for b in BLOCKS:
        rounded = (gate * values[b, rows, :]).astype(BF16)
        gated[rows, lanes(b)] = rounded
        gg = gg + rounded.astype(F32) * rounded.astype(F32)
    scale = mean_scale(jnp.sum(gg, axis=1, keepdims=True))
    own = pl.ds(pl.multiple_of(PAD + t * TILE, TILE), TILE)
    for b in BLOCKS:
        gnorm[own, lanes(b)] = gated[rows, lanes(b)].astype(F32) * scale
    for name, value in zip(STATS, (key_scale, hidden_scale, score, gate, scale)):
        keep(stats, name, rows, value)


def same_docs(docs, t, sign):
    window = docs[pl.ds(pl.multiple_of(t * TILE, TILE), 3 * TILE), :][:, 0:1]
    center = window[TILE : 2 * TILE]
    shifted = [window[TILE + sign * DILATION_STEP * j : 2 * TILE + sign * DILATION_STEP * j] for j in range(TAPS)]
    return [center == other for other in shifted]


def conv_tile(t, docs, taps, gnorm, gated, grad, cgrad, out):
    rows = row_tile(t)
    masks = same_docs(docs, t, -1)
    both = pl.ds(pl.multiple_of(t * TILE, TILE), 2 * TILE)
    for b in BLOCKS:
        window = gnorm[both, lanes(b)]
        conv = taps[0:1, lanes(b)] * window[TILE:]
        for j in range(1, TAPS):
            low = TILE - DILATION_STEP * j
            conv = conv + jnp.where(masks[j], taps[j : j + 1, lanes(b)] * window[low : low + TILE], 0.0)
        sig = jax.nn.sigmoid(conv)
        out[rows, lanes(b)] = (conv * sig + gated[rows, lanes(b)].astype(F32)).astype(BF16)
        cgrad[rows, lanes(b)] = grad[rows, lanes(b)].astype(F32) * sig * (1.0 + conv * (1.0 - sig))


def grad_tile(t, docs, taps, gnorm, cgrad, grad, keys, values, hidden, stats, ngrad, key_grad, value_grad):
    rows = row_tile(t)
    masks = same_docs(docs, t, 1)
    both = pl.ds(pl.multiple_of(t * TILE, TILE), 2 * TILE)
    own = pl.ds(pl.multiple_of(PAD + t * TILE, TILE), TILE)
    dots = jnp.zeros((TILE, CB), F32)
    for b in BLOCKS:
        window = cgrad[both, lanes(b)]
        total = taps[0:1, lanes(b)] * window[:TILE]
        for j in range(1, TAPS):
            low = DILATION_STEP * j
            total = total + jnp.where(masks[j], taps[j : j + 1, lanes(b)] * window[low : low + TILE], 0.0)
        ngrad[:, lanes(b)] = total
        dots = dots + gnorm[own, lanes(b)] * total
    mean = jnp.sum(dots, axis=1, keepdims=True) / D
    key_scale, hidden_scale, score, gate, scale = [kept(stats, name, rows) for name in STATS]
    dots = jnp.zeros((TILE, CB), F32)
    for b in BLOCKS:
        total = grad[rows, lanes(b)].astype(F32) + scale * (ngrad[:, lanes(b)] - gnorm[own, lanes(b)] * mean)
        value_grad[rows, lanes(b)] = (total * gate).astype(BF16)
        dots = dots + total * values[b, rows, :]
    score_grad = gate * (1.0 - gate) * jnp.sum(dots, axis=1, keepdims=True)
    front = key_scale * score_grad / D**0.5
    by_hidden, by_key = front * hidden_scale, front * (key_scale * score / D)
    for b in BLOCKS:
        target = by_hidden * hidden[rows, lanes(b)].astype(F32) - by_key * keys[b, rows, :]
        key_grad[rows, lanes(b)] = target.astype(BF16)


def adamw(current, moment, second, gradient):
    moment_new = BETA_ONE * moment + (1.0 - BETA_ONE) * gradient
    second_new = BETA_TWO * second + (1.0 - BETA_TWO) * gradient * gradient
    first_hat = moment_new / (1.0 - BETA_ONE**STEP_COUNT)
    second_hat = second_new / (1.0 - BETA_TWO**STEP_COUNT)
    updated = current - LEARN_RATE * (first_hat / (jnp.sqrt(second_hat) + ADAM_EPS) + DECAY_RATE * current)
    return updated, moment_new, second_new


def kernel(
    owner_ref, local_ref, expand_ref, lengths_ref, taps_ref, table_ref, m_ref, v_ref, hidden_ref, grad_ref, wk_ref, wv_ref,
    memory_out_ref, table_out, m_out, v_out,
    weights, tab, req_out, req_in, reply, fetched, slots, arrived, partial, give, take,
    spread, spread_t, serve, serve_t, docs, memory, keys, values, hidden, grad, gated, gnorm, cgrad, ngrad, stats,
    key_grad, value_grad, out, halo_out, halo_in,
    load_sem, in_sem, req_send, req_recv, rep_send, rep_recv, tz_send, tz_recv, wz_send, wz_recv,
    xy_send, xy_recv, core_send, core_recv, halo_send, halo_recv, slot_send, slot_recv, ring_send, ring_recv,
):
    here = Here()
    greeted = greet(here)
    loads = []
    for b in range(NB):
        src = wk_ref if b < NB // 2 else wv_ref
        loads.append(pltpu.make_async_copy(src.at[:, pl.ds(lanes(b).start, CB)], weights.at[b, here.z, here.core], load_sem.at[b]))
    inputs = [pltpu.make_async_copy(hidden_ref, hidden, in_sem.at[0]), pltpu.make_async_copy(grad_ref, grad, in_sem.at[1])]
    for load in loads + inputs:
        load.start()
    for c in range(NC):
        tab[c, here.z, 0:R_DEV, :] = table_ref[:, c * CW : (c + 1) * CW].astype(BF16)
        tab[c, here.z, R_DEV:TROWS, :] = jnp.zeros((TROWS - R_DEV, CW), BF16)
    plan_slots(owner_ref, local_ref, expand_ref, spread, spread_t, req_out)
    greeted()

    tables = [Ring(here, lambda zz, c=c: tab.at[c, zz], tz_send.at[c], tz_recv.at[c], c % 2) for c in range(NC)]
    blocks = [here.x, NB // 2 + here.y, NB // 2 - 1, NB - 1]
    pieces = [
        Ring(here, lambda zz, b=b: weights.at[b, zz, here.core], wz_send.at[i], wz_recv.at[i], i % 2)
        for i, b in enumerate(blocks)
    ]
    crosses = [
        Cross(here, "x", weights, 0, xy_send.at[0], xy_recv.at[0]),
        Cross(here, "y", weights, NB // 2, xy_send.at[1], xy_recv.at[1]),
    ]
    zeds = [here.zed(step) for step in (0, -1, 1, -2, 2, -3, 3, 4)]
    for ring in tables:
        ring.start(1)
    send_mates(here, req_out, req_in, req_send, req_recv)
    req_in[here.plane] = req_out[here.plane]
    for load in loads:
        load.wait()
    plan_docs(here, lengths_ref, docs)
    for step in (2, 3, 4):
        for ring in tables:
            ring.arrived(step - 1)
            ring.start(step)
        if step == 2:
            mates_arrived(here, req_in, req_recv)
            plan_serve(req_in, serve, serve_t)
        if step == 3:
            for ring in pieces[:2]:
                ring.start(1)
    for c in range(NC):
        tables[c].arrived(4)
        rows = nn(serve[...], tab[c].reshape(Z * TROWS, CW))
        reply[c] = rows.astype(BF16).reshape(PLANE, MSG, CW)
        fetched[c, here.plane] = reply[c, here.plane]
        send_mates(here, reply.at[c], fetched.at[c], rep_send.at[c], rep_recv.at[c])

    def to_partner(b):
        ref = weights.at[b, :, here.core]
        return remote(ref, ref, core_send.at[b], core_recv.at[b], here.partner())

    def from_partner(b):
        ref = weights.at[b, :, 1 - here.core]
        remote(ref, ref, core_send.at[b], core_recv.at[b], here.partner()).wait_recv()

    seen = relayed = 1
    for step in (1, 2, 3, 4):
        for ring in pieces[:2]:
            ring.arrived(step)
            if step < 4:
                ring.start(step + 1)
        if step == 4:
            for ring in pieces[2:]:
                ring.start(1)
        upto = min(Z, seen + 2)
        for i in range(seen, upto):
            for cross in crosses:
                cross.start(zeds[i], i)
        for i in range(relayed, seen):
            for cross in crosses:
                cross.relay(zeds[i], i)
        relayed, seen = seen, upto
    for b in (here.x, NB // 2 + here.y):
        to_partner(b).start()

    def project(b):
        from_partner(b)
        return nn(memory[...], weights[b].reshape(E, CB))

    def project_key(b):
        keys[b] = project(b)

    def project_value(b):
        values[b] = project(NB // 2 + b)

    for i in range(relayed, Z):
        for cross in crosses:
            cross.relay(zeds[i], i)
    for step in (-1, 1):
        to_partner(here.exx(step)).start()
        to_partner(NB // 2 + here.wye(step)).start()
    for ring in pieces[2:]:
        ring.arrived(1)
        ring.start(2)
    for c in range(NC):
        mates_arrived(here, fetched.at[c], rep_recv.at[c])
        memory[:, c * CW : (c + 1) * CW] = nn(spread[...], fetched[c].reshape(PLACES, CW)).astype(BF16)
    project_key(here.x)
    project_value(here.y)
    for ring in pieces[2:]:
        ring.arrived(2)
        ring.start(3)
    for step in (-1, 1):
        project_key(here.exx(step))
        project_value(here.wye(step))
    for i in range(1, Z):
        for cross in crosses:
            cross.finish(zeds[i], i)
    to_partner(here.exx(2)).start()
    to_partner(NB // 2 + here.wye(2)).start()
    for ring in pieces[2:]:
        ring.arrived(3)
        ring.start(4)
    project_key(here.exx(2))
    project_value(here.wye(2))
    for ring in pieces[2:]:
        ring.arrived(4)
    to_partner(NB // 2 - 1).start()
    to_partner(NB - 1).start()
    for load in inputs:
        load.wait()
    project_key(NB // 2 - 1)
    project_value(NB // 2 - 1)

    def halo(way):
        sign = 1 if way == 0 else -1
        device = (here.row, lax.rem(here.col + sign + X * Y, X * Y))
        return remote(halo_out.at[way], halo_in.at[way], halo_send.at[way], halo_recv.at[way], device)

    last = TOK // TILE - 1

    def gate_step(t, carry):
        gate_tile(t, keys, values, hidden, gated, gnorm, stats)
        return carry

    gate_tile(last, keys, values, hidden, gated, gnorm, stats)
    halo_out[0] = gated[TOK - TILE : TOK, :]
    halo(0).start()
    lax.fori_loop(0, last, gate_step, 0)
    halo(0).wait_recv()
    total = jnp.zeros((TILE, CB), F32)
    for b in BLOCKS:
        rows = halo_in[0, :, lanes(b)].astype(F32)
        total = total + rows * rows
    scale = mean_scale(jnp.sum(total, axis=1, keepdims=True))
    for b in BLOCKS:
        gnorm[0:PAD, lanes(b)] = halo_in[0, :, lanes(b)].astype(F32) * scale

    def conv_step(t, carry):
        conv_tile(t, docs, taps_ref, gnorm, gated, grad, cgrad, out)
        return carry

    conv_tile(0, docs, taps_ref, gnorm, gated, grad, cgrad, out)
    halo_out[1] = cgrad[0:TILE, :].astype(BF16)
    halo(1).start()
    lax.fori_loop(1, last + 1, conv_step, 0)
    out_copy = pltpu.make_async_copy(out, memory_out_ref, in_sem.at[2])
    out_copy.start()

    def grad_step(t, carry):
        grad_tile(t, docs, taps_ref, gnorm, cgrad, grad, keys, values, hidden, stats, ngrad, key_grad, value_grad)
        return carry

    lax.fori_loop(0, last, grad_step, 0)
    halo(1).wait_recv()
    cgrad[TOK : TOK + PAD, :] = halo_in[1].astype(F32)
    grad_step(last, 0)

    for c in range(NC):
        first, stop = c * CW // (2 * WROWS), -(-(c + 1) * CW // (2 * WROWS))
        skip = c * CW - first * 2 * WROWS
        total = jnp.zeros((TOK, CW), F32)
        for b in range(NB):
            part = weights[b, first:stop].reshape((stop - first) * 2 * WROWS, CB)[skip : skip + CW]
            source = key_grad if b < NB // 2 else value_grad
            total = total + nt(source[:, lanes(b)], part)
        slots[c] = nn(spread_t[...], total.astype(BF16)).astype(BF16).reshape(PLANE, MSG, CW)
        arrived[c, here.plane] = slots[c, here.plane]
        send_mates(here, slots.at[c], arrived.at[c], slot_send.at[c], slot_recv.at[c])

    def hop(c, way, step):
        sign = 1 if way == 0 else -1
        return remote(
            give.at[c, way, step - 1], take.at[c, way, step - 1],
            ring_send.at[c, way, step - 1], ring_recv.at[c, way, step - 1], here.at_z(sign),
        )

    def length(c, way):
        return Z // 2 if way == c % 2 else Z // 2 - 1

    def advance(c, step):
        for way in range(2):
            final = length(c, way)
            if step > final:
                continue
            sign = 1 if way == 0 else -1
            mine = partial[c, here.zed(sign * (final - step + 1))]
            if step > 1:
                hop(c, way, step - 1).wait_recv()
                mine = mine + take[c, way, step - 2].astype(F32)
            give[c, way, step - 1] = mine.astype(BF16)
            hop(c, way, step).start()

    def finish(c):
        total = partial[c, here.z]
        for way in range(2):
            final = length(c, way)
            hop(c, way, final).wait_recv()
            total = total + take[c, way, final - 1].astype(F32)
        cols = slice(c * CW, (c + 1) * CW)
        new_t, new_m, new_v = adamw(table_ref[:, cols], m_ref[:, cols], v_ref[:, cols], total[:R_DEV])
        table_out[:, cols] = new_t
        m_out[:, cols] = new_m
        v_out[:, cols] = new_v

    for c in range(NC):
        mates_arrived(here, arrived.at[c], slot_recv.at[c])
        partial[c] = nn(serve_t[...], arrived[c].reshape(PLACES, CW)).reshape(Z, TROWS, CW)
        advance(c, 1)
        for back in range(1, min(c, 3) + 1):
            advance(c - back, back + 1)
    for step in range(2, 5):
        for c in range(NC):
            if c + step > NC:
                advance(c, step)
    for c in range(NC):
        finish(c)

    out_copy.wait()
    for b in range(NB):
        to_partner(b).wait_send()
    for ring in tables + pieces:
        ring.drain()
    for i in range(1, Z):
        for cross in crosses:
            cross.drain(zeds[i], i)
    for way in range(2):
        halo(way).wait_send()
    mates_sent(here, req_out, req_send)
    for c in range(NC):
        mates_sent(here, reply.at[c], rep_send.at[c])
        mates_sent(here, slots.at[c], slot_send.at[c])
        for way in range(2):
            for step in range(1, length(c, way) + 1):
                hop(c, way, step).wait_send()


def on_device(
    hidden, grad_out, w_key, w_value, depthwise_weight, table, adam_m, adam_v,
    row_owner, row_local, expand_index, doc_lengths,
):
    vmem = pl.BlockSpec(memory_space=pltpu.VMEM)
    any_ = pl.BlockSpec(memory_space=pl.ANY)
    dma = pltpu.SemaphoreType.DMA
    rows = (NC, PLANE, MSG, CW)
    hops = (NC, 2, Z // 2)
    row_out = jax.ShapeDtypeStruct((R_DEV, E), F32)
    memory_out, new_table, new_moment, new_second = pl.pallas_call(
        kernel,
        out_shape=(jax.ShapeDtypeStruct((TOK, D), BF16), row_out, row_out, row_out),
        in_specs=[vmem] * 8 + [any_] * 4,
        out_specs=(any_, vmem, vmem, vmem),
        scratch_shapes=[
            pltpu.VMEM((NB, Z, 2, WROWS, CB), BF16),
            pltpu.VMEM((NC, Z, TROWS, CW), BF16),
            pltpu.VMEM((PLANE, 1, 128), F32),
            pltpu.VMEM((PLANE, 1, 128), F32),
            pltpu.VMEM(rows, BF16),
            pltpu.VMEM(rows, BF16),
            pltpu.VMEM(rows, BF16),
            pltpu.VMEM(rows, BF16),
            pltpu.VMEM((NC, Z, TROWS, CW), F32),
            pltpu.VMEM(hops + (TROWS, CW), BF16),
            pltpu.VMEM(hops + (TROWS, CW), BF16),
            pltpu.VMEM((TOK, PLACES), BF16),
            pltpu.VMEM((PLACES, TOK), BF16),
            pltpu.VMEM((PLACES, Z * TROWS), BF16),
            pltpu.VMEM((Z * TROWS, PLACES), BF16),
            pltpu.VMEM((TOK + 2 * PAD, 128), F32),
            pltpu.VMEM((TOK, E), BF16),
            pltpu.VMEM((NB // 2, TOK, CB), F32),
            pltpu.VMEM((NB // 2, TOK, CB), F32),
            pltpu.VMEM((TOK, D), BF16),
            pltpu.VMEM((TOK, D), BF16),
            pltpu.VMEM((TOK, D), BF16),
            pltpu.VMEM((PAD + TOK, D), F32),
            pltpu.VMEM((TOK + PAD, D), F32),
            pltpu.VMEM((TILE, D), F32),
            pltpu.VMEM((len(STATS), TOK, 128), F32),
            pltpu.VMEM((TOK, D), BF16),
            pltpu.VMEM((TOK, D), BF16),
            pltpu.VMEM((TOK, D), BF16),
            pltpu.VMEM((2, TILE, D), BF16),
            pltpu.VMEM((2, TILE, D), BF16),
            dma((NB,)), dma((3,)), dma, dma, dma((NC,)), dma((NC,)),
            dma(hops), dma(hops), dma((4, 2, Z // 2)), dma((4, 2, Z // 2)),
            dma((2, 4, Z)), dma((2, 4, Z)), dma((NB,)), dma((NB,)),
            dma((2,)), dma((2,)), dma((NC,)), dma((NC,)), dma(hops), dma(hops),
        ],
        compiler_params=pltpu.CompilerParams(
            collective_id=0, has_side_effects=True, vmem_limit_bytes=56 * 1024 * 1024
        ),
        name="memory_branch",
    )(
        row_owner.reshape(1, U), row_local, expand_index[0].T, doc_lengths, depthwise_weight,
        table, adam_m, adam_v, hidden[0], grad_out[0], w_key, w_value,
    )
    return (memory_out[None], new_table, new_moment, new_second)


def solution(mesh):
    placed = (
        P("row", "col", None),
        P("row", "col", None),
        P("row", None),
        P("row", None),
        P(),
        P(("row", "col"), None),
        P(("row", "col"), None),
        P(("row", "col"), None),
        P("row", "col", None),
        P("row", "col"),
        P("row", "col", None),
        P("row", None),
    )
    return jax.shard_map(
        on_device,
        mesh=mesh,
        in_specs=placed,
        out_specs=(
            P("row", "col", None),
            P(("row", "col"), None),
            P(("row", "col"), None),
            P(("row", "col"), None),
        ),
        check_vma=False,
    )
```

```python
import jax
import jax.numpy as jnp
from jax import lax
from jax.experimental import pallas as pl
from jax.experimental.pallas import tpu as pltpu
from jax.sharding import PartitionSpec as P

DILATION_STEP = 3
NORM_EPS = 1e-06
BETA_ONE = 0.9
BETA_TWO = 0.95
ADAM_EPS = 1e-08
LEARN_RATE = 0.01
DECAY_RATE = 0.1
STEP_COUNT = 10.0

Z, X, Y = 8, 4, 4
PLANE = 2 * X * Y
D, E = 2560, 1280
TOK, U, R_DEV = 128, 144, 40
CW = 256
NC = E // CW
RINGS = 3
TROWS = 48
MSG = 2 * Z
PLACES = PLANE * MSG
CB = 512
NB = 2 * D // CB
WROWS = 80
TILE = 16
PAD = 16
TAPS = 4

MESH = pl.DeviceIdType.MESH
F32, BF16, I32 = jnp.float32, jnp.bfloat16, jnp.int32


class Here:
    def __init__(self):
        self.row = lax.axis_index("row")
        self.col = lax.axis_index("col")
        self.z = self.row // 2
        self.core = self.row % 2
        self.x = self.col // Y
        self.y = self.col % Y
        self.plane = self.core * (X * Y) + self.col

    def mate(self, i):
        q = lax.rem(self.plane + i, PLANE)
        return q, (self.z * 2 + q // (X * Y), q % (X * Y))

    def zed(self, step):
        return lax.rem(self.z + step + Z, Z)

    def at_z(self, step):
        return (self.zed(step) * 2 + self.core, self.col)

    def exx(self, step):
        return lax.rem(self.x + step + X, X)

    def wye(self, step):
        return lax.rem(self.y + step + Y, Y)

    def at_x(self, step):
        return (self.row, self.exx(step) * Y + self.y)

    def at_y(self, step):
        return (self.row, self.x * Y + self.wye(step))

    def partner(self):
        return (self.z * 2 + 1 - self.core, self.col)


def remote(src, dst, send, recv, device):
    return pltpu.make_async_remote_copy(
        src_ref=src, dst_ref=dst, send_sem=send, recv_sem=recv, device_id=device, device_id_type=MESH
    )


def greet(here):
    barrier = pltpu.get_barrier_semaphore()

    def one(i, carry):
        _, device = here.mate(i)
        pl.semaphore_signal(barrier, inc=1, device_id=device, device_id_type=MESH)
        return carry

    lax.fori_loop(1, PLANE, one, 0)
    for step in range(1, Z):
        pl.semaphore_signal(barrier, inc=1, device_id=here.at_z(step), device_id_type=MESH)
    return lambda: pl.semaphore_wait(barrier, PLANE - 1 + Z - 1)


def iota(shape, dim):
    return lax.broadcasted_iota(I32, shape, dim)


def one_hot(mask):
    return jnp.where(mask, 1.0, 0.0).astype(BF16)


def nn(left, right):
    return jnp.dot(left, right, preferred_element_type=F32)


def tn(left, right):
    return lax.dot_general(left, right, (((0,), (0,)), ((), ())), preferred_element_type=F32)


def nt(left, right):
    return lax.dot_general(left, right, (((1,), (1,)), ((), ())), preferred_element_type=F32)


def column_of(row, size):
    eye = iota((size, size), 0) == iota((size, size), 1)
    return jnp.sum(jnp.where(eye, row, 0), axis=1, keepdims=True)


def plan_slots(owner_ref, local_ref, expand_ref, spread, spread_t, req_out):
    owner_r = owner_ref[...]
    owner_c = column_of(owner_r, U)
    local_c = column_of(local_ref[...], U)
    same = owner_c == owner_r
    earlier_c = same & (iota((U, U), 1) < iota((U, U), 0))
    earlier_r = same & (iota((U, U), 0) < iota((U, U), 1))
    k_c = (owner_c >> 5) * 2 + jnp.sum(jnp.where(earlier_c, 1, 0), axis=1, keepdims=True)
    k_r = (owner_r >> 5) * 2 + jnp.sum(jnp.where(earlier_r, 1, 0), axis=0, keepdims=True)
    mates = one_hot((owner_r & 31) == iota((PLANE, U), 0))
    wanted = jnp.where(k_c == iota((U, 128), 1), local_c + 1, 0).astype(F32).astype(BF16)
    request = nn(mates, wanted)
    for q in range(PLANE):
        req_out[q] = request[q : q + 1, :]
    expand = expand_ref[...]
    reads = jnp.zeros((U, TOK), F32)
    for lookup in range(2):
        reads = reads + jnp.where(expand[lookup : lookup + 1, :] == iota((U, TOK), 0), 1.0, 0.0)
    reads = reads.astype(BF16)
    places = one_hot((owner_c & 31) * MSG + k_c == iota((U, PLACES), 1))
    places_t = one_hot((owner_r & 31) * MSG + k_r == iota((PLACES, U), 0))
    spread[...] = tn(reads, places).astype(BF16)
    spread_t[...] = nn(places_t, reads).astype(BF16)


def plan_serve(req_in, serve, serve_t):
    asked = req_in[:, 0, :].astype(BF16)
    wide = nn(one_hot(iota((PLACES, PLANE), 0) // MSG == iota((PLACES, PLANE), 1)), asked)
    k = iota((PLACES, 128), 0) % MSG
    value = jnp.sum(jnp.where(k == iota((PLACES, 128), 1), wide, 0.0), axis=1, keepdims=True)
    zed = (iota((PLACES, 1), 0) % MSG) // 2
    target = jnp.where(value > 0.5, zed * TROWS + value.astype(I32) - 1, -1)
    serve[...] = one_hot(target == iota((PLACES, Z * TROWS), 1))
    tall = tn(asked, one_hot(iota((PLANE, PLACES), 1) // MSG == iota((PLANE, PLACES), 0)))
    k = iota((128, PLACES), 1) % MSG
    value = jnp.sum(jnp.where(k == iota((128, PLACES), 0), tall, 0.0), axis=0, keepdims=True)
    zed = (iota((1, PLACES), 1) % MSG) // 2
    target = jnp.where(value > 0.5, zed * TROWS + value.astype(I32) - 1, -1)
    serve_t[...] = one_hot(target == iota((Z * TROWS, PLACES), 0))


def plan_docs(here, lengths_ref, docs):
    n = lengths_ref.shape[1]
    length_c = column_of(lengths_ref[...], n)
    ends = jnp.sum(jnp.where(iota((n, n), 0) <= iota((n, n), 1), length_c, 0), axis=0, keepdims=True)
    rows = docs.shape[0]
    position = here.col * TOK - PAD + iota((rows, 1), 0)
    passed = (position >= ends) & (iota((rows, n), 1) < n - 1)
    doc = jnp.sum(jnp.where(passed, 1.0, 0.0), axis=1, keepdims=True)
    doc = jnp.where(position < 0, -1.0, jnp.where(position >= 16 * TOK, -2.0, doc))
    docs[...] = jnp.broadcast_to(doc, (rows, 128))


def send_mates(here, src, dst, send, recv):
    def one(i, carry):
        q, device = here.mate(i)
        remote(src.at[q], dst.at[here.plane], send, recv, device).start()
        return carry

    lax.fori_loop(1, PLANE, one, 0)


def mates_arrived(here, dst, recv):
    ref = dst.at[pl.ds(0, PLANE - 1)]
    pltpu.make_async_copy(ref, ref, recv).wait()


def mates_sent(here, src, send):
    ref = src.at[pl.ds(0, PLANE - 1)]
    pltpu.make_async_copy(ref, ref, send).wait()


class Ring:
    def __init__(self, here, block, send, recv, far):
        self.here, self.block, self.send, self.recv, self.far = here, block, send, recv, far

    def copy(self, way, step):
        sign = 1 if way == 0 else -1
        ref = self.block(self.here.zed(-sign * (step - 1)))
        return remote(ref, ref, self.send.at[way, step - 1], self.recv.at[way, step - 1], self.here.at_z(sign))

    def steps(self, way):
        return Z // 2 if way == self.far else Z // 2 - 1

    def start(self, step):
        for way in range(2):
            if step <= self.steps(way):
                self.copy(way, step).start()

    def arrived(self, step):
        got = []
        for way in range(2):
            if step <= self.steps(way):
                sign = 1 if way == 0 else -1
                ref = self.block(self.here.zed(-sign * step))
                remote(ref, ref, self.send.at[way, step - 1], self.recv.at[way, step - 1], self.here.at_z(-sign)).wait_recv()
                got.append(-sign * step)
        return got

    def drain(self):
        for way in range(2):
            for step in range(1, self.steps(way) + 1):
                self.copy(way, step).wait_send()


class Cross:
    def __init__(self, here, axis, weights, base, send, recv):
        self.here, self.weights, self.base, self.send, self.recv = here, weights, base, send, recv
        self.at = here.at_x if axis == "x" else here.at_y
        self.place = here.exx if axis == "x" else here.wye

    def copy(self, way, zz, i):
        sign = 1 if way % 2 == 0 else -1
        if way < 2:
            ref = self.weights.at[self.base + self.place(0), zz, self.here.core]
        else:
            ref = self.weights.at[self.base + self.place(-sign), zz, self.here.core, :, pl.ds((way - 2) * (CB // 2), CB // 2)]
        return remote(ref, ref, self.send.at[way, i], self.recv.at[way, i], self.at(sign))

    def got(self, way, zz, i):
        sign = 1 if way % 2 == 0 else -1
        if way < 2:
            ref = self.weights.at[self.base + self.place(-sign), zz, self.here.core]
        else:
            ref = self.weights.at[
                self.base + self.place(-2 * sign), zz, self.here.core, :, pl.ds((way - 2) * (CB // 2), CB // 2)
            ]
        return remote(ref, ref, self.send.at[way, i], self.recv.at[way, i], self.at(-sign))

    def start(self, zz, i):
        for way in (0, 1):
            self.copy(way, zz, i).start()

    def relay(self, zz, i):
        for way in (0, 1):
            self.got(way, zz, i).wait_recv()
            self.copy(way + 2, zz, i).start()

    def finish(self, zz, i):
        for way in (2, 3):
            self.got(way, zz, i).wait_recv()

    def drain(self, zz, i):
        for way in range(4):
            self.copy(way, zz, i).wait_send()


def lanes(b):
    return slice((b % (NB // 2)) * CB, (b % (NB // 2) + 1) * CB)


def row_tile(t):
    return pl.ds(pl.multiple_of(t * TILE, TILE), TILE)


def mean_scale(total):
    return lax.rsqrt(total / D + NORM_EPS)


BLOCKS = range(NB // 2)
STATS = ("key_scale", "hidden_scale", "score", "gate", "gated_scale")


def keep(stats, name, rows, value):
    stats[STATS.index(name), rows, :] = jnp.broadcast_to(value, (TILE, 128))


def kept(stats, name, rows):
    return wide(stats[STATS.index(name), rows, :])


def wide(value):
    return jnp.concatenate([value] * (CB // 128), axis=1)


def gate_tile(t, keys, values, hidden, gated, gnorm, stats):
    rows = row_tile(t)
    kk = jnp.zeros((TILE, CB), F32)
    hh, hk = kk, kk
    for b in BLOCKS:
        key = keys[b, rows, :]
        hid = hidden[rows, lanes(b)].astype(F32)
        kk, hh, hk = kk + key * key, hh + hid * hid, hk + hid * key
    key_scale = mean_scale(jnp.sum(kk, axis=1, keepdims=True))
    hidden_scale = mean_scale(jnp.sum(hh, axis=1, keepdims=True))
    score = jnp.sum(hk, axis=1, keepdims=True) * key_scale * hidden_scale
    gate = jax.nn.sigmoid(score / D**0.5)
    gg = jnp.zeros((TILE, CB), F32)
    for b in BLOCKS:
        rounded = (gate * values[b, rows, :]).astype(BF16)
        gated[rows, lanes(b)] = rounded
        gg = gg + rounded.astype(F32) * rounded.astype(F32)
    scale = mean_scale(jnp.sum(gg, axis=1, keepdims=True))
    own = pl.ds(pl.multiple_of(PAD + t * TILE, TILE), TILE)
    for b in BLOCKS:
        gnorm[own, lanes(b)] = gated[rows, lanes(b)].astype(F32) * scale
    for name, value in zip(STATS, (key_scale, hidden_scale, score, gate, scale)):
        keep(stats, name, rows, value)


def same_docs(docs, t, sign):
    window = docs[pl.ds(pl.multiple_of(t * TILE, TILE), 3 * TILE), :]
    center = window[TILE : 2 * TILE]
    shifted = [window[TILE + sign * DILATION_STEP * j : 2 * TILE + sign * DILATION_STEP * j] for j in range(TAPS)]
    return [wide(jnp.where(center == other, 1.0, 0.0)) for other in shifted]


def conv_tile(t, docs, taps, gnorm, gated, grad, cgrad, out):
    rows = row_tile(t)
    masks = same_docs(docs, t, -1)
    both = pl.ds(pl.multiple_of(t * TILE, TILE), 2 * TILE)
    for b in BLOCKS:
        window = gnorm[both, lanes(b)]
        conv = taps[0:1, lanes(b)] * window[TILE:]
        for j in range(1, TAPS):
            low = TILE - DILATION_STEP * j
            conv = conv + masks[j] * (taps[j : j + 1, lanes(b)] * window[low : low + TILE])
        sig = jax.nn.sigmoid(conv)
        out[rows, lanes(b)] = (conv * sig + gated[rows, lanes(b)].astype(F32)).astype(BF16)
        cgrad[rows, lanes(b)] = grad[rows, lanes(b)].astype(F32) * sig * (1.0 + conv * (1.0 - sig))


def grad_tile(t, docs, taps, gnorm, cgrad, grad, keys, values, hidden, stats, ngrad, key_grad, value_grad):
    rows = row_tile(t)
    masks = same_docs(docs, t, 1)
    both = pl.ds(pl.multiple_of(t * TILE, TILE), 2 * TILE)
    own = pl.ds(pl.multiple_of(PAD + t * TILE, TILE), TILE)
    dots = jnp.zeros((TILE, CB), F32)
    for b in BLOCKS:
        window = cgrad[both, lanes(b)]
        total = taps[0:1, lanes(b)] * window[:TILE]
        for j in range(1, TAPS):
            low = DILATION_STEP * j
            total = total + masks[j] * (taps[j : j + 1, lanes(b)] * window[low : low + TILE])
        ngrad[:, lanes(b)] = total
        dots = dots + gnorm[own, lanes(b)] * total
    mean = jnp.sum(dots, axis=1, keepdims=True) / D
    key_scale, hidden_scale, score, gate, scale = [kept(stats, name, rows) for name in STATS]
    dots = jnp.zeros((TILE, CB), F32)
    for b in BLOCKS:
        total = grad[rows, lanes(b)].astype(F32) + scale * (ngrad[:, lanes(b)] - gnorm[own, lanes(b)] * mean)
        value_grad[rows, lanes(b)] = (total * gate).astype(BF16)
        dots = dots + total * values[b, rows, :]
    score_grad = gate * (1.0 - gate) * jnp.sum(dots, axis=1, keepdims=True)
    front = key_scale * score_grad / D**0.5
    by_hidden, by_key = front * hidden_scale, front * (key_scale * score / D)
    for b in BLOCKS:
        target = by_hidden * hidden[rows, lanes(b)].astype(F32) - by_key * keys[b, rows, :]
        key_grad[rows, lanes(b)] = target.astype(BF16)


def adamw(current, moment, second, gradient):
    moment_new = BETA_ONE * moment + (1.0 - BETA_ONE) * gradient
    second_new = BETA_TWO * second + (1.0 - BETA_TWO) * gradient * gradient
    first_hat = moment_new / (1.0 - BETA_ONE**STEP_COUNT)
    second_hat = second_new / (1.0 - BETA_TWO**STEP_COUNT)
    updated = current - LEARN_RATE * (first_hat / (jnp.sqrt(second_hat) + ADAM_EPS) + DECAY_RATE * current)
    return updated, moment_new, second_new


def kernel(
    owner_ref, local_ref, expand_ref, lengths_ref, taps_ref, table_ref, hidden_ref, grad_ref, wk_ref, wv_ref,
    out, row_grad,
    weights, tab, req_out, req_in, reply, fetched, slots, arrived, partial, give, take,
    spread, spread_t, serve, serve_t, docs, memory, keys, values, hidden, grad, gated, gnorm, cgrad, ngrad, stats,
    key_grad, value_grad, grads_t, halo_out, halo_in, give_far, take_far,
    load_sem, in_sem, req_send, req_recv, rep_send, rep_recv, tz_send, tz_recv, wz_send, wz_recv,
    xy_send, xy_recv, core_send, core_recv, halo_send, halo_recv, slot_send, slot_recv, ring_send, ring_recv,
    far_send, far_recv,
):
    here = Here()
    greeted = greet(here)
    loads = []
    for b in range(NB):
        src = wk_ref if b < NB // 2 else wv_ref
        loads.append(pltpu.make_async_copy(src.at[:, pl.ds(lanes(b).start, CB)], weights.at[b, here.z, here.core], load_sem.at[b]))
    inputs = [pltpu.make_async_copy(hidden_ref, hidden, in_sem.at[0]), pltpu.make_async_copy(grad_ref, grad, in_sem.at[1])]
    for load in loads + inputs:
        load.start()
    for c in range(NC):
        tab[c, here.z, 0:R_DEV, :] = table_ref[:, c * CW : (c + 1) * CW].astype(BF16)
        tab[c, here.z, R_DEV:TROWS, :] = jnp.zeros((TROWS - R_DEV, CW), BF16)
    plan_slots(owner_ref, local_ref, expand_ref, spread, spread_t, req_out)
    greeted()

    tables = [Ring(here, lambda zz, c=c: tab.at[c, zz], tz_send.at[c], tz_recv.at[c], c % 2) for c in range(NC)]
    blocks = [here.x, NB // 2 + here.y, NB // 2 - 1, NB - 1]
    pieces = [
        Ring(here, lambda zz, b=b: weights.at[b, zz, here.core], wz_send.at[i], wz_recv.at[i], i % 2)
        for i, b in enumerate(blocks)
    ]
    crosses = [
        Cross(here, "x", weights, 0, xy_send.at[0], xy_recv.at[0]),
        Cross(here, "y", weights, NB // 2, xy_send.at[1], xy_recv.at[1]),
    ]
    zeds = [here.zed(step) for step in (0, -1, 1, -2, 2, -3, 3, 4)]
    for load in loads:
        load.wait()
    for ring in tables:
        ring.start(1)
    for ring in pieces[:2]:
        ring.start(1)
    send_mates(here, req_out, req_in, req_send, req_recv)
    req_in[here.plane] = req_out[here.plane]
    plan_docs(here, lengths_ref, docs)
    for step in (1, 2, 3):
        for ring in tables:
            ring.arrived(step)
            ring.start(step + 1)
        for ring in pieces[:2]:
            ring.arrived(step)
            ring.start(step + 1)
        for cross in crosses:
            for i in (2 * step - 1, 2 * step):
                cross.start(zeds[i], i)
        if step == 1:
            mates_arrived(here, req_in, req_recv)
            plan_serve(req_in, serve, serve_t)
        if step > 1:
            for cross in crosses:
                for i in (2 * step - 3, 2 * step - 2):
                    cross.relay(zeds[i], i)
    for ring in pieces[2:]:
        ring.start(1)
    for ring in pieces[:2]:
        ring.arrived(4)
    for cross in crosses:
        cross.start(zeds[Z - 1], Z - 1)
    for c in range(NC):
        tables[c].arrived(4)
        rows = nn(serve[...], tab[c].reshape(Z * TROWS, CW))
        reply[c] = rows.astype(BF16).reshape(PLANE, MSG, CW)
        fetched[c, here.plane] = reply[c, here.plane]
        send_mates(here, reply.at[c], fetched.at[c], rep_send.at[c], rep_recv.at[c])

    def to_partner(b):
        ref = weights.at[b, :, here.core]
        return remote(ref, ref, core_send.at[b], core_recv.at[b], here.partner())

    def from_partner(b):
        ref = weights.at[b, :, 1 - here.core]
        remote(ref, ref, core_send.at[b], core_recv.at[b], here.partner()).wait_recv()

    def project(b):
        from_partner(b)
        return nn(memory[...], weights[b].reshape(E, CB))

    def project_key(b):
        keys[b] = project(b)

    def project_value(b):
        values[b] = project(NB // 2 + b)

    for b in (here.x, NB // 2 + here.y):
        to_partner(b).start()
    for ring in pieces[2:]:
        ring.arrived(1)
        ring.start(2)
    for cross in crosses:
        for i in (Z - 3, Z - 2):
            cross.relay(zeds[i], i)
    for step in (2, 3):
        for ring in pieces[2:]:
            ring.arrived(step)
            ring.start(step + 1)
    for load in inputs:
        load.wait()
    for cross in crosses:
        cross.relay(zeds[Z - 1], Z - 1)
    for step in (-1, 1):
        to_partner(here.exx(step)).start()
        to_partner(NB // 2 + here.wye(step)).start()
    for c in range(NC):
        mates_arrived(here, fetched.at[c], rep_recv.at[c])
        memory[:, c * CW : (c + 1) * CW] = nn(spread[...], fetched[c].reshape(PLACES, CW)).astype(BF16)
    project_key(here.x)
    project_value(here.y)
    for i in range(1, Z):
        for cross in crosses:
            cross.finish(zeds[i], i)
    to_partner(here.exx(2)).start()
    to_partner(NB // 2 + here.wye(2)).start()
    for ring in pieces[2:]:
        ring.arrived(4)
    to_partner(NB // 2 - 1).start()
    to_partner(NB - 1).start()
    for step in (-1, 1, 2):
        project_key(here.exx(step))
        project_value(here.wye(step))
    project_key(NB // 2 - 1)
    project_value(NB // 2 - 1)

    def halo(way):
        sign = 1 if way == 0 else -1
        device = (here.row, lax.rem(here.col + sign + X * Y, X * Y))
        return remote(halo_out.at[way], halo_in.at[way], halo_send.at[way], halo_recv.at[way], device)

    last = TOK // TILE - 1

    def gate_step(t, carry):
        gate_tile(t, keys, values, hidden, gated, gnorm, stats)
        return carry

    gate_tile(last, keys, values, hidden, gated, gnorm, stats)
    halo_out[0] = gated[TOK - TILE : TOK, :]
    halo(0).start()
    lax.fori_loop(0, last, gate_step, 0)
    halo(0).wait_recv()
    total = jnp.zeros((TILE, CB), F32)
    for b in BLOCKS:
        rows = halo_in[0, :, lanes(b)].astype(F32)
        total = total + rows * rows
    scale = mean_scale(jnp.sum(total, axis=1, keepdims=True))
    for b in BLOCKS:
        gnorm[0:PAD, lanes(b)] = halo_in[0, :, lanes(b)].astype(F32) * scale

    def conv_step(t, carry):
        conv_tile(t, docs, taps_ref, gnorm, gated, grad, cgrad, out)
        return carry

    conv_tile(0, docs, taps_ref, gnorm, gated, grad, cgrad, out)
    halo_out[1] = cgrad[0:TILE, :].astype(BF16)
    halo(1).start()
    lax.fori_loop(1, last + 1, conv_step, 0)

    def grad_step(t, carry):
        grad_tile(t, docs, taps_ref, gnorm, cgrad, grad, keys, values, hidden, stats, ngrad, key_grad, value_grad)
        return carry

    lax.fori_loop(0, last, grad_step, 0)
    halo(1).wait_recv()
    cgrad[TOK : TOK + PAD, :] = halo_in[1].astype(F32)
    grad_step(last, 0)

    for b in range(NB):
        source = key_grad if b < NB // 2 else value_grad
        grads_t[b] = source[:, lanes(b)].T
    for c in range(NC):
        first, stop = c * CW // (2 * WROWS), -(-(c + 1) * CW // (2 * WROWS))
        skip = c * CW - first * 2 * WROWS
        total = jnp.zeros((CW, TOK), F32)
        for b in range(NB):
            part = weights[b, first:stop].reshape((stop - first) * 2 * WROWS, CB)[skip : skip + CW]
            total = total + nn(part, grads_t[b])
        slots[c] = nt(spread_t[...], total.astype(BF16)).astype(BF16).reshape(PLANE, MSG, CW)
        arrived[c, here.plane] = slots[c, here.plane]
        send_mates(here, slots.at[c], arrived.at[c], slot_send.at[c], slot_recv.at[c])

    def hop(c, way, step):
        sign = 1 if way == 0 else -1
        return remote(
            give.at[c, way, step - 1], take.at[c, way, step - 1],
            ring_send.at[c, way, step - 1], ring_recv.at[c, way, step - 1], here.at_z(sign),
        )

    def length(c, way):
        return Z // 2 if way == c % 2 else Z // 2 - 1

    def advance(c, step):
        for way in range(2):
            final = length(c, way)
            if step > final:
                continue
            sign = 1 if way == 0 else -1
            mine = partial[c, here.zed(sign * (final - step + 1))]
            if step > 1:
                hop(c, way, step - 1).wait_recv()
                mine = mine + take[c, way, step - 2].astype(F32)
            give[c, way, step - 1] = mine.astype(BF16)
            hop(c, way, step).start()

    def far(c, step):
        place = c - RINGS
        return remote(
            give_far.at[place, here.zed(step)], take_far.at[place, step],
            far_send.at[place, step], far_recv.at[place, step], here.at_z(step),
        )

    def send_far(c):
        give_far[c - RINGS] = partial[c].astype(BF16)
        for step in range(1, Z):
            far(c, step).start()

    def finish(c):
        total = partial[c, here.z]
        if c < RINGS:
            for way in range(2):
                final = length(c, way)
                hop(c, way, final).wait_recv()
                total = total + take[c, way, final - 1].astype(F32)
        else:
            for step in range(1, Z):
                far(c, step).wait_recv()
                total = total + take_far[c - RINGS, step].astype(F32)
        row_grad[:, c * CW : (c + 1) * CW] = total[:R_DEV]

    for c in range(NC):
        mates_arrived(here, arrived.at[c], slot_recv.at[c])
        partial[c] = nn(serve_t[...], arrived[c].reshape(PLACES, CW)).reshape(Z, TROWS, CW)
        if c < RINGS:
            advance(c, 1)
        else:
            send_far(c)
        for back in range(1, 4):
            if 0 <= c - back < RINGS:
                advance(c - back, back + 1)
    for step in range(2, Z // 2 + 1):
        for c in range(RINGS):
            if c + step > NC:
                advance(c, step)
    for c in range(NC):
        finish(c)

    for b in range(NB):
        to_partner(b).wait_send()
    for ring in tables + pieces:
        ring.drain()
    for i in range(1, Z):
        for cross in crosses:
            cross.drain(zeds[i], i)
    for way in range(2):
        halo(way).wait_send()
    mates_sent(here, req_out, req_send)
    for c in range(NC):
        mates_sent(here, reply.at[c], rep_send.at[c])
        mates_sent(here, slots.at[c], slot_send.at[c])
        if c < RINGS:
            for way in range(2):
                for step in range(1, length(c, way) + 1):
                    hop(c, way, step).wait_send()
        else:
            for step in range(1, Z):
                far(c, step).wait_send()


def on_device(
    hidden, grad_out, w_key, w_value, depthwise_weight, table, adam_m, adam_v,
    row_owner, row_local, expand_index, doc_lengths,
):
    vmem = pl.BlockSpec(memory_space=pltpu.VMEM)
    any_ = pl.BlockSpec(memory_space=pl.ANY)
    dma = pltpu.SemaphoreType.DMA
    rows = (NC, PLANE, MSG, CW)
    hops = (RINGS, 2, Z // 2)
    fars = (NC - RINGS, Z)
    memory_out, row_grad = pl.pallas_call(
        kernel,
        out_shape=(jax.ShapeDtypeStruct((TOK, D), BF16), jax.ShapeDtypeStruct((R_DEV, E), F32)),
        in_specs=[vmem] * 6 + [any_] * 4,
        out_specs=(vmem, vmem),
        scratch_shapes=[
            pltpu.VMEM((NB, Z, 2, WROWS, CB), BF16),
            pltpu.VMEM((NC, Z, TROWS, CW), BF16),
            pltpu.VMEM((PLANE, 1, 128), F32),
            pltpu.VMEM((PLANE, 1, 128), F32),
            pltpu.VMEM(rows, BF16),
            pltpu.VMEM(rows, BF16),
            pltpu.VMEM(rows, BF16),
            pltpu.VMEM(rows, BF16),
            pltpu.VMEM((NC, Z, TROWS, CW), F32),
            pltpu.VMEM(hops + (TROWS, CW), BF16),
            pltpu.VMEM(hops + (TROWS, CW), BF16),
            pltpu.VMEM((TOK, PLACES), BF16),
            pltpu.VMEM((PLACES, TOK), BF16),
            pltpu.VMEM((PLACES, Z * TROWS), BF16),
            pltpu.VMEM((Z * TROWS, PLACES), BF16),
            pltpu.VMEM((TOK + 2 * PAD, 128), F32),
            pltpu.VMEM((TOK, E), BF16),
            pltpu.VMEM((NB // 2, TOK, CB), F32),
            pltpu.VMEM((NB // 2, TOK, CB), F32),
            pltpu.VMEM((TOK, D), BF16),
            pltpu.VMEM((TOK, D), BF16),
            pltpu.VMEM((TOK, D), BF16),
            pltpu.VMEM((PAD + TOK, D), F32),
            pltpu.VMEM((TOK + PAD, D), F32),
            pltpu.VMEM((TILE, D), F32),
            pltpu.VMEM((len(STATS), TOK, 128), F32),
            pltpu.VMEM((TOK, D), BF16),
            pltpu.VMEM((TOK, D), BF16),
            pltpu.VMEM((NB, CB, TOK), BF16),
            pltpu.VMEM((2, TILE, D), BF16),
            pltpu.VMEM((2, TILE, D), BF16),
            pltpu.VMEM(fars + (TROWS, CW), BF16),
            pltpu.VMEM(fars + (TROWS, CW), BF16),
            dma((NB,)), dma((2,)), dma, dma, dma((NC,)), dma((NC,)),
            dma((NC, 2, Z // 2)), dma((NC, 2, Z // 2)), dma((4, 2, Z // 2)), dma((4, 2, Z // 2)),
            dma((2, 4, Z)), dma((2, 4, Z)), dma((NB,)), dma((NB,)),
            dma((2,)), dma((2,)), dma((NC,)), dma((NC,)), dma(hops), dma(hops), dma(fars), dma(fars),
        ],
        compiler_params=pltpu.CompilerParams(
            collective_id=0, has_side_effects=True, vmem_limit_bytes=56 * 1024 * 1024
        ),
        name="memory_branch",
    )(
        row_owner.reshape(1, U), row_local, expand_index[0].T, doc_lengths, depthwise_weight,
        table, hidden[0], grad_out[0], w_key, w_value,
    )
    new_table, new_moment, new_second = adamw(table, adam_m, adam_v, row_grad)
    return (memory_out[None], new_table, new_moment, new_second)


def solution(mesh):
    placed = (
        P("row", "col", None),
        P("row", "col", None),
        P("row", None),
        P("row", None),
        P(),
        P(("row", "col"), None),
        P(("row", "col"), None),
        P(("row", "col"), None),
        P("row", "col", None),
        P("row", "col"),
        P("row", "col", None),
        P("row", None),
    )
    return jax.shard_map(
        on_device,
        mesh=mesh,
        in_specs=placed,
        out_specs=(
            P("row", "col", None),
            P(("row", "col"), None),
            P(("row", "col"), None),
            P(("row", "col"), None),
        ),
        check_vma=False,
    )
```

```python
import jax
import jax.numpy as jnp
from jax import lax
from jax.experimental import pallas as pl
from jax.experimental.pallas import tpu as pltpu
from jax.sharding import PartitionSpec as P

DILATION_STEP = 3
NORM_EPS = 1e-06
BETA_ONE = 0.9
BETA_TWO = 0.95
ADAM_EPS = 1e-08
LEARN_RATE = 0.01
DECAY_RATE = 0.1
STEP_COUNT = 10.0

Z, X, Y = 8, 4, 4
PLANE = 2 * X * Y
D, E = 2560, 1280
TOK, U, R_DEV = 128, 144, 40
CW = 256
NC = E // CW
RINGS = 3
AHEAD = 2
TROWS = 48
MSG = 2 * Z
PLACES = PLANE * MSG
CB = 512
NB = 2 * D // CB
WROWS = 80
TILE = 16
PAD = 16
TAPS = 4

MESH = pl.DeviceIdType.MESH
F32, BF16, I32 = jnp.float32, jnp.bfloat16, jnp.int32


class Here:
    def __init__(self):
        self.row = lax.axis_index("row")
        self.col = lax.axis_index("col")
        self.z = self.row // 2
        self.core = self.row % 2
        self.x = self.col // Y
        self.y = self.col % Y
        self.plane = self.core * (X * Y) + self.col

    def mate(self, i):
        q = lax.rem(self.plane + i, PLANE)
        return q, (self.z * 2 + q // (X * Y), q % (X * Y))

    def zed(self, step):
        return lax.rem(self.z + step + Z, Z)

    def at_z(self, step):
        return (self.zed(step) * 2 + self.core, self.col)

    def exx(self, step):
        return lax.rem(self.x + step + X, X)

    def wye(self, step):
        return lax.rem(self.y + step + Y, Y)

    def at_x(self, step):
        return (self.row, self.exx(step) * Y + self.y)

    def at_y(self, step):
        return (self.row, self.x * Y + self.wye(step))

    def neighbour(self, step):
        return (self.row, lax.rem(self.col + step + X * Y, X * Y))

    def partner(self):
        return (self.z * 2 + 1 - self.core, self.col)


def remote(src, dst, send, recv, device):
    return pltpu.make_async_remote_copy(
        src_ref=src, dst_ref=dst, send_sem=send, recv_sem=recv, device_id=device, device_id_type=MESH
    )


def greet(here):
    barrier = pltpu.get_barrier_semaphore()

    def one(i, carry):
        _, device = here.mate(i)
        pl.semaphore_signal(barrier, inc=1, device_id=device, device_id_type=MESH)
        return carry

    lax.fori_loop(1, PLANE, one, 0)
    for step in range(1, Z):
        pl.semaphore_signal(barrier, inc=1, device_id=here.at_z(step), device_id_type=MESH)
    return lambda: pl.semaphore_wait(barrier, PLANE - 1 + Z - 1)


def iota(shape, dim):
    return lax.broadcasted_iota(I32, shape, dim)


def one_hot(mask):
    return jnp.where(mask, 1.0, 0.0).astype(BF16)


def nn(left, right):
    return jnp.dot(left, right, preferred_element_type=F32)


def tn(left, right):
    return lax.dot_general(left, right, (((0,), (0,)), ((), ())), preferred_element_type=F32)


def nt(left, right):
    return lax.dot_general(left, right, (((1,), (1,)), ((), ())), preferred_element_type=F32)


def column_of(row, size):
    eye = iota((size, size), 0) == iota((size, size), 1)
    return jnp.sum(jnp.where(eye, row, 0), axis=1, keepdims=True)


def plan_slots(owner_ref, local_ref, expand_ref, spread, spread_t, req_out):
    owner_r = owner_ref[...]
    owner_c = column_of(owner_r, U)
    local_c = column_of(local_ref[...], U)
    same = owner_c == owner_r
    earlier_c = same & (iota((U, U), 1) < iota((U, U), 0))
    earlier_r = same & (iota((U, U), 0) < iota((U, U), 1))
    k_c = (owner_c >> 5) * 2 + jnp.sum(jnp.where(earlier_c, 1, 0), axis=1, keepdims=True)
    k_r = (owner_r >> 5) * 2 + jnp.sum(jnp.where(earlier_r, 1, 0), axis=0, keepdims=True)
    mates = one_hot((owner_r & 31) == iota((PLANE, U), 0))
    wanted = jnp.where(k_c == iota((U, 128), 1), local_c + 1, 0).astype(F32).astype(BF16)
    request = nn(mates, wanted)
    for q in range(PLANE):
        req_out[q] = request[q : q + 1, :]
    expand = expand_ref[...]
    reads = jnp.zeros((U, TOK), F32)
    for lookup in range(2):
        reads = reads + jnp.where(expand[lookup : lookup + 1, :] == iota((U, TOK), 0), 1.0, 0.0)
    reads = reads.astype(BF16)
    places = one_hot((owner_c & 31) * MSG + k_c == iota((U, PLACES), 1))
    places_t = one_hot((owner_r & 31) * MSG + k_r == iota((PLACES, U), 0))
    spread[...] = tn(reads, places).astype(BF16)
    spread_t[...] = nn(places_t, reads).astype(BF16)


def plan_serve(req_in, serve, serve_t):
    asked = req_in[:, 0, :].astype(BF16)
    wide = nn(one_hot(iota((PLACES, PLANE), 0) // MSG == iota((PLACES, PLANE), 1)), asked)
    k = iota((PLACES, 128), 0) % MSG
    value = jnp.sum(jnp.where(k == iota((PLACES, 128), 1), wide, 0.0), axis=1, keepdims=True)
    zed = (iota((PLACES, 1), 0) % MSG) // 2
    target = jnp.where(value > 0.5, zed * TROWS + value.astype(I32) - 1, -1)
    serve[...] = one_hot(target == iota((PLACES, Z * TROWS), 1))
    tall = tn(asked, one_hot(iota((PLANE, PLACES), 1) // MSG == iota((PLANE, PLACES), 0)))
    k = iota((128, PLACES), 1) % MSG
    value = jnp.sum(jnp.where(k == iota((128, PLACES), 0), tall, 0.0), axis=0, keepdims=True)
    zed = (iota((1, PLACES), 1) % MSG) // 2
    target = jnp.where(value > 0.5, zed * TROWS + value.astype(I32) - 1, -1)
    serve_t[...] = one_hot(target == iota((Z * TROWS, PLACES), 0))


def plan_docs(here, lengths_ref, docs):
    n = lengths_ref.shape[1]
    length_c = column_of(lengths_ref[...], n)
    ends = jnp.sum(jnp.where(iota((n, n), 0) <= iota((n, n), 1), length_c, 0), axis=0, keepdims=True)
    rows = docs.shape[0]
    position = here.col * TOK - PAD + iota((rows, 1), 0)
    passed = (position >= ends) & (iota((rows, n), 1) < n - 1)
    doc = jnp.sum(jnp.where(passed, 1.0, 0.0), axis=1, keepdims=True)
    doc = jnp.where(position < 0, -1.0, jnp.where(position >= 16 * TOK, -2.0, doc))
    docs[...] = jnp.broadcast_to(doc, (rows, 128))


def send_mates(here, src, dst, send, recv):
    def one(i, carry):
        q, device = here.mate(i)
        remote(src.at[q], dst.at[here.plane], send, recv, device).start()
        return carry

    lax.fori_loop(1, PLANE, one, 0)


def mates_arrived(here, dst, recv):
    ref = dst.at[pl.ds(0, PLANE - 1)]
    pltpu.make_async_copy(ref, ref, recv).wait()


def mates_sent(here, src, send):
    ref = src.at[pl.ds(0, PLANE - 1)]
    pltpu.make_async_copy(ref, ref, send).wait()


class Ring:
    def __init__(self, here, block, send, recv, far):
        self.here, self.block, self.send, self.recv, self.far = here, block, send, recv, far

    def copy(self, way, step):
        sign = 1 if way == 0 else -1
        ref = self.block(self.here.zed(-sign * (step - 1)))
        return remote(ref, ref, self.send.at[way, step - 1], self.recv.at[way, step - 1], self.here.at_z(sign))

    def steps(self, way):
        return Z // 2 if way == self.far else Z // 2 - 1

    def start(self, step):
        for way in range(2):
            if step <= self.steps(way):
                self.copy(way, step).start()

    def arrived(self, step):
        got = []
        for way in range(2):
            if step <= self.steps(way):
                sign = 1 if way == 0 else -1
                ref = self.block(self.here.zed(-sign * step))
                remote(ref, ref, self.send.at[way, step - 1], self.recv.at[way, step - 1], self.here.at_z(-sign)).wait_recv()
                got.append(-sign * step)
        return got

    def sent(self, step):
        for way in range(2):
            if step <= self.steps(way):
                self.copy(way, step).wait_send()

    def drain(self):
        for way in range(2):
            for step in range(2, self.steps(way) + 1):
                self.copy(way, step).wait_send()


class Cross:
    def __init__(self, here, axis, weights, base, send, recv):
        self.here, self.weights, self.base, self.send, self.recv = here, weights, base, send, recv
        self.at = here.at_x if axis == "x" else here.at_y
        self.place = here.exx if axis == "x" else here.wye

    def copy(self, way, zz, i):
        sign = 1 if way % 2 == 0 else -1
        if way < 2:
            ref = self.weights.at[self.base + self.place(0), zz, self.here.core]
        else:
            ref = self.weights.at[self.base + self.place(-sign), zz, self.here.core, :, pl.ds((way - 2) * (CB // 2), CB // 2)]
        return remote(ref, ref, self.send.at[way, i], self.recv.at[way, i], self.at(sign))

    def got(self, way, zz, i):
        sign = 1 if way % 2 == 0 else -1
        if way < 2:
            ref = self.weights.at[self.base + self.place(-sign), zz, self.here.core]
        else:
            ref = self.weights.at[
                self.base + self.place(-2 * sign), zz, self.here.core, :, pl.ds((way - 2) * (CB // 2), CB // 2)
            ]
        return remote(ref, ref, self.send.at[way, i], self.recv.at[way, i], self.at(-sign))

    def start(self, zz, i):
        for way in (0, 1):
            self.copy(way, zz, i).start()

    def relay(self, zz, i):
        for way in (0, 1):
            self.got(way, zz, i).wait_recv()
            self.copy(way + 2, zz, i).start()

    def finish(self, zz, i):
        for way in (2, 3):
            self.got(way, zz, i).wait_recv()

    def drain(self, zz, i):
        for way in range(4):
            self.copy(way, zz, i).wait_send()


def lanes(b):
    return slice((b % (NB // 2)) * CB, (b % (NB // 2) + 1) * CB)


def row_tile(t):
    return pl.ds(pl.multiple_of(t * TILE, TILE), TILE)


def mean_scale(total):
    return lax.rsqrt(total / D + NORM_EPS)


BLOCKS = range(NB // 2)
STATS = ("key_scale", "hidden_scale", "score", "gate", "gated_scale")


def keep(stats, name, rows, value):
    stats[STATS.index(name), rows, :] = jnp.broadcast_to(value, (TILE, 128))


def kept(stats, name, rows):
    return wide(stats[STATS.index(name), rows, :])


def wide(value):
    return jnp.concatenate([value] * (CB // 128), axis=1)


def gate_tile(t, keys, values, hidden, gated, gnorm, stats):
    rows = row_tile(t)
    kk = jnp.zeros((TILE, CB), F32)
    hh, hk = kk, kk
    for b in BLOCKS:
        key = keys[b, rows, :]
        hid = hidden[rows, lanes(b)].astype(F32)
        kk, hh, hk = kk + key * key, hh + hid * hid, hk + hid * key
    key_scale = mean_scale(jnp.sum(kk, axis=1, keepdims=True))
    hidden_scale = mean_scale(jnp.sum(hh, axis=1, keepdims=True))
    score = jnp.sum(hk, axis=1, keepdims=True) * key_scale * hidden_scale
    gate = jax.nn.sigmoid(score / D**0.5)
    gg = jnp.zeros((TILE, CB), F32)
    for b in BLOCKS:
        rounded = (gate * values[b, rows, :]).astype(BF16)
        gated[rows, lanes(b)] = rounded
        gg = gg + rounded.astype(F32) * rounded.astype(F32)
    scale = mean_scale(jnp.sum(gg, axis=1, keepdims=True))
    own = pl.ds(pl.multiple_of(PAD + t * TILE, TILE), TILE)
    for b in BLOCKS:
        gnorm[own, lanes(b)] = gated[rows, lanes(b)].astype(F32) * scale
    for name, value in zip(STATS, (key_scale, hidden_scale, score, gate, scale)):
        keep(stats, name, rows, value)


def same_docs(docs, t, sign):
    window = docs[pl.ds(pl.multiple_of(t * TILE, TILE), 3 * TILE), :]
    center = window[TILE : 2 * TILE]
    shifted = [window[TILE + sign * DILATION_STEP * j : 2 * TILE + sign * DILATION_STEP * j] for j in range(TAPS)]
    return [wide(jnp.where(center == other, 1.0, 0.0)) for other in shifted]


def conv_tile(t, docs, taps, gnorm, gated, grad, cgrad, out=None):
    rows = row_tile(t)
    masks = same_docs(docs, t, -1)
    both = pl.ds(pl.multiple_of(t * TILE, TILE), 2 * TILE)
    for b in BLOCKS:
        window = gnorm[both, lanes(b)]
        conv = taps[0:1, lanes(b)] * window[TILE:]
        for j in range(1, TAPS):
            low = TILE - DILATION_STEP * j
            conv = conv + masks[j] * (taps[j : j + 1, lanes(b)] * window[low : low + TILE])
        sig = jax.nn.sigmoid(conv)
        if out is not None:
            out[rows, lanes(b)] = (conv * sig + gated[rows, lanes(b)].astype(F32)).astype(BF16)
        cgrad[rows, lanes(b)] = grad[rows, lanes(b)].astype(F32) * sig * (1.0 + conv * (1.0 - sig))


def grad_tile(t, docs, taps, gnorm, cgrad, grad, keys, values, hidden, stats, ngrad, key_grad, value_grad):
    rows = row_tile(t)
    masks = same_docs(docs, t, 1)
    both = pl.ds(pl.multiple_of(t * TILE, TILE), 2 * TILE)
    own = pl.ds(pl.multiple_of(PAD + t * TILE, TILE), TILE)
    dots = jnp.zeros((TILE, CB), F32)
    for b in BLOCKS:
        window = cgrad[both, lanes(b)]
        total = taps[0:1, lanes(b)] * window[:TILE]
        for j in range(1, TAPS):
            low = DILATION_STEP * j
            total = total + masks[j] * (taps[j : j + 1, lanes(b)] * window[low : low + TILE])
        ngrad[:, lanes(b)] = total
        dots = dots + gnorm[own, lanes(b)] * total
    mean = jnp.sum(dots, axis=1, keepdims=True) / D
    key_scale, hidden_scale, score, gate, scale = [kept(stats, name, rows) for name in STATS]
    dots = jnp.zeros((TILE, CB), F32)
    for b in BLOCKS:
        total = grad[rows, lanes(b)].astype(F32) + scale * (ngrad[:, lanes(b)] - gnorm[own, lanes(b)] * mean)
        value_grad[rows, lanes(b)] = (total * gate).astype(BF16)
        dots = dots + total * values[b, rows, :]
    score_grad = gate * (1.0 - gate) * jnp.sum(dots, axis=1, keepdims=True)
    front = key_scale * score_grad / D**0.5
    by_hidden, by_key = front * hidden_scale, front * (key_scale * score / D)
    for b in BLOCKS:
        target = by_hidden * hidden[rows, lanes(b)].astype(F32) - by_key * keys[b, rows, :]
        key_grad[rows, lanes(b)] = target.astype(BF16)


def adamw(current, moment, second, gradient):
    moment_new = BETA_ONE * moment + (1.0 - BETA_ONE) * gradient
    second_new = BETA_TWO * second + (1.0 - BETA_TWO) * gradient * gradient
    first_hat = moment_new / (1.0 - BETA_ONE**STEP_COUNT)
    second_hat = second_new / (1.0 - BETA_TWO**STEP_COUNT)
    updated = current - LEARN_RATE * (first_hat / (jnp.sqrt(second_hat) + ADAM_EPS) + DECAY_RATE * current)
    return updated, moment_new, second_new


def kernel(
    owner_ref, local_ref, expand_ref, lengths_ref, taps_ref, table_ref, hidden_ref, grad_ref, wk_ref, wv_ref,
    out, row_grad,
    weights, tab, req_out, req_in, reply, fetched, slots, arrived, partial, give, take,
    spread, spread_t, serve, serve_t, docs, memory, keys, values, hidden, grad, gated, gnorm, cgrad, ngrad, stats,
    key_grad, value_grad, grads_t, halo_in, give_far, take_far,
    load_sem, in_sem, req_send, req_recv, rep_send, rep_recv, tz_send, tz_recv, wz_send, wz_recv,
    xy_send, xy_recv, core_send, core_recv, halo_send, halo_recv, slot_send, slot_recv, ring_send, ring_recv,
    far_send, far_recv,
):
    here = Here()
    greeted = greet(here)
    loads = []
    for b in range(NB):
        src = wk_ref if b < NB // 2 else wv_ref
        loads.append(pltpu.make_async_copy(src.at[:, pl.ds(lanes(b).start, CB)], weights.at[b, here.z, here.core], load_sem.at[b]))
    inputs = [pltpu.make_async_copy(hidden_ref, hidden, in_sem.at[0]), pltpu.make_async_copy(grad_ref, grad.at[pl.ds(0, TOK)], in_sem.at[1])]
    for load in loads + inputs:
        load.start()
    for c in range(NC):
        tab[here.z, c, 0:R_DEV, :] = table_ref[:, c * CW : (c + 1) * CW].astype(BF16)
        tab[here.z, c, R_DEV:TROWS, :] = jnp.zeros((TROWS - R_DEV, CW), BF16)
    plan_slots(owner_ref, local_ref, expand_ref, spread, spread_t, req_out)
    greeted()

    spans = (pl.ds(0, NC // 2 + 1), pl.ds(NC // 2 + 1, NC // 2))
    tables = [
        Ring(here, lambda zz, span=span: tab.at[zz, span], tz_send.at[i], tz_recv.at[i], i) for i, span in enumerate(spans)
    ]
    blocks = [here.x, NB // 2 + here.y, NB // 2 - 1, NB - 1]
    pieces = [
        Ring(here, lambda zz, b=b: weights.at[b, zz, here.core], wz_send.at[i], wz_recv.at[i], i % 2)
        for i, b in enumerate(blocks)
    ]
    crosses = [
        Cross(here, "x", weights, 0, xy_send.at[0], xy_recv.at[0]),
        Cross(here, "y", weights, NB // 2, xy_send.at[1], xy_recv.at[1]),
    ]
    zeds = [here.zed(step) for step in (0, -1, 1, -2, 2, -3, 3, 4)]
    key_ring, value_ring, last_key, last_value = pieces
    x_cross, y_cross = crosses
    for ring in tables:
        ring.start(1)
    send_mates(here, req_out, req_in, req_send, req_recv)
    req_in[here.plane] = req_out[here.plane]
    for load in loads + inputs:
        load.wait()
    early = remote(
        grad.at[pl.ds(0, PAD)], grad.at[pl.ds(TOK, PAD)], halo_send.at[2], halo_recv.at[2], here.neighbour(-1)
    )
    early.start()
    plan_docs(here, lengths_ref, docs)
    for ring in tables:
        ring.sent(1)
    key_ring.start(1)
    mates_arrived(here, req_in, req_recv)
    plan_serve(req_in, serve, serve_t)
    key_ring.sent(1)
    value_ring.start(1)
    for step in (1, 2, 3):
        for ring in tables:
            ring.arrived(step)
            ring.start(step + 1)
        for ring, cross in ((key_ring, x_cross), (value_ring, y_cross)):
            ring.arrived(step)
            ring.start(step + 1)
            for i in (2 * step - 1, 2 * step):
                cross.start(zeds[i], i)
        if step > 1:
            for cross in crosses:
                for i in (2 * step - 3, 2 * step - 2):
                    cross.relay(zeds[i], i)
    last_key.start(1)
    for ring in tables:
        ring.arrived(4)
    for c in range(NC):
        rows = nn(serve[...], tab[:, c].reshape(Z * TROWS, CW))
        reply[c] = rows.astype(BF16).reshape(PLANE, MSG, CW)
        fetched[c, here.plane] = reply[c, here.plane]
        send_mates(here, reply.at[c], fetched.at[c], rep_send.at[c], rep_recv.at[c])
    last_key.sent(1)
    last_value.start(1)
    for ring, cross in ((key_ring, x_cross), (value_ring, y_cross)):
        ring.arrived(4)
        cross.start(zeds[Z - 1], Z - 1)

    def to_partner(b):
        ref = weights.at[b, :, here.core]
        return remote(ref, ref, core_send.at[b], core_recv.at[b], here.partner())

    def from_partner(b):
        ref = weights.at[b, :, 1 - here.core]
        remote(ref, ref, core_send.at[b], core_recv.at[b], here.partner()).wait_recv()

    def project(b):
        from_partner(b)
        return nn(memory[...], weights[b].reshape(E, CB))

    def project_key(b):
        keys[b] = project(b)

    def project_value(b):
        values[b] = project(NB // 2 + b)

    for b in (here.x, NB // 2 + here.y):
        to_partner(b).start()
    for step in (1, 2, 3):
        for ring in pieces[2:]:
            ring.arrived(step)
            ring.start(step + 1)
        if step == 1:
            for cross in crosses:
                for i in (Z - 3, Z - 2):
                    cross.relay(zeds[i], i)
    for cross in crosses:
        cross.relay(zeds[Z - 1], Z - 1)
    for step in (-1, 1):
        to_partner(here.exx(step)).start()
        to_partner(NB // 2 + here.wye(step)).start()
    for c in range(NC):
        mates_arrived(here, fetched.at[c], rep_recv.at[c])
        memory[:, c * CW : (c + 1) * CW] = nn(spread[...], fetched[c].reshape(PLACES, CW)).astype(BF16)
    project_key(here.x)
    project_value(here.y)
    for i in range(1, Z):
        for cross in crosses:
            cross.finish(zeds[i], i)
    to_partner(here.exx(2)).start()
    to_partner(NB // 2 + here.wye(2)).start()
    for ring in pieces[2:]:
        ring.arrived(4)
    to_partner(NB // 2 - 1).start()
    to_partner(NB - 1).start()
    for step in (-1, 1, 2):
        project_key(here.exx(step))
        project_value(here.wye(step))
    project_key(NB // 2 - 1)
    project_value(NB // 2 - 1)

    last = TOK // TILE - 1

    def halo(way):
        src = gated.at[pl.ds(last * TILE if way == 0 else 0, TILE)]
        return remote(src, halo_in.at[way], halo_send.at[way], halo_recv.at[way], here.neighbour(1 - 2 * way))

    def gate_step(t, carry):
        gate_tile(t, keys, values, hidden, gated, gnorm, stats)
        return carry

    def conv_step(t, carry):
        conv_tile(t, docs, taps_ref, gnorm, gated, grad, cgrad, out)
        return carry

    def grad_step(t, carry):
        grad_tile(t, docs, taps_ref, gnorm, cgrad, grad, keys, values, hidden, stats, ngrad, key_grad, value_grad)
        return carry

    gate_step(last, 0)
    halo(0).start()
    gate_step(0, 0)
    halo(1).start()
    lax.fori_loop(1, last, gate_step, 0)
    lax.fori_loop(1, last + 1, conv_step, 0)
    for way, start in ((0, 0), (1, PAD + TOK)):
        halo(way).wait_recv()
        total = jnp.zeros((TILE, CB), F32)
        for b in BLOCKS:
            rows = halo_in[way, :, lanes(b)].astype(F32)
            total = total + rows * rows
        scale = mean_scale(jnp.sum(total, axis=1, keepdims=True))
        for b in BLOCKS:
            gnorm[start : start + PAD, lanes(b)] = halo_in[way, :, lanes(b)].astype(F32) * scale
    early.wait_recv()
    conv_step(0, 0)
    conv_tile(last + 1, docs, taps_ref, gnorm, gated, grad, cgrad)
    lax.fori_loop(0, last + 1, grad_step, 0)

    for b in range(NB):
        source = key_grad if b < NB // 2 else value_grad
        grads_t[b] = source[:, lanes(b)].T
    def send_slots(c):
        first, stop = c * CW // (2 * WROWS), -(-(c + 1) * CW // (2 * WROWS))
        skip = c * CW - first * 2 * WROWS
        total = jnp.zeros((CW, TOK), F32)
        for b in range(NB):
            part = weights[b, first:stop].reshape((stop - first) * 2 * WROWS, CB)[skip : skip + CW]
            total = total + nn(part, grads_t[b])
        slots[c] = nt(spread_t[...], total.astype(BF16)).astype(BF16).reshape(PLANE, MSG, CW)
        arrived[c, here.plane] = slots[c, here.plane]
        if c >= AHEAD:
            mates_sent(here, slots.at[c - AHEAD], slot_send.at[c - AHEAD])
        send_mates(here, slots.at[c], arrived.at[c], slot_send.at[c], slot_recv.at[c])

    def hop(c, way, step):
        sign = 1 if way == 0 else -1
        return remote(
            give.at[c, way, step - 1], take.at[c, way, step - 1],
            ring_send.at[c, way, step - 1], ring_recv.at[c, way, step - 1], here.at_z(sign),
        )

    def length(c, way):
        return Z // 2 if way == c % 2 else Z // 2 - 1

    def advance(c, step):
        for way in range(2):
            final = length(c, way)
            if step > final:
                continue
            sign = 1 if way == 0 else -1
            mine = partial[c, here.zed(sign * (final - step + 1))]
            if step > 1:
                hop(c, way, step - 1).wait_recv()
                mine = mine + take[c, way, step - 2].astype(F32)
            give[c, way, step - 1] = mine.astype(BF16)
            hop(c, way, step).start()

    def far(c, step):
        place = c - RINGS
        return remote(
            give_far.at[place, here.zed(step)], take_far.at[place, step],
            far_send.at[place, step], far_recv.at[place, step], here.at_z(step),
        )

    def send_far(c):
        give_far[c - RINGS] = partial[c].astype(BF16)
        for step in range(1, Z):
            far(c, step).start()

    def finish(c):
        total = partial[c, here.z]
        if c < RINGS:
            for way in range(2):
                final = length(c, way)
                hop(c, way, final).wait_recv()
                total = total + take[c, way, final - 1].astype(F32)
        else:
            for step in range(1, Z):
                far(c, step).wait_recv()
                total = total + take_far[c - RINGS, step].astype(F32)
        row_grad[:, c * CW : (c + 1) * CW] = total[:R_DEV]

    for c in range(AHEAD):
        send_slots(c)
    for c in range(NC):
        if c + AHEAD < NC:
            send_slots(c + AHEAD)
        mates_arrived(here, arrived.at[c], slot_recv.at[c])
        partial[c] = nn(serve_t[...], arrived[c].reshape(PLACES, CW)).reshape(Z, TROWS, CW)
        if c < RINGS:
            advance(c, 1)
        else:
            send_far(c)
        for back in range(1, 4):
            if 0 <= c - back < RINGS:
                advance(c - back, back + 1)
    for step in range(2, Z // 2 + 1):
        for c in range(RINGS):
            if c + step > NC:
                advance(c, step)
    for c in range(NC):
        finish(c)

    value_ring.sent(1)
    last_value.sent(1)
    for b in range(NB):
        to_partner(b).wait_send()
    for ring in tables + pieces:
        ring.drain()
    for i in range(1, Z):
        for cross in crosses:
            cross.drain(zeds[i], i)
    early.wait_send()
    for way in range(2):
        halo(way).wait_send()
    mates_sent(here, req_out, req_send)
    for c in range(NC):
        mates_sent(here, reply.at[c], rep_send.at[c])
        if c >= NC - AHEAD:
            mates_sent(here, slots.at[c], slot_send.at[c])
        if c < RINGS:
            for way in range(2):
                for step in range(1, length(c, way) + 1):
                    hop(c, way, step).wait_send()
        else:
            for step in range(1, Z):
                far(c, step).wait_send()


def on_device(
    hidden, grad_out, w_key, w_value, depthwise_weight, table, adam_m, adam_v,
    row_owner, row_local, expand_index, doc_lengths,
):
    vmem = pl.BlockSpec(memory_space=pltpu.VMEM)
    any_ = pl.BlockSpec(memory_space=pl.ANY)
    dma = pltpu.SemaphoreType.DMA
    rows = (NC, PLANE, MSG, CW)
    hops = (RINGS, 2, Z // 2)
    fars = (NC - RINGS, Z)
    memory_out, row_grad = pl.pallas_call(
        kernel,
        out_shape=(jax.ShapeDtypeStruct((TOK, D), BF16), jax.ShapeDtypeStruct((R_DEV, E), F32)),
        in_specs=[vmem] * 6 + [any_] * 4,
        out_specs=(vmem, vmem),
        scratch_shapes=[
            pltpu.VMEM((NB, Z, 2, WROWS, CB), BF16),
            pltpu.VMEM((Z, NC, TROWS, CW), BF16),
            pltpu.VMEM((PLANE, 1, 128), F32),
            pltpu.VMEM((PLANE, 1, 128), F32),
            pltpu.VMEM(rows, BF16),
            pltpu.VMEM(rows, BF16),
            pltpu.VMEM(rows, BF16),
            pltpu.VMEM(rows, BF16),
            pltpu.VMEM((NC, Z, TROWS, CW), F32),
            pltpu.VMEM(hops + (TROWS, CW), BF16),
            pltpu.VMEM(hops + (TROWS, CW), BF16),
            pltpu.VMEM((TOK, PLACES), BF16),
            pltpu.VMEM((PLACES, TOK), BF16),
            pltpu.VMEM((PLACES, Z * TROWS), BF16),
            pltpu.VMEM((Z * TROWS, PLACES), BF16),
            pltpu.VMEM((TOK + 3 * PAD, 128), F32),
            pltpu.VMEM((TOK, E), BF16),
            pltpu.VMEM((NB // 2, TOK, CB), F32),
            pltpu.VMEM((NB // 2, TOK, CB), F32),
            pltpu.VMEM((TOK, D), BF16),
            pltpu.VMEM((TOK + PAD, D), BF16),
            pltpu.VMEM((TOK, D), BF16),
            pltpu.VMEM((PAD + TOK + PAD, D), F32),
            pltpu.VMEM((TOK + PAD, D), F32),
            pltpu.VMEM((TILE, D), F32),
            pltpu.VMEM((len(STATS), TOK, 128), F32),
            pltpu.VMEM((TOK, D), BF16),
            pltpu.VMEM((TOK, D), BF16),
            pltpu.VMEM((NB, CB, TOK), BF16),
            pltpu.VMEM((2, TILE, D), BF16),
            pltpu.VMEM(fars + (TROWS, CW), BF16),
            pltpu.VMEM(fars + (TROWS, CW), BF16),
            dma((NB,)), dma((2,)), dma, dma, dma((NC,)), dma((NC,)),
            dma((2, 2, Z // 2)), dma((2, 2, Z // 2)), dma((4, 2, Z // 2)), dma((4, 2, Z // 2)),
            dma((2, 4, Z)), dma((2, 4, Z)), dma((NB,)), dma((NB,)),
            dma((3,)), dma((3,)), dma((NC,)), dma((NC,)), dma(hops), dma(hops), dma(fars), dma(fars),
        ],
        compiler_params=pltpu.CompilerParams(
            collective_id=0, has_side_effects=True, vmem_limit_bytes=56 * 1024 * 1024
        ),
        name="memory_branch",
    )(
        row_owner.reshape(1, U), row_local, expand_index[0].T, doc_lengths, depthwise_weight,
        table, hidden[0], grad_out[0], w_key, w_value,
    )
    new_table, new_moment, new_second = adamw(table, adam_m, adam_v, row_grad)
    return (memory_out[None], new_table, new_moment, new_second)


def solution(mesh):
    placed = (
        P("row", "col", None),
        P("row", "col", None),
        P("row", None),
        P("row", None),
        P(),
        P(("row", "col"), None),
        P(("row", "col"), None),
        P(("row", "col"), None),
        P("row", "col", None),
        P("row", "col"),
        P("row", "col", None),
        P("row", None),
    )
    return jax.shard_map(
        on_device,
        mesh=mesh,
        in_specs=placed,
        out_specs=(
            P("row", "col", None),
            P(("row", "col"), None),
            P(("row", "col"), None),
            P(("row", "col"), None),
        ),
        check_vma=False,
    )
```

```python
import jax
import jax.numpy as jnp
from jax import lax
from jax.experimental import pallas as pl
from jax.experimental.pallas import tpu as pltpu
from jax.sharding import PartitionSpec as P

DILATION_STEP = 3
NORM_EPS = 1e-06
BETA_ONE = 0.9
BETA_TWO = 0.95
ADAM_EPS = 1e-08
LEARN_RATE = 0.01
DECAY_RATE = 0.1
STEP_COUNT = 10.0

Z, X, Y = 8, 4, 4
PLANE = 2 * X * Y
D, E = 2560, 1280
TOK, U, R_DEV = 128, 144, 40
CW = 256
NC = E // CW
RINGS = 2
AHEAD = 2
TROWS = 48
MSG = 2 * Z
PLACES = PLANE * MSG
CB = 512
NB = 2 * D // CB
WROWS = 80
TILE = 16
PAD = 16
TAPS = 4

MESH = pl.DeviceIdType.MESH
F32, BF16, I32 = jnp.float32, jnp.bfloat16, jnp.int32


class Here:
    def __init__(self):
        self.row = lax.axis_index("row")
        self.col = lax.axis_index("col")
        self.z = self.row // 2
        self.core = self.row % 2
        self.x = self.col // Y
        self.y = self.col % Y
        self.plane = self.core * (X * Y) + self.col

    def mate(self, i):
        q = lax.rem(self.plane + i, PLANE)
        return q, (self.z * 2 + q // (X * Y), q % (X * Y))

    def zed(self, step):
        return lax.rem(self.z + step + Z, Z)

    def at_z(self, step):
        return (self.zed(step) * 2 + self.core, self.col)

    def exx(self, step):
        return lax.rem(self.x + step + X, X)

    def wye(self, step):
        return lax.rem(self.y + step + Y, Y)

    def at_x(self, step):
        return (self.row, self.exx(step) * Y + self.y)

    def at_y(self, step):
        return (self.row, self.x * Y + self.wye(step))

    def neighbour(self, step):
        return (self.row, lax.rem(self.col + step + X * Y, X * Y))

    def partner(self):
        return (self.z * 2 + 1 - self.core, self.col)


def remote(src, dst, send, recv, device):
    return pltpu.make_async_remote_copy(
        src_ref=src, dst_ref=dst, send_sem=send, recv_sem=recv, device_id=device, device_id_type=MESH
    )


def greet(here):
    barrier = pltpu.get_barrier_semaphore()

    def one(i, carry):
        _, device = here.mate(i)
        pl.semaphore_signal(barrier, inc=1, device_id=device, device_id_type=MESH)
        return carry

    lax.fori_loop(1, PLANE, one, 0)
    for step in range(1, Z):
        pl.semaphore_signal(barrier, inc=1, device_id=here.at_z(step), device_id_type=MESH)
    return lambda: pl.semaphore_wait(barrier, PLANE - 1 + Z - 1)


def iota(shape, dim):
    return lax.broadcasted_iota(I32, shape, dim)


def one_hot(mask):
    return jnp.where(mask, 1.0, 0.0).astype(BF16)


def nn(left, right):
    return jnp.dot(left, right, preferred_element_type=F32)


def tn(left, right):
    return lax.dot_general(left, right, (((0,), (0,)), ((), ())), preferred_element_type=F32)


def nt(left, right):
    return lax.dot_general(left, right, (((1,), (1,)), ((), ())), preferred_element_type=F32)


def column_of(row, size):
    eye = iota((size, size), 0) == iota((size, size), 1)
    return jnp.sum(jnp.where(eye, row, 0), axis=1, keepdims=True)


def plan_slots(owner_ref, local_ref, expand_ref, spread, spread_t, req_out):
    owner_r = owner_ref[...]
    owner_c = column_of(owner_r, U)
    local_c = column_of(local_ref[...], U)
    same = owner_c == owner_r
    earlier_c = same & (iota((U, U), 1) < iota((U, U), 0))
    earlier_r = same & (iota((U, U), 0) < iota((U, U), 1))
    k_c = (owner_c >> 5) * 2 + jnp.sum(jnp.where(earlier_c, 1, 0), axis=1, keepdims=True)
    k_r = (owner_r >> 5) * 2 + jnp.sum(jnp.where(earlier_r, 1, 0), axis=0, keepdims=True)
    mates = one_hot((owner_r & 31) == iota((PLANE, U), 0))
    wanted = jnp.where(k_c == iota((U, 128), 1), local_c + 1, 0).astype(F32).astype(BF16)
    request = nn(mates, wanted)
    for q in range(PLANE):
        req_out[q] = request[q : q + 1, :]
    expand = expand_ref[...]
    reads = jnp.zeros((U, TOK), F32)
    for lookup in range(2):
        reads = reads + jnp.where(expand[lookup : lookup + 1, :] == iota((U, TOK), 0), 1.0, 0.0)
    reads = reads.astype(BF16)
    places = one_hot((owner_c & 31) * MSG + k_c == iota((U, PLACES), 1))
    places_t = one_hot((owner_r & 31) * MSG + k_r == iota((PLACES, U), 0))
    spread[...] = tn(reads, places).astype(BF16)
    spread_t[...] = nn(places_t, reads).astype(BF16)


def plan_serve(req_in, serve, serve_t):
    asked = req_in[:, 0, :].astype(BF16)
    wide = nn(one_hot(iota((PLACES, PLANE), 0) // MSG == iota((PLACES, PLANE), 1)), asked)
    k = iota((PLACES, 128), 0) % MSG
    value = jnp.sum(jnp.where(k == iota((PLACES, 128), 1), wide, 0.0), axis=1, keepdims=True)
    zed = (iota((PLACES, 1), 0) % MSG) // 2
    target = jnp.where(value > 0.5, zed * TROWS + value.astype(I32) - 1, -1)
    serve[...] = one_hot(target == iota((PLACES, Z * TROWS), 1))
    tall = tn(asked, one_hot(iota((PLANE, PLACES), 1) // MSG == iota((PLANE, PLACES), 0)))
    k = iota((128, PLACES), 1) % MSG
    value = jnp.sum(jnp.where(k == iota((128, PLACES), 0), tall, 0.0), axis=0, keepdims=True)
    zed = (iota((1, PLACES), 1) % MSG) // 2
    target = jnp.where(value > 0.5, zed * TROWS + value.astype(I32) - 1, -1)
    serve_t[...] = one_hot(target == iota((Z * TROWS, PLACES), 0))


def plan_docs(here, lengths_ref, docs):
    n = lengths_ref.shape[1]
    length_c = column_of(lengths_ref[...], n)
    ends = jnp.sum(jnp.where(iota((n, n), 0) <= iota((n, n), 1), length_c, 0), axis=0, keepdims=True)
    rows = docs.shape[0]
    position = here.col * TOK - PAD + iota((rows, 1), 0)
    passed = (position >= ends) & (iota((rows, n), 1) < n - 1)
    doc = jnp.sum(jnp.where(passed, 1.0, 0.0), axis=1, keepdims=True)
    doc = jnp.where(position < 0, -1.0, jnp.where(position >= 16 * TOK, -2.0, doc))
    docs[...] = jnp.broadcast_to(doc, (rows, 128))


def send_mates(here, src, dst, send, recv):
    def one(i, carry):
        q, device = here.mate(i)
        remote(src.at[q], dst.at[here.plane], send, recv, device).start()
        return carry

    lax.fori_loop(1, PLANE, one, 0)


def mates_arrived(here, dst, recv):
    ref = dst.at[pl.ds(0, PLANE - 1)]
    pltpu.make_async_copy(ref, ref, recv).wait()


def mates_sent(here, src, send):
    ref = src.at[pl.ds(0, PLANE - 1)]
    pltpu.make_async_copy(ref, ref, send).wait()


class Ring:
    def __init__(self, here, block, send, recv, far):
        self.here, self.block, self.send, self.recv, self.far = here, block, send, recv, far

    def copy(self, way, step):
        sign = 1 if way == 0 else -1
        ref = self.block(self.here.zed(-sign * (step - 1)))
        return remote(ref, ref, self.send.at[way, step - 1], self.recv.at[way, step - 1], self.here.at_z(sign))

    def steps(self, way):
        return Z // 2 if way == self.far else Z // 2 - 1

    def start(self, step):
        for way in range(2):
            if step <= self.steps(way):
                self.copy(way, step).start()

    def arrived(self, step):
        got = []
        for way in range(2):
            if step <= self.steps(way):
                sign = 1 if way == 0 else -1
                ref = self.block(self.here.zed(-sign * step))
                remote(ref, ref, self.send.at[way, step - 1], self.recv.at[way, step - 1], self.here.at_z(-sign)).wait_recv()
                got.append(-sign * step)
        return got

    def sent(self, step):
        for way in range(2):
            if step <= self.steps(way):
                self.copy(way, step).wait_send()

    def drain(self):
        for way in range(2):
            for step in range(2, self.steps(way) + 1):
                self.copy(way, step).wait_send()


class Cross:
    def __init__(self, here, axis, weights, base, send, recv):
        self.here, self.weights, self.base, self.send, self.recv = here, weights, base, send, recv
        self.at = here.at_x if axis == "x" else here.at_y
        self.place = here.exx if axis == "x" else here.wye

    def copy(self, way, zz, i):
        sign = 1 if way % 2 == 0 else -1
        if way < 2:
            ref = self.weights.at[self.base + self.place(0), zz, self.here.core]
        else:
            ref = self.weights.at[self.base + self.place(-sign), zz, self.here.core, :, pl.ds((way - 2) * (CB // 2), CB // 2)]
        return remote(ref, ref, self.send.at[way, i], self.recv.at[way, i], self.at(sign))

    def got(self, way, zz, i):
        sign = 1 if way % 2 == 0 else -1
        if way < 2:
            ref = self.weights.at[self.base + self.place(-sign), zz, self.here.core]
        else:
            ref = self.weights.at[
                self.base + self.place(-2 * sign), zz, self.here.core, :, pl.ds((way - 2) * (CB // 2), CB // 2)
            ]
        return remote(ref, ref, self.send.at[way, i], self.recv.at[way, i], self.at(-sign))

    def block(self, step):
        return self.base + self.place(step)

    def start(self, zz, i):
        for way in (0, 1):
            self.copy(way, zz, i).start()

    def relay(self, zz, i):
        for way in (0, 1):
            self.got(way, zz, i).wait_recv()
            self.copy(way + 2, zz, i).start()

    def finish(self, zz, i):
        for way in (2, 3):
            self.got(way, zz, i).wait_recv()

    def drain(self, zz, i):
        for way in range(4):
            self.copy(way, zz, i).wait_send()


def lanes(b):
    return slice((b % (NB // 2)) * CB, (b % (NB // 2) + 1) * CB)


def row_tile(t):
    return pl.ds(pl.multiple_of(t * TILE, TILE), TILE)


def mean_scale(total):
    return lax.rsqrt(total / D + NORM_EPS)


BLOCKS = range(NB // 2)
STATS = ("key_scale", "hidden_scale", "score", "gate", "gated_scale")


def keep(stats, name, rows, value):
    stats[STATS.index(name), rows, :] = jnp.broadcast_to(value, (TILE, 128))


def kept(stats, name, rows):
    return wide(stats[STATS.index(name), rows, :])


def wide(value):
    return jnp.concatenate([value] * (CB // 128), axis=1)


def gate_tile(t, keys, values, hidden, gated, gnorm, stats):
    rows = row_tile(t)
    kk = jnp.zeros((TILE, CB), F32)
    hh, hk = kk, kk
    for b in BLOCKS:
        key = keys[b, rows, :]
        hid = hidden[rows, lanes(b)].astype(F32)
        kk, hh, hk = kk + key * key, hh + hid * hid, hk + hid * key
    key_scale = mean_scale(jnp.sum(kk, axis=1, keepdims=True))
    hidden_scale = mean_scale(jnp.sum(hh, axis=1, keepdims=True))
    score = jnp.sum(hk, axis=1, keepdims=True) * key_scale * hidden_scale
    gate = jax.nn.sigmoid(score / D**0.5)
    gg = jnp.zeros((TILE, CB), F32)
    for b in BLOCKS:
        rounded = (gate * values[b, rows, :]).astype(BF16)
        gated[rows, lanes(b)] = rounded
        gg = gg + rounded.astype(F32) * rounded.astype(F32)
    scale = mean_scale(jnp.sum(gg, axis=1, keepdims=True))
    own = pl.ds(pl.multiple_of(PAD + t * TILE, TILE), TILE)
    for b in BLOCKS:
        gnorm[own, lanes(b)] = gated[rows, lanes(b)].astype(F32) * scale
    for name, value in zip(STATS, (key_scale, hidden_scale, score, gate, scale)):
        keep(stats, name, rows, value)


def same_docs(docs, t, sign):
    window = docs[pl.ds(pl.multiple_of(t * TILE, TILE), 3 * TILE), :]
    center = window[TILE : 2 * TILE]
    shifted = [window[TILE + sign * DILATION_STEP * j : 2 * TILE + sign * DILATION_STEP * j] for j in range(TAPS)]
    return [wide(jnp.where(center == other, 1.0, 0.0)) for other in shifted]


def conv_tile(t, docs, taps, gnorm, gated, grad, cgrad, out=None):
    rows = row_tile(t)
    masks = same_docs(docs, t, -1)
    both = pl.ds(pl.multiple_of(t * TILE, TILE), 2 * TILE)
    for b in BLOCKS:
        window = gnorm[both, lanes(b)]
        conv = taps[0:1, lanes(b)] * window[TILE:]
        for j in range(1, TAPS):
            low = TILE - DILATION_STEP * j
            conv = conv + masks[j] * (taps[j : j + 1, lanes(b)] * window[low : low + TILE])
        sig = jax.nn.sigmoid(conv)
        if out is not None:
            out[rows, lanes(b)] = (conv * sig + gated[rows, lanes(b)].astype(F32)).astype(BF16)
        cgrad[rows, lanes(b)] = grad[rows, lanes(b)].astype(F32) * sig * (1.0 + conv * (1.0 - sig))


def grad_tile(t, docs, taps, gnorm, cgrad, grad, keys, values, hidden, stats, ngrad, key_grad, value_grad):
    rows = row_tile(t)
    masks = same_docs(docs, t, 1)
    both = pl.ds(pl.multiple_of(t * TILE, TILE), 2 * TILE)
    own = pl.ds(pl.multiple_of(PAD + t * TILE, TILE), TILE)
    dots = jnp.zeros((TILE, CB), F32)
    for b in BLOCKS:
        window = cgrad[both, lanes(b)]
        total = taps[0:1, lanes(b)] * window[:TILE]
        for j in range(1, TAPS):
            low = DILATION_STEP * j
            total = total + masks[j] * (taps[j : j + 1, lanes(b)] * window[low : low + TILE])
        ngrad[:, lanes(b)] = total
        dots = dots + gnorm[own, lanes(b)] * total
    mean = jnp.sum(dots, axis=1, keepdims=True) / D
    key_scale, hidden_scale, score, gate, scale = [kept(stats, name, rows) for name in STATS]
    dots = jnp.zeros((TILE, CB), F32)
    for b in BLOCKS:
        total = grad[rows, lanes(b)].astype(F32) + scale * (ngrad[:, lanes(b)] - gnorm[own, lanes(b)] * mean)
        value_grad[rows, lanes(b)] = (total * gate).astype(BF16)
        dots = dots + total * values[b, rows, :]
    score_grad = gate * (1.0 - gate) * jnp.sum(dots, axis=1, keepdims=True)
    front = key_scale * score_grad / D**0.5
    by_hidden, by_key = front * hidden_scale, front * (key_scale * score / D)
    for b in BLOCKS:
        target = by_hidden * hidden[rows, lanes(b)].astype(F32) - by_key * keys[b, rows, :]
        key_grad[rows, lanes(b)] = target.astype(BF16)


def adamw(current, moment, second, gradient):
    moment_new = BETA_ONE * moment + (1.0 - BETA_ONE) * gradient
    second_new = BETA_TWO * second + (1.0 - BETA_TWO) * gradient * gradient
    first_hat = moment_new / (1.0 - BETA_ONE**STEP_COUNT)
    second_hat = second_new / (1.0 - BETA_TWO**STEP_COUNT)
    updated = current - LEARN_RATE * (first_hat / (jnp.sqrt(second_hat) + ADAM_EPS) + DECAY_RATE * current)
    return updated, moment_new, second_new


def kernel(
    owner_ref, local_ref, expand_ref, lengths_ref, taps_ref, table_ref, hidden_ref, grad_ref, wk_ref, wv_ref,
    out, row_grad,
    weights, tab, req_out, req_in, reply, fetched, slots, arrived, partial, give, take,
    spread, spread_t, serve, serve_t, docs, memory, keys, values, hidden, grad, gated, gnorm, cgrad, ngrad, stats,
    key_grad, value_grad, grads_t, halo_in, give_far, take_far,
    load_sem, in_sem, req_send, req_recv, rep_send, rep_recv, tz_send, tz_recv, wz_send, wz_recv,
    xy_send, xy_recv, core_send, core_recv, own_send, own_recv, halo_send, halo_recv, slot_send, slot_recv, ring_send, ring_recv,
    far_send, far_recv,
):
    here = Here()
    greeted = greet(here)
    loads = []
    for b in range(NB):
        src = wk_ref if b < NB // 2 else wv_ref
        loads.append(pltpu.make_async_copy(src.at[:, pl.ds(lanes(b).start, CB)], weights.at[b, here.z, here.core], load_sem.at[b]))
    inputs = [pltpu.make_async_copy(hidden_ref, hidden, in_sem.at[0]), pltpu.make_async_copy(grad_ref, grad.at[pl.ds(0, TOK)], in_sem.at[1])]
    for load in loads + inputs:
        load.start()
    for c in range(NC):
        tab[here.z, c, 0:R_DEV, :] = table_ref[:, c * CW : (c + 1) * CW].astype(BF16)
        tab[here.z, c, R_DEV:TROWS, :] = jnp.zeros((TROWS - R_DEV, CW), BF16)
    plan_slots(owner_ref, local_ref, expand_ref, spread, spread_t, req_out)
    greeted()

    spans = (pl.ds(0, NC // 2 + 1), pl.ds(NC // 2 + 1, NC // 2))
    tables = [
        Ring(here, lambda zz, span=span: tab.at[zz, span], tz_send.at[i], tz_recv.at[i], i) for i, span in enumerate(spans)
    ]
    blocks = [here.x, NB // 2 + here.y, NB // 2 - 1, NB - 1]
    pieces = [
        Ring(here, lambda zz, b=b: weights.at[b, zz, here.core], wz_send.at[i], wz_recv.at[i], i % 2)
        for i, b in enumerate(blocks)
    ]
    crosses = [
        Cross(here, "x", weights, 0, xy_send.at[0], xy_recv.at[0]),
        Cross(here, "y", weights, NB // 2, xy_send.at[1], xy_recv.at[1]),
    ]
    zeds = [here.zed(step) for step in (0, -1, 1, -2, 2, -3, 3, 4)]
    def to_partner(b, zz):
        ref = weights.at[b, zz, here.core]
        return remote(ref, ref, core_send.at[b, zz], core_recv.at[b, zz], here.partner())

    def own_to_partner():
        ref = weights.at[:, here.z, here.core]
        return remote(ref, ref, own_send, own_recv, here.partner())

    def from_partner(b):
        for i in range(1, Z):
            ref = weights.at[b, zeds[i], 1 - here.core]
            remote(ref, ref, core_send.at[b, zeds[i]], core_recv.at[b, zeds[i]], here.partner()).wait_recv()

    key_ring, value_ring, last_key, last_value = pieces
    x_cross, y_cross = crosses
    for ring in tables:
        ring.start(1)
    send_mates(here, req_out, req_in, req_send, req_recv)
    req_in[here.plane] = req_out[here.plane]
    for load in loads + inputs:
        load.wait()
    early = remote(
        grad.at[pl.ds(0, PAD)], grad.at[pl.ds(TOK, PAD)], halo_send.at[2], halo_recv.at[2], here.neighbour(-1)
    )
    early.start()
    own_to_partner().start()
    plan_docs(here, lengths_ref, docs)
    for ring in tables:
        ring.sent(1)
    key_ring.start(1)
    mates_arrived(here, req_in, req_recv)
    plan_serve(req_in, serve, serve_t)
    key_ring.sent(1)
    value_ring.start(1)
    for step in (1, 2, 3):
        for ring in tables:
            ring.arrived(step)
            ring.start(step + 1)
        for ring, cross in ((key_ring, x_cross), (value_ring, y_cross)):
            ring.arrived(step)
            ring.start(step + 1)
            for i in (2 * step - 1, 2 * step):
                cross.start(zeds[i], i)
                to_partner(cross.block(0), zeds[i]).start()
        if step > 1:
            for cross in crosses:
                for i in (2 * step - 3, 2 * step - 2):
                    cross.relay(zeds[i], i)
                    for side in (-1, 1):
                        to_partner(cross.block(side), zeds[i]).start()
    last_key.start(1)
    for ring in tables:
        ring.arrived(4)
    for c in range(NC):
        rows = nn(serve[...], tab[:, c].reshape(Z * TROWS, CW))
        reply[c] = rows.astype(BF16).reshape(PLANE, MSG, CW)
        fetched[c, here.plane] = reply[c, here.plane]
        send_mates(here, reply.at[c], fetched.at[c], rep_send.at[c], rep_recv.at[c])
    last_key.sent(1)
    last_value.start(1)
    for ring, cross in ((key_ring, x_cross), (value_ring, y_cross)):
        ring.arrived(4)
        cross.start(zeds[Z - 1], Z - 1)
        to_partner(cross.block(0), zeds[Z - 1]).start()

    def project(b):
        from_partner(b)
        return nn(memory[...], weights[b].reshape(E, CB))

    def project_key(b):
        keys[b] = project(b)

    def project_value(b):
        values[b] = project(NB // 2 + b)

    for step in (1, 2, 3):
        for ring, b in zip(pieces[2:], (NB // 2 - 1, NB - 1)):
            ring.arrived(step)
            ring.start(step + 1)
            for i in (2 * step - 1, 2 * step):
                to_partner(b, zeds[i]).start()
        if step == 1:
            for cross in crosses:
                for i in (Z - 3, Z - 2):
                    cross.relay(zeds[i], i)
                    for side in (-1, 1):
                        to_partner(cross.block(side), zeds[i]).start()
        else:
            for cross in crosses:
                for i in (2 * step - 3, 2 * step - 2):
                    cross.finish(zeds[i], i)
                    to_partner(cross.block(2), zeds[i]).start()
    for cross in crosses:
        cross.relay(zeds[Z - 1], Z - 1)
        for side in (-1, 1):
            to_partner(cross.block(side), zeds[Z - 1]).start()
    for c in range(NC):
        mates_arrived(here, fetched.at[c], rep_recv.at[c])
        memory[:, c * CW : (c + 1) * CW] = nn(spread[...], fetched[c].reshape(PLACES, CW)).astype(BF16)
    own_to_partner().wait_recv()
    project_key(here.x)
    project_value(here.y)
    for ring, b in zip(pieces[2:], (NB // 2 - 1, NB - 1)):
        ring.arrived(4)
        to_partner(b, zeds[Z - 1]).start()
    for i in range(5, Z):
        for cross in crosses:
            cross.finish(zeds[i], i)
            to_partner(cross.block(2), zeds[i]).start()
    for step in (-1, 1, 2):
        project_key(here.exx(step))
        project_value(here.wye(step))
    project_key(NB // 2 - 1)
    project_value(NB // 2 - 1)

    last = TOK // TILE - 1

    def halo(way):
        src = gated.at[pl.ds(last * TILE if way == 0 else 0, TILE)]
        return remote(src, halo_in.at[way], halo_send.at[way], halo_recv.at[way], here.neighbour(1 - 2 * way))

    def gate_step(t, carry):
        gate_tile(t, keys, values, hidden, gated, gnorm, stats)
        return carry

    def conv_step(t, carry):
        conv_tile(t, docs, taps_ref, gnorm, gated, grad, cgrad, out)
        return carry

    def grad_step(t, carry):
        grad_tile(t, docs, taps_ref, gnorm, cgrad, grad, keys, values, hidden, stats, ngrad, key_grad, value_grad)
        return carry

    gate_step(last, 0)
    halo(0).start()
    gate_step(0, 0)
    halo(1).start()
    lax.fori_loop(1, last, gate_step, 0)
    lax.fori_loop(1, last + 1, conv_step, 0)
    for way, start in ((0, 0), (1, PAD + TOK)):
        halo(way).wait_recv()
        total = jnp.zeros((TILE, CB), F32)
        for b in BLOCKS:
            rows = halo_in[way, :, lanes(b)].astype(F32)
            total = total + rows * rows
        scale = mean_scale(jnp.sum(total, axis=1, keepdims=True))
        for b in BLOCKS:
            gnorm[start : start + PAD, lanes(b)] = halo_in[way, :, lanes(b)].astype(F32) * scale
    early.wait_recv()
    conv_step(0, 0)
    conv_tile(last + 1, docs, taps_ref, gnorm, gated, grad, cgrad)
    lax.fori_loop(0, last + 1, grad_step, 0)

    for b in range(NB):
        source = key_grad if b < NB // 2 else value_grad
        grads_t[b] = source[:, lanes(b)].T
    def send_slots(c):
        first, stop = c * CW // (2 * WROWS), -(-(c + 1) * CW // (2 * WROWS))
        skip = c * CW - first * 2 * WROWS
        total = jnp.zeros((CW, TOK), F32)
        for b in range(NB):
            part = weights[b, first:stop].reshape((stop - first) * 2 * WROWS, CB)[skip : skip + CW]
            total = total + nn(part, grads_t[b])
        slots[c] = nt(spread_t[...], total.astype(BF16)).astype(BF16).reshape(PLANE, MSG, CW)
        arrived[c, here.plane] = slots[c, here.plane]
        if c >= AHEAD:
            mates_sent(here, slots.at[c - AHEAD], slot_send.at[c - AHEAD])
        send_mates(here, slots.at[c], arrived.at[c], slot_send.at[c], slot_recv.at[c])

    def hop(c, way, step):
        sign = 1 if way == 0 else -1
        return remote(
            give.at[c, way, step - 1], take.at[c, way, step - 1],
            ring_send.at[c, way, step - 1], ring_recv.at[c, way, step - 1], here.at_z(sign),
        )

    def length(c, way):
        return Z // 2 if way == c % 2 else Z // 2 - 1

    def advance(c, step):
        for way in range(2):
            final = length(c, way)
            if step > final:
                continue
            sign = 1 if way == 0 else -1
            mine = partial[c, here.zed(sign * (final - step + 1))]
            if step > 1:
                hop(c, way, step - 1).wait_recv()
                mine = mine + take[c, way, step - 2].astype(F32)
            give[c, way, step - 1] = mine.astype(BF16)
            hop(c, way, step).start()

    def far(c, step):
        place = c - RINGS
        return remote(
            give_far.at[place, here.zed(step)], take_far.at[place, step],
            far_send.at[place, step], far_recv.at[place, step], here.at_z(step),
        )

    def send_far(c):
        give_far[c - RINGS] = partial[c].astype(BF16)
        for step in range(1, Z):
            far(c, step).start()

    def finish(c):
        total = partial[c, here.z]
        if c < RINGS:
            for way in range(2):
                final = length(c, way)
                hop(c, way, final).wait_recv()
                total = total + take[c, way, final - 1].astype(F32)
        else:
            for step in range(1, Z):
                far(c, step).wait_recv()
                total = total + take_far[c - RINGS, step].astype(F32)
        row_grad[:, c * CW : (c + 1) * CW] = total[:R_DEV]

    for c in range(AHEAD):
        send_slots(c)
    for c in range(NC):
        if c + AHEAD < NC:
            send_slots(c + AHEAD)
        mates_arrived(here, arrived.at[c], slot_recv.at[c])
        partial[c] = nn(serve_t[...], arrived[c].reshape(PLACES, CW)).reshape(Z, TROWS, CW)
        if c < RINGS:
            advance(c, 1)
        else:
            send_far(c)
        for back in range(1, 4):
            if 0 <= c - back < RINGS:
                advance(c - back, back + 1)
    for step in range(2, Z // 2 + 1):
        for c in range(RINGS):
            if c + step > NC:
                advance(c, step)
    for c in range(NC):
        finish(c)

    value_ring.sent(1)
    last_value.sent(1)
    own_to_partner().wait_send()
    for b in range(NB):
        for i in range(1, Z):
            to_partner(b, zeds[i]).wait_send()
    for ring in tables + pieces:
        ring.drain()
    for i in range(1, Z):
        for cross in crosses:
            cross.drain(zeds[i], i)
    early.wait_send()
    for way in range(2):
        halo(way).wait_send()
    mates_sent(here, req_out, req_send)
    for c in range(NC):
        mates_sent(here, reply.at[c], rep_send.at[c])
        if c >= NC - AHEAD:
            mates_sent(here, slots.at[c], slot_send.at[c])
        if c < RINGS:
            for way in range(2):
                for step in range(1, length(c, way) + 1):
                    hop(c, way, step).wait_send()
        else:
            for step in range(1, Z):
                far(c, step).wait_send()


def on_device(
    hidden, grad_out, w_key, w_value, depthwise_weight, table, adam_m, adam_v,
    row_owner, row_local, expand_index, doc_lengths,
):
    vmem = pl.BlockSpec(memory_space=pltpu.VMEM)
    any_ = pl.BlockSpec(memory_space=pl.ANY)
    dma = pltpu.SemaphoreType.DMA
    rows = (NC, PLANE, MSG, CW)
    hops = (RINGS, 2, Z // 2)
    fars = (NC - RINGS, Z)
    memory_out, row_grad = pl.pallas_call(
        kernel,
        out_shape=(jax.ShapeDtypeStruct((TOK, D), BF16), jax.ShapeDtypeStruct((R_DEV, E), F32)),
        in_specs=[vmem] * 6 + [any_] * 4,
        out_specs=(vmem, vmem),
        scratch_shapes=[
            pltpu.VMEM((NB, Z, 2, WROWS, CB), BF16),
            pltpu.VMEM((Z, NC, TROWS, CW), BF16),
            pltpu.VMEM((PLANE, 1, 128), F32),
            pltpu.VMEM((PLANE, 1, 128), F32),
            pltpu.VMEM(rows, BF16),
            pltpu.VMEM(rows, BF16),
            pltpu.VMEM(rows, BF16),
            pltpu.VMEM(rows, BF16),
            pltpu.VMEM((NC, Z, TROWS, CW), F32),
            pltpu.VMEM(hops + (TROWS, CW), BF16),
            pltpu.VMEM(hops + (TROWS, CW), BF16),
            pltpu.VMEM((TOK, PLACES), BF16),
            pltpu.VMEM((PLACES, TOK), BF16),
            pltpu.VMEM((PLACES, Z * TROWS), BF16),
            pltpu.VMEM((Z * TROWS, PLACES), BF16),
            pltpu.VMEM((TOK + 3 * PAD, 128), F32),
            pltpu.VMEM((TOK, E), BF16),
            pltpu.VMEM((NB // 2, TOK, CB), F32),
            pltpu.VMEM((NB // 2, TOK, CB), F32),
            pltpu.VMEM((TOK, D), BF16),
            pltpu.VMEM((TOK + PAD, D), BF16),
            pltpu.VMEM((TOK, D), BF16),
            pltpu.VMEM((PAD + TOK + PAD, D), F32),
            pltpu.VMEM((TOK + PAD, D), F32),
            pltpu.VMEM((TILE, D), F32),
            pltpu.VMEM((len(STATS), TOK, 128), F32),
            pltpu.VMEM((TOK, D), BF16),
            pltpu.VMEM((TOK, D), BF16),
            pltpu.VMEM((NB, CB, TOK), BF16),
            pltpu.VMEM((2, TILE, D), BF16),
            pltpu.VMEM(fars + (TROWS, CW), BF16),
            pltpu.VMEM(fars + (TROWS, CW), BF16),
            dma((NB,)), dma((2,)), dma, dma, dma((NC,)), dma((NC,)),
            dma((2, 2, Z // 2)), dma((2, 2, Z // 2)), dma((4, 2, Z // 2)), dma((4, 2, Z // 2)),
            dma((2, 4, Z)), dma((2, 4, Z)), dma((NB, Z)), dma((NB, Z)), dma, dma,
            dma((3,)), dma((3,)), dma((NC,)), dma((NC,)), dma(hops), dma(hops), dma(fars), dma(fars),
        ],
        compiler_params=pltpu.CompilerParams(
            collective_id=0, has_side_effects=True, vmem_limit_bytes=56 * 1024 * 1024
        ),
        name="memory_branch",
    )(
        row_owner.reshape(1, U), row_local, expand_index[0].T, doc_lengths, depthwise_weight,
        table, hidden[0], grad_out[0], w_key, w_value,
    )
    new_table, new_moment, new_second = adamw(table, adam_m, adam_v, row_grad)
    return (memory_out[None], new_table, new_moment, new_second)


def solution(mesh):
    placed = (
        P("row", "col", None),
        P("row", "col", None),
        P("row", None),
        P("row", None),
        P(),
        P(("row", "col"), None),
        P(("row", "col"), None),
        P(("row", "col"), None),
        P("row", "col", None),
        P("row", "col"),
        P("row", "col", None),
        P("row", None),
    )
    return jax.shard_map(
        on_device,
        mesh=mesh,
        in_specs=placed,
        out_specs=(
            P("row", "col", None),
            P(("row", "col"), None),
            P(("row", "col"), None),
            P(("row", "col"), None),
        ),
        check_vma=False,
    )
```

```python
import jax
import jax.numpy as jnp
from jax import lax
from jax.experimental import pallas as pl
from jax.experimental.pallas import tpu as pltpu
from jax.sharding import PartitionSpec as P

DILATION_STEP = 3
NORM_EPS = 1e-06
BETA_ONE = 0.9
BETA_TWO = 0.95
ADAM_EPS = 1e-08
LEARN_RATE = 0.01
DECAY_RATE = 0.1
STEP_COUNT = 10.0

Z, X, Y = 8, 4, 4
PLANE = 2 * X * Y
D, E = 2560, 1280
TOK, U, R_DEV = 128, 144, 40
CW = 256
NC = E // CW
RINGS = 2
AHEAD = 2
TROWS = 48
MSG = 2 * Z
PLACES = PLANE * MSG
CB = 512
NB = 2 * D // CB
WROWS = 80
TILE = 16
PAD = 16
TAPS = 4

MESH = pl.DeviceIdType.MESH
F32, BF16, I32 = jnp.float32, jnp.bfloat16, jnp.int32


class Here:
    def __init__(self):
        self.row = lax.axis_index("row")
        self.col = lax.axis_index("col")
        self.z = self.row // 2
        self.core = self.row % 2
        self.x = self.col // Y
        self.y = self.col % Y
        self.plane = self.core * (X * Y) + self.col

    def mate(self, i):
        q = lax.rem(self.plane + i, PLANE)
        return q, (self.z * 2 + q // (X * Y), q % (X * Y))

    def zed(self, step):
        return lax.rem(self.z + step + Z, Z)

    def at_z(self, step):
        return (self.zed(step) * 2 + self.core, self.col)

    def exx(self, step):
        return lax.rem(self.x + step + X, X)

    def wye(self, step):
        return lax.rem(self.y + step + Y, Y)

    def at_x(self, step):
        return (self.row, self.exx(step) * Y + self.y)

    def at_y(self, step):
        return (self.row, self.x * Y + self.wye(step))

    def neighbour(self, step):
        return (self.row, lax.rem(self.col + step + X * Y, X * Y))

    def partner(self):
        return (self.z * 2 + 1 - self.core, self.col)


def remote(src, dst, send, recv, device):
    return pltpu.make_async_remote_copy(
        src_ref=src, dst_ref=dst, send_sem=send, recv_sem=recv, device_id=device, device_id_type=MESH
    )


def greet(here):
    barrier = pltpu.get_barrier_semaphore()

    def one(i, carry):
        _, device = here.mate(i)
        pl.semaphore_signal(barrier, inc=1, device_id=device, device_id_type=MESH)
        return carry

    lax.fori_loop(1, PLANE, one, 0)
    for step in range(1, Z):
        pl.semaphore_signal(barrier, inc=1, device_id=here.at_z(step), device_id_type=MESH)
    return lambda: pl.semaphore_wait(barrier, PLANE - 1 + Z - 1)


def iota(shape, dim):
    return lax.broadcasted_iota(I32, shape, dim)


def one_hot(mask):
    return jnp.where(mask, 1.0, 0.0).astype(BF16)


def nn(left, right):
    return jnp.dot(left, right, preferred_element_type=F32)


def tn(left, right):
    return lax.dot_general(left, right, (((0,), (0,)), ((), ())), preferred_element_type=F32)


def nt(left, right):
    return lax.dot_general(left, right, (((1,), (1,)), ((), ())), preferred_element_type=F32)


def column_of(row, size):
    eye = iota((size, size), 0) == iota((size, size), 1)
    return jnp.sum(jnp.where(eye, row, 0), axis=1, keepdims=True)


def plan_slots(owner_ref, local_ref, expand_ref, spread, spread_t, req_out):
    owner_r = owner_ref[...]
    owner_c = column_of(owner_r, U)
    local_c = column_of(local_ref[...], U)
    same = owner_c == owner_r
    earlier_c = same & (iota((U, U), 1) < iota((U, U), 0))
    earlier_r = same & (iota((U, U), 0) < iota((U, U), 1))
    k_c = (owner_c >> 5) * 2 + jnp.sum(jnp.where(earlier_c, 1, 0), axis=1, keepdims=True)
    k_r = (owner_r >> 5) * 2 + jnp.sum(jnp.where(earlier_r, 1, 0), axis=0, keepdims=True)
    mates = one_hot((owner_r & 31) == iota((PLANE, U), 0))
    wanted = jnp.where(k_c == iota((U, 128), 1), local_c + 1, 0).astype(F32).astype(BF16)
    request = nn(mates, wanted)
    for q in range(PLANE):
        req_out[q] = request[q : q + 1, :]
    expand = expand_ref[...]
    reads = jnp.zeros((U, TOK), F32)
    for lookup in range(2):
        reads = reads + jnp.where(expand[lookup : lookup + 1, :] == iota((U, TOK), 0), 1.0, 0.0)
    reads = reads.astype(BF16)
    places = one_hot((owner_c & 31) * MSG + k_c == iota((U, PLACES), 1))
    places_t = one_hot((owner_r & 31) * MSG + k_r == iota((PLACES, U), 0))
    spread[...] = tn(reads, places).astype(BF16)
    spread_t[...] = nn(places_t, reads).astype(BF16)


def plan_serve(req_in, serve, serve_t):
    asked = req_in[:, 0, :].astype(BF16)
    wide = nn(one_hot(iota((PLACES, PLANE), 0) // MSG == iota((PLACES, PLANE), 1)), asked)
    k = iota((PLACES, 128), 0) % MSG
    value = jnp.sum(jnp.where(k == iota((PLACES, 128), 1), wide, 0.0), axis=1, keepdims=True)
    zed = (iota((PLACES, 1), 0) % MSG) // 2
    target = jnp.where(value > 0.5, zed * TROWS + value.astype(I32) - 1, -1)
    serve[...] = one_hot(target == iota((PLACES, Z * TROWS), 1))
    tall = tn(asked, one_hot(iota((PLANE, PLACES), 1) // MSG == iota((PLANE, PLACES), 0)))
    k = iota((128, PLACES), 1) % MSG
    value = jnp.sum(jnp.where(k == iota((128, PLACES), 0), tall, 0.0), axis=0, keepdims=True)
    zed = (iota((1, PLACES), 1) % MSG) // 2
    target = jnp.where(value > 0.5, zed * TROWS + value.astype(I32) - 1, -1)
    serve_t[...] = one_hot(target == iota((Z * TROWS, PLACES), 0))


def plan_docs(here, lengths_ref, docs):
    n = lengths_ref.shape[1]
    length_c = column_of(lengths_ref[...], n)
    ends = jnp.sum(jnp.where(iota((n, n), 0) <= iota((n, n), 1), length_c, 0), axis=0, keepdims=True)
    rows = docs.shape[0]
    position = here.col * TOK - PAD + iota((rows, 1), 0)
    passed = (position >= ends) & (iota((rows, n), 1) < n - 1)
    doc = jnp.sum(jnp.where(passed, 1.0, 0.0), axis=1, keepdims=True)
    doc = jnp.where(position < 0, -1.0, jnp.where(position >= 16 * TOK, -2.0, doc))
    docs[...] = jnp.broadcast_to(doc, (rows, 128))


def send_mates(here, src, dst, send, recv):
    def one(i, carry):
        q, device = here.mate(i)
        remote(src.at[q], dst.at[here.plane], send, recv, device).start()
        return carry

    lax.fori_loop(1, PLANE, one, 0)


def mates_arrived(here, dst, recv):
    ref = dst.at[pl.ds(0, PLANE - 1)]
    pltpu.make_async_copy(ref, ref, recv).wait()


def mates_sent(here, src, send):
    ref = src.at[pl.ds(0, PLANE - 1)]
    pltpu.make_async_copy(ref, ref, send).wait()


class Ring:
    def __init__(self, here, block, send, recv, far):
        self.here, self.block, self.send, self.recv, self.far = here, block, send, recv, far

    def copy(self, way, step):
        sign = 1 if way == 0 else -1
        ref = self.block(self.here.zed(-sign * (step - 1)))
        return remote(ref, ref, self.send.at[way, step - 1], self.recv.at[way, step - 1], self.here.at_z(sign))

    def steps(self, way):
        return Z // 2 if way == self.far else Z // 2 - 1

    def start(self, step):
        for way in range(2):
            if step <= self.steps(way):
                self.copy(way, step).start()

    def arrived(self, step):
        got = []
        for way in range(2):
            if step <= self.steps(way):
                sign = 1 if way == 0 else -1
                ref = self.block(self.here.zed(-sign * step))
                remote(ref, ref, self.send.at[way, step - 1], self.recv.at[way, step - 1], self.here.at_z(-sign)).wait_recv()
                got.append(-sign * step)
        return got

    def drain(self):
        for way in range(2):
            for step in range(1, self.steps(way) + 1):
                self.copy(way, step).wait_send()


class Cross:
    def __init__(self, here, axis, weights, base, send, recv):
        self.here, self.weights, self.base, self.send, self.recv = here, weights, base, send, recv
        self.at = here.at_x if axis == "x" else here.at_y
        self.place = here.exx if axis == "x" else here.wye

    def copy(self, way, zz, i):
        sign = 1 if way % 2 == 0 else -1
        if way < 2:
            ref = self.weights.at[self.base + self.place(0), zz, self.here.core]
        else:
            ref = self.weights.at[self.base + self.place(-sign), zz, self.here.core, :, pl.ds((way - 2) * (CB // 2), CB // 2)]
        return remote(ref, ref, self.send.at[way, i], self.recv.at[way, i], self.at(sign))

    def got(self, way, zz, i):
        sign = 1 if way % 2 == 0 else -1
        if way < 2:
            ref = self.weights.at[self.base + self.place(-sign), zz, self.here.core]
        else:
            ref = self.weights.at[
                self.base + self.place(-2 * sign), zz, self.here.core, :, pl.ds((way - 2) * (CB // 2), CB // 2)
            ]
        return remote(ref, ref, self.send.at[way, i], self.recv.at[way, i], self.at(-sign))

    def block(self, step):
        return self.base + self.place(step)

    def start(self, zz, i):
        for way in (0, 1):
            self.copy(way, zz, i).start()

    def relay(self, zz, i):
        for way in (0, 1):
            self.got(way, zz, i).wait_recv()
            self.copy(way + 2, zz, i).start()

    def finish(self, zz, i):
        for way in (2, 3):
            self.got(way, zz, i).wait_recv()

    def drain(self, zz, i):
        for way in range(4):
            self.copy(way, zz, i).wait_send()


def lanes(b):
    return slice((b % (NB // 2)) * CB, (b % (NB // 2) + 1) * CB)


def row_tile(t):
    return pl.ds(pl.multiple_of(t * TILE, TILE), TILE)


def mean_scale(total):
    return lax.rsqrt(total / D + NORM_EPS)


BLOCKS = range(NB // 2)
STATS = ("key_scale", "hidden_scale", "score", "gate", "gated_scale")


def keep(stats, name, rows, value):
    stats[STATS.index(name), rows, :] = jnp.broadcast_to(value, (TILE, 128))


def kept(stats, name, rows):
    return wide(stats[STATS.index(name), rows, :])


def wide(value):
    return jnp.concatenate([value] * (CB // 128), axis=1)


def gate_tile(t, keys, values, hidden, gated, gnorm, stats):
    rows = row_tile(t)
    kk = jnp.zeros((TILE, CB), F32)
    hh, hk = kk, kk
    for b in BLOCKS:
        key = keys[b, rows, :]
        hid = hidden[rows, lanes(b)].astype(F32)
        kk, hh, hk = kk + key * key, hh + hid * hid, hk + hid * key
    key_scale = mean_scale(jnp.sum(kk, axis=1, keepdims=True))
    hidden_scale = mean_scale(jnp.sum(hh, axis=1, keepdims=True))
    score = jnp.sum(hk, axis=1, keepdims=True) * key_scale * hidden_scale
    gate = jax.nn.sigmoid(score / D**0.5)
    gg = jnp.zeros((TILE, CB), F32)
    for b in BLOCKS:
        rounded = (gate * values[b, rows, :]).astype(BF16)
        gated[rows, lanes(b)] = rounded
        gg = gg + rounded.astype(F32) * rounded.astype(F32)
    scale = mean_scale(jnp.sum(gg, axis=1, keepdims=True))
    own = pl.ds(pl.multiple_of(PAD + t * TILE, TILE), TILE)
    for b in BLOCKS:
        gnorm[own, lanes(b)] = gated[rows, lanes(b)].astype(F32) * scale
    for name, value in zip(STATS, (key_scale, hidden_scale, score, gate, scale)):
        keep(stats, name, rows, value)


def same_docs(docs, t, sign):
    window = docs[pl.ds(pl.multiple_of(t * TILE, TILE), 3 * TILE), :]
    center = window[TILE : 2 * TILE]
    shifted = [window[TILE + sign * DILATION_STEP * j : 2 * TILE + sign * DILATION_STEP * j] for j in range(TAPS)]
    return [wide(jnp.where(center == other, 1.0, 0.0)) for other in shifted]


def conv_tile(t, docs, taps, gnorm, gated, grad, cgrad, out=None):
    rows = row_tile(t)
    masks = same_docs(docs, t, -1)
    both = pl.ds(pl.multiple_of(t * TILE, TILE), 2 * TILE)
    for b in BLOCKS:
        window = gnorm[both, lanes(b)]
        conv = taps[0:1, lanes(b)] * window[TILE:]
        for j in range(1, TAPS):
            low = TILE - DILATION_STEP * j
            conv = conv + masks[j] * (taps[j : j + 1, lanes(b)] * window[low : low + TILE])
        sig = jax.nn.sigmoid(conv)
        if out is not None:
            out[rows, lanes(b)] = (conv * sig + gated[rows, lanes(b)].astype(F32)).astype(BF16)
        cgrad[rows, lanes(b)] = grad[rows, lanes(b)].astype(F32) * sig * (1.0 + conv * (1.0 - sig))


def grad_tile(t, docs, taps, gnorm, cgrad, grad, keys, values, hidden, stats, ngrad, key_grad, value_grad):
    rows = row_tile(t)
    masks = same_docs(docs, t, 1)
    both = pl.ds(pl.multiple_of(t * TILE, TILE), 2 * TILE)
    own = pl.ds(pl.multiple_of(PAD + t * TILE, TILE), TILE)
    dots = jnp.zeros((TILE, CB), F32)
    for b in BLOCKS:
        window = cgrad[both, lanes(b)]
        total = taps[0:1, lanes(b)] * window[:TILE]
        for j in range(1, TAPS):
            low = DILATION_STEP * j
            total = total + masks[j] * (taps[j : j + 1, lanes(b)] * window[low : low + TILE])
        ngrad[:, lanes(b)] = total
        dots = dots + gnorm[own, lanes(b)] * total
    mean = jnp.sum(dots, axis=1, keepdims=True) / D
    key_scale, hidden_scale, score, gate, scale = [kept(stats, name, rows) for name in STATS]
    dots = jnp.zeros((TILE, CB), F32)
    for b in BLOCKS:
        total = grad[rows, lanes(b)].astype(F32) + scale * (ngrad[:, lanes(b)] - gnorm[own, lanes(b)] * mean)
        value_grad[rows, lanes(b)] = (total * gate).astype(BF16)
        dots = dots + total * values[b, rows, :]
    score_grad = gate * (1.0 - gate) * jnp.sum(dots, axis=1, keepdims=True)
    front = key_scale * score_grad / D**0.5
    by_hidden, by_key = front * hidden_scale, front * (key_scale * score / D)
    for b in BLOCKS:
        target = by_hidden * hidden[rows, lanes(b)].astype(F32) - by_key * keys[b, rows, :]
        key_grad[rows, lanes(b)] = target.astype(BF16)


def adamw(current, moment, second, gradient):
    moment_new = BETA_ONE * moment + (1.0 - BETA_ONE) * gradient
    second_new = BETA_TWO * second + (1.0 - BETA_TWO) * gradient * gradient
    first_hat = moment_new / (1.0 - BETA_ONE**STEP_COUNT)
    second_hat = second_new / (1.0 - BETA_TWO**STEP_COUNT)
    updated = current - LEARN_RATE * (first_hat / (jnp.sqrt(second_hat) + ADAM_EPS) + DECAY_RATE * current)
    return updated, moment_new, second_new


def kernel(
    owner_ref, local_ref, expand_ref, lengths_ref, taps_ref, table_ref, hidden_ref, grad_ref, wk_ref, wv_ref,
    out, row_grad,
    weights, tab, req_out, req_in, reply, fetched, slots, arrived, partial, give, take,
    spread, spread_t, serve, serve_t, docs, memory, keys, values, hidden, grad, gated, gnorm, cgrad, ngrad, stats,
    key_grad, value_grad, grads_t, halo_in, give_far, take_far,
    load_sem, in_sem, req_send, req_recv, rep_send, rep_recv, tz_send, tz_recv, wz_send, wz_recv,
    xy_send, xy_recv, core_send, core_recv, own_send, own_recv, halo_send, halo_recv, slot_send, slot_recv, ring_send, ring_recv,
    far_send, far_recv,
):
    here = Here()
    greeted = greet(here)
    loads = []
    for b in range(NB):
        src = wk_ref if b < NB // 2 else wv_ref
        loads.append(pltpu.make_async_copy(src.at[:, pl.ds(lanes(b).start, CB)], weights.at[b, here.z, here.core], load_sem.at[b]))
    inputs = [pltpu.make_async_copy(hidden_ref, hidden, in_sem.at[0]), pltpu.make_async_copy(grad_ref, grad.at[pl.ds(0, TOK)], in_sem.at[1])]
    for load in loads + inputs:
        load.start()
    for c in range(NC):
        tab[here.z, c, 0:R_DEV, :] = table_ref[:, c * CW : (c + 1) * CW].astype(BF16)
        tab[here.z, c, R_DEV:TROWS, :] = jnp.zeros((TROWS - R_DEV, CW), BF16)
    plan_slots(owner_ref, local_ref, expand_ref, spread, spread_t, req_out)
    plan_docs(here, lengths_ref, docs)
    greeted()

    spans = (pl.ds(0, NC // 2 + 1), pl.ds(NC // 2 + 1, NC // 2))
    tables = [
        Ring(here, lambda zz, span=span: tab.at[zz, span], tz_send.at[i], tz_recv.at[i], i) for i, span in enumerate(spans)
    ]
    blocks = [here.x, NB // 2 + here.y, NB // 2 - 1, NB - 1]
    pieces = [
        Ring(here, lambda zz, b=b: weights.at[b, zz, here.core], wz_send.at[i], wz_recv.at[i], i % 2)
        for i, b in enumerate(blocks)
    ]
    crosses = [
        Cross(here, "x", weights, 0, xy_send.at[0], xy_recv.at[0]),
        Cross(here, "y", weights, NB // 2, xy_send.at[1], xy_recv.at[1]),
    ]
    zeds = [here.zed(step) for step in (0, -1, 1, -2, 2, -3, 3, 4)]
    def to_partner(b, zz):
        ref = weights.at[b, zz, here.core]
        return remote(ref, ref, core_send.at[b, zz], core_recv.at[b, zz], here.partner())

    def own_to_partner():
        ref = weights.at[:, here.z, here.core]
        return remote(ref, ref, own_send, own_recv, here.partner())

    def from_partner(b):
        for i in range(1, Z):
            ref = weights.at[b, zeds[i], 1 - here.core]
            remote(ref, ref, core_send.at[b, zeds[i]], core_recv.at[b, zeds[i]], here.partner()).wait_recv()

    key_ring, value_ring = pieces[:2]
    x_cross, y_cross = crosses
    for load in loads + inputs:
        load.wait()
    for ring in pieces[:2]:
        ring.start(1)
    for ring in tables:
        ring.start(1)
    send_mates(here, req_out, req_in, req_send, req_recv)
    req_in[here.plane] = req_out[here.plane]
    early = remote(
        grad.at[pl.ds(0, PAD)], grad.at[pl.ds(TOK, PAD)], halo_send.at[2], halo_recv.at[2], here.neighbour(-1)
    )
    early.start()
    own_to_partner().start()
    mates_arrived(here, req_in, req_recv)
    plan_serve(req_in, serve, serve_t)
    for step in (1, 2, 3):
        for ring, cross in ((key_ring, x_cross), (value_ring, y_cross)):
            ring.arrived(step)
            ring.start(step + 1)
            for i in (2 * step - 1, 2 * step):
                cross.start(zeds[i], i)
                to_partner(cross.block(0), zeds[i]).start()
        for ring in tables:
            ring.arrived(step)
            ring.start(step + 1)
        if step > 1:
            for cross in crosses:
                for i in (2 * step - 3, 2 * step - 2):
                    cross.relay(zeds[i], i)
                    for side in (-1, 1):
                        to_partner(cross.block(side), zeds[i]).start()
    for ring in pieces[2:]:
        ring.start(1)
    for ring in tables:
        ring.arrived(4)
    for c in range(NC):
        rows = nn(serve[...], tab[:, c].reshape(Z * TROWS, CW))
        reply[c] = rows.astype(BF16).reshape(PLANE, MSG, CW)
        fetched[c, here.plane] = reply[c, here.plane]
        send_mates(here, reply.at[c], fetched.at[c], rep_send.at[c], rep_recv.at[c])
    for ring, cross in ((key_ring, x_cross), (value_ring, y_cross)):
        ring.arrived(4)
        cross.start(zeds[Z - 1], Z - 1)
        to_partner(cross.block(0), zeds[Z - 1]).start()

    def project(b):
        from_partner(b)
        return nn(memory[...], weights[b].reshape(E, CB))

    def project_key(b):
        keys[b] = project(b)

    def project_value(b):
        values[b] = project(NB // 2 + b)

    for step in (1, 2, 3):
        for ring, b in zip(pieces[2:], (NB // 2 - 1, NB - 1)):
            ring.arrived(step)
            ring.start(step + 1)
            for i in (2 * step - 1, 2 * step):
                to_partner(b, zeds[i]).start()
        if step == 1:
            for cross in crosses:
                for i in (Z - 3, Z - 2):
                    cross.relay(zeds[i], i)
                    for side in (-1, 1):
                        to_partner(cross.block(side), zeds[i]).start()
        else:
            for cross in crosses:
                for i in (2 * step - 3, 2 * step - 2):
                    cross.finish(zeds[i], i)
                    to_partner(cross.block(2), zeds[i]).start()
    for cross in crosses:
        cross.relay(zeds[Z - 1], Z - 1)
        for side in (-1, 1):
            to_partner(cross.block(side), zeds[Z - 1]).start()
    for c in range(NC):
        mates_arrived(here, fetched.at[c], rep_recv.at[c])
        memory[:, c * CW : (c + 1) * CW] = nn(spread[...], fetched[c].reshape(PLACES, CW)).astype(BF16)
    own_to_partner().wait_recv()
    project_key(here.x)
    project_value(here.y)
    for ring, b in zip(pieces[2:], (NB // 2 - 1, NB - 1)):
        ring.arrived(4)
        to_partner(b, zeds[Z - 1]).start()
    for i in range(5, Z):
        for cross in crosses:
            cross.finish(zeds[i], i)
            to_partner(cross.block(2), zeds[i]).start()
    for step in (-1, 1, 2):
        project_key(here.exx(step))
        project_value(here.wye(step))
    project_key(NB // 2 - 1)
    project_value(NB // 2 - 1)

    last = TOK // TILE - 1

    def halo(way):
        src = gated.at[pl.ds(last * TILE if way == 0 else 0, TILE)]
        return remote(src, halo_in.at[way], halo_send.at[way], halo_recv.at[way], here.neighbour(1 - 2 * way))

    def gate_step(t, carry):
        gate_tile(t, keys, values, hidden, gated, gnorm, stats)
        return carry

    def conv_step(t, carry):
        conv_tile(t, docs, taps_ref, gnorm, gated, grad, cgrad, out)
        return carry

    def grad_step(t, carry):
        grad_tile(t, docs, taps_ref, gnorm, cgrad, grad, keys, values, hidden, stats, ngrad, key_grad, value_grad)
        return carry

    gate_step(last, 0)
    halo(0).start()
    gate_step(0, 0)
    halo(1).start()
    lax.fori_loop(1, last, gate_step, 0)
    lax.fori_loop(1, last + 1, conv_step, 0)
    for way, start in ((0, 0), (1, PAD + TOK)):
        halo(way).wait_recv()
        total = jnp.zeros((TILE, CB), F32)
        for b in BLOCKS:
            rows = halo_in[way, :, lanes(b)].astype(F32)
            total = total + rows * rows
        scale = mean_scale(jnp.sum(total, axis=1, keepdims=True))
        for b in BLOCKS:
            gnorm[start : start + PAD, lanes(b)] = halo_in[way, :, lanes(b)].astype(F32) * scale
    early.wait_recv()
    conv_step(0, 0)
    conv_tile(last + 1, docs, taps_ref, gnorm, gated, grad, cgrad)
    lax.fori_loop(0, last + 1, grad_step, 0)

    for b in range(NB):
        source = key_grad if b < NB // 2 else value_grad
        grads_t[b] = source[:, lanes(b)].T
    def send_slots(c):
        first, stop = c * CW // (2 * WROWS), -(-(c + 1) * CW // (2 * WROWS))
        skip = c * CW - first * 2 * WROWS
        total = jnp.zeros((CW, TOK), F32)
        for b in range(NB):
            part = weights[b, first:stop].reshape((stop - first) * 2 * WROWS, CB)[skip : skip + CW]
            total = total + nn(part, grads_t[b])
        slots[c] = nt(spread_t[...], total.astype(BF16)).astype(BF16).reshape(PLANE, MSG, CW)
        arrived[c, here.plane] = slots[c, here.plane]
        if c >= AHEAD:
            mates_sent(here, slots.at[c - AHEAD], slot_send.at[c - AHEAD])
        send_mates(here, slots.at[c], arrived.at[c], slot_send.at[c], slot_recv.at[c])

    def hop(c, way, step):
        sign = 1 if way == 0 else -1
        return remote(
            give.at[c, way, step - 1], take.at[c, way, step - 1],
            ring_send.at[c, way, step - 1], ring_recv.at[c, way, step - 1], here.at_z(sign),
        )

    def length(c, way):
        return Z // 2 if way == c % 2 else Z // 2 - 1

    def advance(c, step):
        for way in range(2):
            final = length(c, way)
            if step > final:
                continue
            sign = 1 if way == 0 else -1
            mine = partial[c, here.zed(sign * (final - step + 1))]
            if step > 1:
                hop(c, way, step - 1).wait_recv()
                mine = mine + take[c, way, step - 2].astype(F32)
            give[c, way, step - 1] = mine.astype(BF16)
            hop(c, way, step).start()

    def far(c, step):
        place = c - RINGS
        return remote(
            give_far.at[place, here.zed(step)], take_far.at[place, step],
            far_send.at[place, step], far_recv.at[place, step], here.at_z(step),
        )

    def send_far(c):
        give_far[c - RINGS] = partial[c].astype(BF16)
        for step in range(1, Z):
            far(c, step).start()

    def finish(c):
        total = partial[c, here.z]
        if c < RINGS:
            for way in range(2):
                final = length(c, way)
                hop(c, way, final).wait_recv()
                total = total + take[c, way, final - 1].astype(F32)
        else:
            for step in range(1, Z):
                far(c, step).wait_recv()
                total = total + take_far[c - RINGS, step].astype(F32)
        row_grad[:, c * CW : (c + 1) * CW] = total[:R_DEV]

    for c in range(AHEAD):
        send_slots(c)
    for c in range(NC):
        if c + AHEAD < NC:
            send_slots(c + AHEAD)
        mates_arrived(here, arrived.at[c], slot_recv.at[c])
        partial[c] = nn(serve_t[...], arrived[c].reshape(PLACES, CW)).reshape(Z, TROWS, CW)
        if c < RINGS:
            advance(c, 1)
        else:
            send_far(c)
        for back in range(1, 4):
            if 0 <= c - back < RINGS:
                advance(c - back, back + 1)
    for step in range(2, Z // 2 + 1):
        for c in range(RINGS):
            if c + step > NC:
                advance(c, step)
    for c in range(NC):
        finish(c)

    own_to_partner().wait_send()
    for b in range(NB):
        for i in range(1, Z):
            to_partner(b, zeds[i]).wait_send()
    for ring in tables + pieces:
        ring.drain()
    for i in range(1, Z):
        for cross in crosses:
            cross.drain(zeds[i], i)
    early.wait_send()
    for way in range(2):
        halo(way).wait_send()
    mates_sent(here, req_out, req_send)
    for c in range(NC):
        mates_sent(here, reply.at[c], rep_send.at[c])
        if c >= NC - AHEAD:
            mates_sent(here, slots.at[c], slot_send.at[c])
        if c < RINGS:
            for way in range(2):
                for step in range(1, length(c, way) + 1):
                    hop(c, way, step).wait_send()
        else:
            for step in range(1, Z):
                far(c, step).wait_send()


def on_device(
    hidden, grad_out, w_key, w_value, depthwise_weight, table, adam_m, adam_v,
    row_owner, row_local, expand_index, doc_lengths,
):
    vmem = pl.BlockSpec(memory_space=pltpu.VMEM)
    any_ = pl.BlockSpec(memory_space=pl.ANY)
    dma = pltpu.SemaphoreType.DMA
    rows = (NC, PLANE, MSG, CW)
    hops = (RINGS, 2, Z // 2)
    fars = (NC - RINGS, Z)
    memory_out, row_grad = pl.pallas_call(
        kernel,
        out_shape=(jax.ShapeDtypeStruct((TOK, D), BF16), jax.ShapeDtypeStruct((R_DEV, E), F32)),
        in_specs=[vmem] * 6 + [any_] * 4,
        out_specs=(vmem, vmem),
        scratch_shapes=[
            pltpu.VMEM((NB, Z, 2, WROWS, CB), BF16),
            pltpu.VMEM((Z, NC, TROWS, CW), BF16),
            pltpu.VMEM((PLANE, 1, 128), F32),
            pltpu.VMEM((PLANE, 1, 128), F32),
            pltpu.VMEM(rows, BF16),
            pltpu.VMEM(rows, BF16),
            pltpu.VMEM(rows, BF16),
            pltpu.VMEM(rows, BF16),
            pltpu.VMEM((NC, Z, TROWS, CW), F32),
            pltpu.VMEM(hops + (TROWS, CW), BF16),
            pltpu.VMEM(hops + (TROWS, CW), BF16),
            pltpu.VMEM((TOK, PLACES), BF16),
            pltpu.VMEM((PLACES, TOK), BF16),
            pltpu.VMEM((PLACES, Z * TROWS), BF16),
            pltpu.VMEM((Z * TROWS, PLACES), BF16),
            pltpu.VMEM((TOK + 3 * PAD, 128), F32),
            pltpu.VMEM((TOK, E), BF16),
            pltpu.VMEM((NB // 2, TOK, CB), F32),
            pltpu.VMEM((NB // 2, TOK, CB), F32),
            pltpu.VMEM((TOK, D), BF16),
            pltpu.VMEM((TOK + PAD, D), BF16),
            pltpu.VMEM((TOK, D), BF16),
            pltpu.VMEM((PAD + TOK + PAD, D), F32),
            pltpu.VMEM((TOK + PAD, D), F32),
            pltpu.VMEM((TILE, D), F32),
            pltpu.VMEM((len(STATS), TOK, 128), F32),
            pltpu.VMEM((TOK, D), BF16),
            pltpu.VMEM((TOK, D), BF16),
            pltpu.VMEM((NB, CB, TOK), BF16),
            pltpu.VMEM((2, TILE, D), BF16),
            pltpu.VMEM(fars + (TROWS, CW), BF16),
            pltpu.VMEM(fars + (TROWS, CW), BF16),
            dma((NB,)), dma((2,)), dma, dma, dma((NC,)), dma((NC,)),
            dma((2, 2, Z // 2)), dma((2, 2, Z // 2)), dma((4, 2, Z // 2)), dma((4, 2, Z // 2)),
            dma((2, 4, Z)), dma((2, 4, Z)), dma((NB, Z)), dma((NB, Z)), dma, dma,
            dma((3,)), dma((3,)), dma((NC,)), dma((NC,)), dma(hops), dma(hops), dma(fars), dma(fars),
        ],
        compiler_params=pltpu.CompilerParams(
            collective_id=0, has_side_effects=True, vmem_limit_bytes=56 * 1024 * 1024
        ),
        name="memory_branch",
    )(
        row_owner.reshape(1, U), row_local, expand_index[0].T, doc_lengths, depthwise_weight,
        table, hidden[0], grad_out[0], w_key, w_value,
    )
    new_table, new_moment, new_second = adamw(table, adam_m, adam_v, row_grad)
    return (memory_out[None], new_table, new_moment, new_second)


def solution(mesh):
    placed = (
        P("row", "col", None),
        P("row", "col", None),
        P("row", None),
        P("row", None),
        P(),
        P(("row", "col"), None),
        P(("row", "col"), None),
        P(("row", "col"), None),
        P("row", "col", None),
        P("row", "col"),
        P("row", "col", None),
        P("row", None),
    )
    return jax.shard_map(
        on_device,
        mesh=mesh,
        in_specs=placed,
        out_specs=(
            P("row", "col", None),
            P(("row", "col"), None),
            P(("row", "col"), None),
            P(("row", "col"), None),
        ),
        check_vma=False,
    )
```

```python
import jax
import jax.numpy as jnp
from jax import lax
from jax.experimental import pallas as pl
from jax.experimental.pallas import tpu as pltpu
from jax.sharding import PartitionSpec as P

DILATION_STEP = 3
NORM_EPS = 1e-06
BETA_ONE = 0.9
BETA_TWO = 0.95
ADAM_EPS = 1e-08
LEARN_RATE = 0.01
DECAY_RATE = 0.1
STEP_COUNT = 10.0

Z, X, Y = 8, 4, 4
PLANE = 2 * X * Y
D, E = 2560, 1280
TOK, U, R_DEV = 128, 144, 40
CW = 256
NC = E // CW
RINGS = 2
AHEAD = 2
TROWS = 48
MSG = 2 * Z
PLACES = PLANE * MSG
CB = 512
NB = 2 * D // CB
WROWS = 80
TILE = 16
PAD = 16
TAPS = 4

MESH = pl.DeviceIdType.MESH
F32, BF16, I32 = jnp.float32, jnp.bfloat16, jnp.int32


class Here:
    def __init__(self):
        self.row = lax.axis_index("row")
        self.col = lax.axis_index("col")
        self.z = self.row // 2
        self.core = self.row % 2
        self.x = self.col // Y
        self.y = self.col % Y
        self.plane = self.core * (X * Y) + self.col

    def mate(self, i):
        q = lax.rem(self.plane + i, PLANE)
        return q, (self.z * 2 + q // (X * Y), q % (X * Y))

    def zed(self, step):
        return lax.rem(self.z + step + Z, Z)

    def at_z(self, step):
        return (self.zed(step) * 2 + self.core, self.col)

    def exx(self, step):
        return lax.rem(self.x + step + X, X)

    def wye(self, step):
        return lax.rem(self.y + step + Y, Y)

    def at_x(self, step):
        return (self.row, self.exx(step) * Y + self.y)

    def at_y(self, step):
        return (self.row, self.x * Y + self.wye(step))

    def neighbour(self, step):
        return (self.row, lax.rem(self.col + step + X * Y, X * Y))

    def partner(self):
        return (self.z * 2 + 1 - self.core, self.col)


def remote(src, dst, send, recv, device):
    return pltpu.make_async_remote_copy(
        src_ref=src, dst_ref=dst, send_sem=send, recv_sem=recv, device_id=device, device_id_type=MESH
    )


def greet(here):
    barrier = pltpu.get_barrier_semaphore()

    def one(i, carry):
        _, device = here.mate(i)
        pl.semaphore_signal(barrier, inc=1, device_id=device, device_id_type=MESH)
        return carry

    lax.fori_loop(1, PLANE, one, 0)
    for step in range(1, Z):
        pl.semaphore_signal(barrier, inc=1, device_id=here.at_z(step), device_id_type=MESH)
    return lambda: pl.semaphore_wait(barrier, PLANE - 1 + Z - 1)


def iota(shape, dim):
    return lax.broadcasted_iota(I32, shape, dim)


def one_hot(mask):
    return jnp.where(mask, 1.0, 0.0).astype(BF16)


def nn(left, right):
    return jnp.dot(left, right, preferred_element_type=F32)


def tn(left, right):
    return lax.dot_general(left, right, (((0,), (0,)), ((), ())), preferred_element_type=F32)


def nt(left, right):
    return lax.dot_general(left, right, (((1,), (1,)), ((), ())), preferred_element_type=F32)


def column_of(row, size):
    eye = iota((size, size), 0) == iota((size, size), 1)
    return jnp.sum(jnp.where(eye, row, 0), axis=1, keepdims=True)


def plan_slots(owner_ref, local_ref, expand_ref, spread, spread_t, req_out):
    owner_r = owner_ref[...]
    owner_c = column_of(owner_r, U)
    local_c = column_of(local_ref[...], U)
    same = owner_c == owner_r
    earlier_c = same & (iota((U, U), 1) < iota((U, U), 0))
    earlier_r = same & (iota((U, U), 0) < iota((U, U), 1))
    k_c = (owner_c >> 5) * 2 + jnp.sum(jnp.where(earlier_c, 1, 0), axis=1, keepdims=True)
    k_r = (owner_r >> 5) * 2 + jnp.sum(jnp.where(earlier_r, 1, 0), axis=0, keepdims=True)
    mates = one_hot((owner_r & 31) == iota((PLANE, U), 0))
    wanted = jnp.where(k_c == iota((U, 128), 1), local_c + 1, 0).astype(F32).astype(BF16)
    request = nn(mates, wanted)
    for q in range(PLANE):
        req_out[q] = request[q : q + 1, :]
    expand = expand_ref[...]
    reads = jnp.zeros((U, TOK), F32)
    for lookup in range(2):
        reads = reads + jnp.where(expand[lookup : lookup + 1, :] == iota((U, TOK), 0), 1.0, 0.0)
    reads = reads.astype(BF16)
    places = one_hot((owner_c & 31) * MSG + k_c == iota((U, PLACES), 1))
    places_t = one_hot((owner_r & 31) * MSG + k_r == iota((PLACES, U), 0))
    spread[...] = tn(reads, places).astype(BF16)
    spread_t[...] = nn(places_t, reads).astype(BF16)


def plan_serve(req_in, serve, serve_t):
    asked = req_in[:, 0, :].astype(BF16)
    wide = nn(one_hot(iota((PLACES, PLANE), 0) // MSG == iota((PLACES, PLANE), 1)), asked)
    k = iota((PLACES, 128), 0) % MSG
    value = jnp.sum(jnp.where(k == iota((PLACES, 128), 1), wide, 0.0), axis=1, keepdims=True)
    zed = (iota((PLACES, 1), 0) % MSG) // 2
    target = jnp.where(value > 0.5, zed * TROWS + value.astype(I32) - 1, -1)
    serve[...] = one_hot(target == iota((PLACES, Z * TROWS), 1))
    tall = tn(asked, one_hot(iota((PLANE, PLACES), 1) // MSG == iota((PLANE, PLACES), 0)))
    k = iota((128, PLACES), 1) % MSG
    value = jnp.sum(jnp.where(k == iota((128, PLACES), 0), tall, 0.0), axis=0, keepdims=True)
    zed = (iota((1, PLACES), 1) % MSG) // 2
    target = jnp.where(value > 0.5, zed * TROWS + value.astype(I32) - 1, -1)
    serve_t[...] = one_hot(target == iota((Z * TROWS, PLACES), 0))


def plan_docs(here, lengths_ref, docs):
    n = lengths_ref.shape[1]
    length_c = column_of(lengths_ref[...], n)
    ends = jnp.sum(jnp.where(iota((n, n), 0) <= iota((n, n), 1), length_c, 0), axis=0, keepdims=True)
    rows = docs.shape[0]
    position = here.col * TOK - PAD + iota((rows, 1), 0)
    passed = (position >= ends) & (iota((rows, n), 1) < n - 1)
    doc = jnp.sum(jnp.where(passed, 1.0, 0.0), axis=1, keepdims=True)
    doc = jnp.where(position < 0, -1.0, jnp.where(position >= 16 * TOK, -2.0, doc))
    docs[...] = jnp.broadcast_to(doc, (rows, 128))


def send_mates(here, src, dst, send, recv):
    def one(i, carry):
        q, device = here.mate(i)
        remote(src.at[q], dst.at[here.plane], send, recv, device).start()
        return carry

    lax.fori_loop(1, PLANE, one, 0)


def mates_arrived(here, dst, recv):
    ref = dst.at[pl.ds(0, PLANE - 1)]
    pltpu.make_async_copy(ref, ref, recv).wait()


def mates_sent(here, src, send):
    ref = src.at[pl.ds(0, PLANE - 1)]
    pltpu.make_async_copy(ref, ref, send).wait()


class Ring:
    def __init__(self, here, block, send, recv, far):
        self.here, self.block, self.send, self.recv, self.far = here, block, send, recv, far

    def copy(self, way, step):
        sign = 1 if way == 0 else -1
        ref = self.block(self.here.zed(-sign * (step - 1)))
        return remote(ref, ref, self.send.at[way, step - 1], self.recv.at[way, step - 1], self.here.at_z(sign))

    def steps(self, way):
        return Z // 2 if way == self.far else Z // 2 - 1

    def start(self, step):
        for way in range(2):
            if step <= self.steps(way):
                self.copy(way, step).start()

    def arrived(self, step):
        got = []
        for way in range(2):
            if step <= self.steps(way):
                sign = 1 if way == 0 else -1
                ref = self.block(self.here.zed(-sign * step))
                remote(ref, ref, self.send.at[way, step - 1], self.recv.at[way, step - 1], self.here.at_z(-sign)).wait_recv()
                got.append(-sign * step)
        return got

    def drain(self):
        for way in range(2):
            for step in range(1, self.steps(way) + 1):
                self.copy(way, step).wait_send()


class Cross:
    def __init__(self, here, axis, weights, base, send, recv):
        self.here, self.weights, self.base, self.send, self.recv = here, weights, base, send, recv
        self.at = here.at_x if axis == "x" else here.at_y
        self.place = here.exx if axis == "x" else here.wye

    def copy(self, way, zz, i):
        sign = 1 if way % 2 == 0 else -1
        if way < 2:
            ref = self.weights.at[self.base + self.place(0), zz, self.here.core]
        else:
            ref = self.weights.at[self.base + self.place(-sign), zz, self.here.core, :, pl.ds((way - 2) * (CB // 2), CB // 2)]
        return remote(ref, ref, self.send.at[way, i], self.recv.at[way, i], self.at(sign))

    def got(self, way, zz, i):
        sign = 1 if way % 2 == 0 else -1
        if way < 2:
            ref = self.weights.at[self.base + self.place(-sign), zz, self.here.core]
        else:
            ref = self.weights.at[
                self.base + self.place(-2 * sign), zz, self.here.core, :, pl.ds((way - 2) * (CB // 2), CB // 2)
            ]
        return remote(ref, ref, self.send.at[way, i], self.recv.at[way, i], self.at(-sign))

    def block(self, step):
        return self.base + self.place(step)

    def start(self, zz, i):
        for way in (0, 1):
            self.copy(way, zz, i).start()

    def relay(self, zz, i):
        for way in (0, 1):
            self.got(way, zz, i).wait_recv()
            self.copy(way + 2, zz, i).start()

    def finish(self, zz, i):
        for way in (2, 3):
            self.got(way, zz, i).wait_recv()

    def drain(self, zz, i):
        for way in range(4):
            self.copy(way, zz, i).wait_send()


def lanes(b):
    return slice((b % (NB // 2)) * CB, (b % (NB // 2) + 1) * CB)


def row_tile(t):
    return pl.ds(pl.multiple_of(t * TILE, TILE), TILE)


def mean_scale(total):
    return lax.rsqrt(total / D + NORM_EPS)


BLOCKS = range(NB // 2)
STATS = ("key_scale", "hidden_scale", "score", "gate", "gated_scale")


def keep(stats, name, rows, value):
    stats[STATS.index(name), rows, :] = jnp.broadcast_to(value, (TILE, 128))


def kept(stats, name, rows):
    return wide(stats[STATS.index(name), rows, :])


def wide(value):
    return jnp.concatenate([value] * (CB // 128), axis=1)


def gate_tile(t, keys, values, hidden, gated, gnorm, stats):
    rows = row_tile(t)
    kk = jnp.zeros((TILE, CB), F32)
    hh, hk = kk, kk
    for b in BLOCKS:
        key = keys[b, rows, :]
        hid = hidden[rows, lanes(b)].astype(F32)
        kk, hh, hk = kk + key * key, hh + hid * hid, hk + hid * key
    key_scale = mean_scale(jnp.sum(kk, axis=1, keepdims=True))
    hidden_scale = mean_scale(jnp.sum(hh, axis=1, keepdims=True))
    score = jnp.sum(hk, axis=1, keepdims=True) * key_scale * hidden_scale
    gate = jax.nn.sigmoid(score / D**0.5)
    gg = jnp.zeros((TILE, CB), F32)
    for b in BLOCKS:
        rounded = (gate * values[b, rows, :]).astype(BF16)
        gated[rows, lanes(b)] = rounded
        gg = gg + rounded.astype(F32) * rounded.astype(F32)
    scale = mean_scale(jnp.sum(gg, axis=1, keepdims=True))
    own = pl.ds(pl.multiple_of(PAD + t * TILE, TILE), TILE)
    for b in BLOCKS:
        gnorm[own, lanes(b)] = gated[rows, lanes(b)].astype(F32) * scale
    for name, value in zip(STATS, (key_scale, hidden_scale, score, gate, scale)):
        keep(stats, name, rows, value)


def same_docs(docs, t, sign):
    window = docs[pl.ds(pl.multiple_of(t * TILE, TILE), 3 * TILE), :]
    center = window[TILE : 2 * TILE]
    shifted = [window[TILE + sign * DILATION_STEP * j : 2 * TILE + sign * DILATION_STEP * j] for j in range(TAPS)]
    return [wide(jnp.where(center == other, 1.0, 0.0)) for other in shifted]


def conv_tile(t, docs, taps, gnorm, gated, grad, cgrad, out=None):
    rows = row_tile(t)
    masks = same_docs(docs, t, -1)
    both = pl.ds(pl.multiple_of(t * TILE, TILE), 2 * TILE)
    for b in BLOCKS:
        window = gnorm[both, lanes(b)]
        conv = taps[0:1, lanes(b)] * window[TILE:]
        for j in range(1, TAPS):
            low = TILE - DILATION_STEP * j
            conv = conv + masks[j] * (taps[j : j + 1, lanes(b)] * window[low : low + TILE])
        sig = jax.nn.sigmoid(conv)
        if out is not None:
            out[rows, lanes(b)] = (conv * sig + gated[rows, lanes(b)].astype(F32)).astype(BF16)
        cgrad[rows, lanes(b)] = grad[rows, lanes(b)].astype(F32) * sig * (1.0 + conv * (1.0 - sig))


def grad_tile(t, docs, taps, gnorm, cgrad, grad, keys, values, hidden, stats, ngrad, key_grad, value_grad):
    rows = row_tile(t)
    masks = same_docs(docs, t, 1)
    both = pl.ds(pl.multiple_of(t * TILE, TILE), 2 * TILE)
    own = pl.ds(pl.multiple_of(PAD + t * TILE, TILE), TILE)
    dots = jnp.zeros((TILE, CB), F32)
    for b in BLOCKS:
        window = cgrad[both, lanes(b)]
        total = taps[0:1, lanes(b)] * window[:TILE]
        for j in range(1, TAPS):
            low = DILATION_STEP * j
            total = total + masks[j] * (taps[j : j + 1, lanes(b)] * window[low : low + TILE])
        ngrad[:, lanes(b)] = total
        dots = dots + gnorm[own, lanes(b)] * total
    mean = jnp.sum(dots, axis=1, keepdims=True) / D
    key_scale, hidden_scale, score, gate, scale = [kept(stats, name, rows) for name in STATS]
    dots = jnp.zeros((TILE, CB), F32)
    for b in BLOCKS:
        total = grad[rows, lanes(b)].astype(F32) + scale * (ngrad[:, lanes(b)] - gnorm[own, lanes(b)] * mean)
        value_grad[rows, lanes(b)] = (total * gate).astype(BF16)
        dots = dots + total * values[b, rows, :]
    score_grad = gate * (1.0 - gate) * jnp.sum(dots, axis=1, keepdims=True)
    front = key_scale * score_grad / D**0.5
    by_hidden, by_key = front * hidden_scale, front * (key_scale * score / D)
    for b in BLOCKS:
        target = by_hidden * hidden[rows, lanes(b)].astype(F32) - by_key * keys[b, rows, :]
        key_grad[rows, lanes(b)] = target.astype(BF16)


def adamw(current, moment, second, gradient):
    moment_new = BETA_ONE * moment + (1.0 - BETA_ONE) * gradient
    second_new = BETA_TWO * second + (1.0 - BETA_TWO) * gradient * gradient
    first_hat = moment_new / (1.0 - BETA_ONE**STEP_COUNT)
    second_hat = second_new / (1.0 - BETA_TWO**STEP_COUNT)
    updated = current - LEARN_RATE * (first_hat / (jnp.sqrt(second_hat) + ADAM_EPS) + DECAY_RATE * current)
    return updated, moment_new, second_new


def kernel(
    owner_ref, local_ref, expand_ref, lengths_ref, taps_ref, table_ref, hidden_ref, grad_ref, wk_ref, wv_ref,
    out, row_grad,
    weights, tab, req_out, req_in, reply, fetched, slots, arrived, partial, give, take,
    spread, spread_t, serve, serve_t, docs, memory, keys, values, hidden, grad, gated, gnorm, cgrad, ngrad, stats,
    key_grad, value_grad, grads_t, halo_in, give_far, take_far,
    load_sem, in_sem, req_send, req_recv, rep_send, rep_recv, tz_send, tz_recv, wz_send, wz_recv,
    xy_send, xy_recv, core_send, core_recv, own_send, own_recv, halo_send, halo_recv, slot_send, slot_recv, ring_send, ring_recv,
    far_send, far_recv,
):
    here = Here()
    greeted = greet(here)
    loads = []
    for b in range(NB):
        src = wk_ref if b < NB // 2 else wv_ref
        loads.append(pltpu.make_async_copy(src.at[:, pl.ds(lanes(b).start, CB)], weights.at[b, here.z, here.core], load_sem.at[b]))
    inputs = [pltpu.make_async_copy(hidden_ref, hidden, in_sem.at[0]), pltpu.make_async_copy(grad_ref, grad.at[pl.ds(0, TOK)], in_sem.at[1])]
    for load in loads + inputs:
        load.start()
    for c in range(NC):
        tab[here.z, c, 0:R_DEV, :] = table_ref[:, c * CW : (c + 1) * CW].astype(BF16)
        tab[here.z, c, R_DEV:TROWS, :] = jnp.zeros((TROWS - R_DEV, CW), BF16)
    plan_slots(owner_ref, local_ref, expand_ref, spread, spread_t, req_out)
    plan_docs(here, lengths_ref, docs)
    greeted()

    spans = (pl.ds(0, NC // 2 + 1), pl.ds(NC // 2 + 1, NC // 2))
    tables = [
        Ring(here, lambda zz, span=span: tab.at[zz, span], tz_send.at[i], tz_recv.at[i], i) for i, span in enumerate(spans)
    ]
    blocks = [here.x, NB // 2 + here.y, NB // 2 - 1, NB - 1]
    pieces = [
        Ring(here, lambda zz, b=b: weights.at[b, zz, here.core], wz_send.at[i], wz_recv.at[i], i % 2)
        for i, b in enumerate(blocks)
    ]
    crosses = [
        Cross(here, "x", weights, 0, xy_send.at[0], xy_recv.at[0]),
        Cross(here, "y", weights, NB // 2, xy_send.at[1], xy_recv.at[1]),
    ]
    zeds = [here.zed(step) for step in (0, -1, 1, -2, 2, -3, 3, 4)]
    def to_partner(b, zz):
        ref = weights.at[b, zz, here.core]
        return remote(ref, ref, core_send.at[b, zz], core_recv.at[b, zz], here.partner())

    def own_to_partner():
        ref = weights.at[:, here.z, here.core]
        return remote(ref, ref, own_send, own_recv, here.partner())

    def from_partner(b):
        for i in range(1, Z):
            ref = weights.at[b, zeds[i], 1 - here.core]
            remote(ref, ref, core_send.at[b, zeds[i]], core_recv.at[b, zeds[i]], here.partner()).wait_recv()

    key_ring, value_ring = pieces[:2]
    x_cross, y_cross = crosses
    for load in loads + inputs:
        load.wait()
    for ring in pieces[:2]:
        ring.start(1)
    for ring in tables:
        ring.start(1)
    send_mates(here, req_out, req_in, req_send, req_recv)
    req_in[here.plane] = req_out[here.plane]
    early = remote(
        grad.at[pl.ds(0, PAD)], grad.at[pl.ds(TOK, PAD)], halo_send.at[2], halo_recv.at[2], here.neighbour(-1)
    )
    early.start()
    own_to_partner().start()
    mates_arrived(here, req_in, req_recv)
    plan_serve(req_in, serve, serve_t)
    for step in (1, 2, 3):
        for ring, cross in ((key_ring, x_cross), (value_ring, y_cross)):
            ring.arrived(step)
            ring.start(step + 1)
            for i in (2 * step - 1, 2 * step):
                cross.start(zeds[i], i)
                to_partner(cross.block(0), zeds[i]).start()
        for ring in tables:
            ring.arrived(step)
            ring.start(step + 1)
        if step > 1:
            for cross in crosses:
                for i in (2 * step - 3, 2 * step - 2):
                    cross.relay(zeds[i], i)
                    for side in (-1, 1):
                        to_partner(cross.block(side), zeds[i]).start()
    for ring in pieces[2:]:
        ring.start(1)
    for ring in tables:
        ring.arrived(4)
    for c in range(NC):
        rows = nn(serve[...], tab[:, c].reshape(Z * TROWS, CW))
        reply[c] = rows.astype(BF16).reshape(PLANE, MSG, CW)
        fetched[c, here.plane] = reply[c, here.plane]
        send_mates(here, reply.at[c], fetched.at[c], rep_send.at[c], rep_recv.at[c])
    for ring, cross in ((key_ring, x_cross), (value_ring, y_cross)):
        ring.arrived(4)
        cross.start(zeds[Z - 1], Z - 1)
        to_partner(cross.block(0), zeds[Z - 1]).start()

    def project(b):
        from_partner(b)
        return nn(memory[...], weights[b].reshape(E, CB))

    def project_key(b):
        keys[b] = project(b)

    def project_value(b):
        values[b] = project(NB // 2 + b)

    for step in (1, 2, 3):
        for ring, b in zip(pieces[2:], (NB // 2 - 1, NB - 1)):
            ring.arrived(step)
            ring.start(step + 1)
            for i in (2 * step - 1, 2 * step):
                to_partner(b, zeds[i]).start()
        if step == 1:
            for cross in crosses:
                for i in (Z - 3, Z - 2):
                    cross.relay(zeds[i], i)
                    for side in (-1, 1):
                        to_partner(cross.block(side), zeds[i]).start()
        else:
            for cross in crosses:
                for i in (2 * step - 3, 2 * step - 2):
                    cross.finish(zeds[i], i)
                    to_partner(cross.block(2), zeds[i]).start()
    for cross in crosses:
        cross.relay(zeds[Z - 1], Z - 1)
        for side in (-1, 1):
            to_partner(cross.block(side), zeds[Z - 1]).start()
    for c in range(NC):
        mates_arrived(here, fetched.at[c], rep_recv.at[c])
        memory[:, c * CW : (c + 1) * CW] = nn(spread[...], fetched[c].reshape(PLACES, CW)).astype(BF16)
    own_to_partner().wait_recv()
    project_key(here.x)
    project_value(here.y)
    for ring, b in zip(pieces[2:], (NB // 2 - 1, NB - 1)):
        ring.arrived(4)
        to_partner(b, zeds[Z - 1]).start()
    for i in range(5, Z):
        for cross in crosses:
            cross.finish(zeds[i], i)
            to_partner(cross.block(2), zeds[i]).start()
    for step in (-1, 1, 2):
        project_key(here.exx(step))
        project_value(here.wye(step))
    project_key(NB // 2 - 1)
    project_value(NB // 2 - 1)

    last = TOK // TILE - 1

    def halo(way):
        src = gated.at[pl.ds(last * TILE if way == 0 else 0, TILE)]
        return remote(src, halo_in.at[way], halo_send.at[way], halo_recv.at[way], here.neighbour(1 - 2 * way))

    def gate_step(t, carry):
        gate_tile(t, keys, values, hidden, gated, gnorm, stats)
        return carry

    def conv_step(t, carry):
        conv_tile(t, docs, taps_ref, gnorm, gated, grad, cgrad, out)
        return carry

    def grad_step(t, carry):
        grad_tile(t, docs, taps_ref, gnorm, cgrad, grad, keys, values, hidden, stats, ngrad, key_grad, value_grad)
        return carry

    gate_step(last, 0)
    halo(0).start()
    gate_step(0, 0)
    halo(1).start()
    lax.fori_loop(1, last, gate_step, 0, unroll=True)
    lax.fori_loop(1, last + 1, conv_step, 0, unroll=True)
    for way, start in ((0, 0), (1, PAD + TOK)):
        halo(way).wait_recv()
        total = jnp.zeros((TILE, CB), F32)
        for b in BLOCKS:
            rows = halo_in[way, :, lanes(b)].astype(F32)
            total = total + rows * rows
        scale = mean_scale(jnp.sum(total, axis=1, keepdims=True))
        for b in BLOCKS:
            gnorm[start : start + PAD, lanes(b)] = halo_in[way, :, lanes(b)].astype(F32) * scale
    early.wait_recv()
    conv_step(0, 0)
    conv_tile(last + 1, docs, taps_ref, gnorm, gated, grad, cgrad)
    lax.fori_loop(0, last + 1, grad_step, 0, unroll=True)

    for b in range(NB):
        source = key_grad if b < NB // 2 else value_grad
        grads_t[b] = source[:, lanes(b)].T
    def send_slots(c):
        first, stop = c * CW // (2 * WROWS), -(-(c + 1) * CW // (2 * WROWS))
        skip = c * CW - first * 2 * WROWS
        total = jnp.zeros((CW, TOK), F32)
        for b in range(NB):
            part = weights[b, first:stop].reshape((stop - first) * 2 * WROWS, CB)[skip : skip + CW]
            total = total + nn(part, grads_t[b])
        slots[c] = nt(spread_t[...], total.astype(BF16)).astype(BF16).reshape(PLANE, MSG, CW)
        arrived[c, here.plane] = slots[c, here.plane]
        if c >= AHEAD:
            mates_sent(here, slots.at[c - AHEAD], slot_send.at[c - AHEAD])
        send_mates(here, slots.at[c], arrived.at[c], slot_send.at[c], slot_recv.at[c])

    def hop(c, way, step):
        sign = 1 if way == 0 else -1
        return remote(
            give.at[c, way, step - 1], take.at[c, way, step - 1],
            ring_send.at[c, way, step - 1], ring_recv.at[c, way, step - 1], here.at_z(sign),
        )

    def length(c, way):
        return Z // 2 if way == c % 2 else Z // 2 - 1

    def advance(c, step):
        for way in range(2):
            final = length(c, way)
            if step > final:
                continue
            sign = 1 if way == 0 else -1
            mine = partial[c, here.zed(sign * (final - step + 1))]
            if step > 1:
                hop(c, way, step - 1).wait_recv()
                mine = mine + take[c, way, step - 2].astype(F32)
            give[c, way, step - 1] = mine.astype(BF16)
            hop(c, way, step).start()

    def far(c, step):
        place = c - RINGS
        return remote(
            give_far.at[place, here.zed(step)], take_far.at[place, step],
            far_send.at[place, step], far_recv.at[place, step], here.at_z(step),
        )

    def send_far(c):
        give_far[c - RINGS] = partial[c].astype(BF16)
        for step in range(1, Z):
            far(c, step).start()

    def finish(c):
        total = partial[c, here.z]
        if c < RINGS:
            for way in range(2):
                final = length(c, way)
                hop(c, way, final).wait_recv()
                total = total + take[c, way, final - 1].astype(F32)
        else:
            for step in range(1, Z):
                far(c, step).wait_recv()
                total = total + take_far[c - RINGS, step].astype(F32)
        row_grad[:, c * CW : (c + 1) * CW] = total[:R_DEV]

    for c in range(AHEAD):
        send_slots(c)
    for c in range(NC):
        if c + AHEAD < NC:
            send_slots(c + AHEAD)
        mates_arrived(here, arrived.at[c], slot_recv.at[c])
        partial[c] = nn(serve_t[...], arrived[c].reshape(PLACES, CW)).reshape(Z, TROWS, CW)
        if c < RINGS:
            advance(c, 1)
        else:
            send_far(c)
        for back in range(1, 4):
            if 0 <= c - back < RINGS:
                advance(c - back, back + 1)
    for step in range(2, Z // 2 + 1):
        for c in range(RINGS):
            if c + step > NC:
                advance(c, step)
    for c in range(NC):
        finish(c)

    own_to_partner().wait_send()
    for b in range(NB):
        for i in range(1, Z):
            to_partner(b, zeds[i]).wait_send()
    for ring in tables + pieces:
        ring.drain()
    for i in range(1, Z):
        for cross in crosses:
            cross.drain(zeds[i], i)
    early.wait_send()
    for way in range(2):
        halo(way).wait_send()
    mates_sent(here, req_out, req_send)
    for c in range(NC):
        mates_sent(here, reply.at[c], rep_send.at[c])
        if c >= NC - AHEAD:
            mates_sent(here, slots.at[c], slot_send.at[c])
        if c < RINGS:
            for way in range(2):
                for step in range(1, length(c, way) + 1):
                    hop(c, way, step).wait_send()
        else:
            for step in range(1, Z):
                far(c, step).wait_send()


def on_device(
    hidden, grad_out, w_key, w_value, depthwise_weight, table, adam_m, adam_v,
    row_owner, row_local, expand_index, doc_lengths,
):
    vmem = pl.BlockSpec(memory_space=pltpu.VMEM)
    any_ = pl.BlockSpec(memory_space=pl.ANY)
    dma = pltpu.SemaphoreType.DMA
    rows = (NC, PLANE, MSG, CW)
    hops = (RINGS, 2, Z // 2)
    fars = (NC - RINGS, Z)
    memory_out, row_grad = pl.pallas_call(
        kernel,
        out_shape=(jax.ShapeDtypeStruct((TOK, D), BF16), jax.ShapeDtypeStruct((R_DEV, E), F32)),
        in_specs=[vmem] * 6 + [any_] * 4,
        out_specs=(vmem, vmem),
        scratch_shapes=[
            pltpu.VMEM((NB, Z, 2, WROWS, CB), BF16),
            pltpu.VMEM((Z, NC, TROWS, CW), BF16),
            pltpu.VMEM((PLANE, 1, 128), F32),
            pltpu.VMEM((PLANE, 1, 128), F32),
            pltpu.VMEM(rows, BF16),
            pltpu.VMEM(rows, BF16),
            pltpu.VMEM(rows, BF16),
            pltpu.VMEM(rows, BF16),
            pltpu.VMEM((NC, Z, TROWS, CW), F32),
            pltpu.VMEM(hops + (TROWS, CW), BF16),
            pltpu.VMEM(hops + (TROWS, CW), BF16),
            pltpu.VMEM((TOK, PLACES), BF16),
            pltpu.VMEM((PLACES, TOK), BF16),
            pltpu.VMEM((PLACES, Z * TROWS), BF16),
            pltpu.VMEM((Z * TROWS, PLACES), BF16),
            pltpu.VMEM((TOK + 3 * PAD, 128), F32),
            pltpu.VMEM((TOK, E), BF16),
            pltpu.VMEM((NB // 2, TOK, CB), F32),
            pltpu.VMEM((NB // 2, TOK, CB), F32),
            pltpu.VMEM((TOK, D), BF16),
            pltpu.VMEM((TOK + PAD, D), BF16),
            pltpu.VMEM((TOK, D), BF16),
            pltpu.VMEM((PAD + TOK + PAD, D), F32),
            pltpu.VMEM((TOK + PAD, D), F32),
            pltpu.VMEM((TILE, D), F32),
            pltpu.VMEM((len(STATS), TOK, 128), F32),
            pltpu.VMEM((TOK, D), BF16),
            pltpu.VMEM((TOK, D), BF16),
            pltpu.VMEM((NB, CB, TOK), BF16),
            pltpu.VMEM((2, TILE, D), BF16),
            pltpu.VMEM(fars + (TROWS, CW), BF16),
            pltpu.VMEM(fars + (TROWS, CW), BF16),
            dma((NB,)), dma((2,)), dma, dma, dma((NC,)), dma((NC,)),
            dma((2, 2, Z // 2)), dma((2, 2, Z // 2)), dma((4, 2, Z // 2)), dma((4, 2, Z // 2)),
            dma((2, 4, Z)), dma((2, 4, Z)), dma((NB, Z)), dma((NB, Z)), dma, dma,
            dma((3,)), dma((3,)), dma((NC,)), dma((NC,)), dma(hops), dma(hops), dma(fars), dma(fars),
        ],
        compiler_params=pltpu.CompilerParams(
            collective_id=0, has_side_effects=True, vmem_limit_bytes=56 * 1024 * 1024
        ),
        name="memory_branch",
    )(
        row_owner.reshape(1, U), row_local, expand_index[0].T, doc_lengths, depthwise_weight,
        table, hidden[0], grad_out[0], w_key, w_value,
    )
    new_table, new_moment, new_second = adamw(table, adam_m, adam_v, row_grad)
    return (memory_out[None], new_table, new_moment, new_second)


def solution(mesh):
    placed = (
        P("row", "col", None),
        P("row", "col", None),
        P("row", None),
        P("row", None),
        P(),
        P(("row", "col"), None),
        P(("row", "col"), None),
        P(("row", "col"), None),
        P("row", "col", None),
        P("row", "col"),
        P("row", "col", None),
        P("row", None),
    )
    return jax.shard_map(
        on_device,
        mesh=mesh,
        in_specs=placed,
        out_specs=(
            P("row", "col", None),
            P(("row", "col"), None),
            P(("row", "col"), None),
            P(("row", "col"), None),
        ),
        check_vma=False,
    )
```
